512 devices in a mesh: view: 32 (over z, core), head: 16 (over y, x).
Axes of the slice: x: 4, y: 4, z: 16, core: 2. Of those that a mesh axis runs over, the one named last changes fastest.
Arguments:
- latents: bfloat16 [1024, 32, 1152], P('head', 'view'), may hold values from -6 to 6
- norm_gain: float32 [1152], replicated, may hold values from 0.25 to 1.75
- qkv_weight: bfloat16 [16, 216, 1152], P('head'), may hold values from -2 to 2
- qk_gain: float32 [16, 2, 72], P('head'), may hold values from 0.5 to 6
- out_weight: bfloat16 [16, 72, 1152], P('head'), may hold values from -0.375 to 0.375
- intersection: int32 [3, 32], P(None, 'view'), may hold values from 0 to 1, as said below
Outputs:
- mixed: bfloat16 [1024, 32, 1152], P('head', 'view')
The draws below stay inside these ranges and needn't reach their ends.
Inputs may be any that keep to these rules, and one draw needn't show every extreme that they name: intersection is symmetric within a round: intersection[r, g] equals intersection[r, partner of g in round r]; views have from 0 to 3 intersecting partners.
All inputs are finite; a program needn't handle non-finite values.
Results may differ from the reference program's by a relative error of at most 0.0065.
The reference program's roundings to bfloat16 on the way (of `normed`, `qkv` and `attended`) count: a program that leaves them out, or rounds other values in their place, can miss the bound.
Values may be sent and summed in bfloat16 or wider, within the bound.
No kernel may reach another device: no remote copies, remote signals or barrier semaphores. Data moves between devices by JAX's collectives and lax.ppermute only.
A program may use at most 64 MiB of HBM per device.

```python
import math
import jax
import jax.numpy as jnp
from jax import lax

D = 1152
HEADS = 16
HD = 72
LEN = 1024
ROUNDS = 3
VIEW_DEV = 1
VIEWS = 32
N_VIEW = 32


def draw_intersection(key, part):
    key = jax.random.fold_in(key, 7)
    levels_drawn = jax.random.randint(key, (ROUNDS, VIEWS), 0, 3)
    groups = VIEWS // VIEW_DEV
    levels = groups.bit_length() - 1
    index = jnp.arange(VIEWS, dtype=jnp.int32)
    rows = []
    for step in range(ROUNDS):
        bit = step * (levels - 1) // (ROUNDS - 1)
        other = (index // VIEW_DEV ^ 1 << bit) * VIEW_DEV + index % VIEW_DEV
        lower = jnp.minimum(index, other)
        rows.append((levels_drawn[step][lower] > 0).astype(jnp.int32))
    return jnp.stack(rows)


def draw_qk_gain(key, part):
    key = jax.random.fold_in(key, 11)
    drawn = jnp.exp(jax.random.uniform(key, (HEADS, 2, HD), jnp.float32, math.log(0.7), math.log(3.0)))
    return drawn.astype(jnp.float32)


def draw_qkv_weight(key, part):
    key = jax.random.fold_in(key, 13)
    drawn = jnp.clip(jax.random.normal(key, (HEADS, 3 * HD, D), jnp.float32), -6.0, 6.0) * D ** (-0.5)
    return drawn.astype(jnp.bfloat16)


def draw_latents(key, part):
    key = jax.random.fold_in(key, 17)
    drawn = jnp.clip(jax.random.normal(key, (LEN, VIEWS, D), jnp.float32), -6.0, 6.0)
    return drawn.astype(jnp.bfloat16)


def shard_levels(rng, shape, shards, least, largest):
    loudness = 1.0
    for axis_at, parts in shards:
        draws = jax.random.uniform(jax.random.fold_in(jax.random.fold_in(rng, 6), axis_at), (parts,), jnp.float32, least / len(shards), largest / len(shards))
        loudness = loudness * jnp.repeat(jnp.exp(draws), shape[axis_at] // parts).reshape((-1,) + (1,) * (len(shape) - 1 - axis_at))
    return loudness


def scatter_about(stream_key, dims, deviation, reach, split=(), held_as=jnp.bfloat16):
    values = jax.random.normal(stream_key, dims, jnp.float32) * deviation
    if len(split) > 0:
        values = shard_levels(stream_key, dims, split, -0.22, 0.18) * values
    return jnp.clip(values, min=-reach, max=reach).astype(held_as)


def setup_inputs(seed: int = 0) -> dict:
    streams_of = jax.random.split(jax.random.key(seed), 7)
    latents = draw_latents(jax.random.fold_in(streams_of[6], 71), 0)
    norm_gain = jnp.clip(1.0 + 0.15 * jax.random.normal(streams_of[1], (D,), jnp.float32), 0.25, 1.75)
    qkv_weight = draw_qkv_weight(jax.random.fold_in(streams_of[6], 71), 0)
    qk_gain = draw_qk_gain(jax.random.fold_in(streams_of[6], 71), 0)
    out_weight = scatter_about(streams_of[4], (HEADS, HD, D), (D // 4) ** -0.5, 0.375, ((0, 16),))
    intersection = draw_intersection(jax.random.fold_in(streams_of[6], 71), 0)
    return dict(latents=latents, norm_gain=norm_gain, qkv_weight=qkv_weight, qk_gain=qk_gain, out_weight=out_weight, intersection=intersection)


def normalize(latents, norm_gain):
    values = latents.astype(jnp.float32)
    mean = lax.optimization_barrier(jnp.mean(values, axis=-1, keepdims=True))
    centred = values - mean
    var = lax.optimization_barrier(jnp.mean(centred * centred, axis=-1, keepdims=True))
    return (centred * lax.rsqrt(var + 1e-06) * norm_gain).astype(jnp.bfloat16)

def rms_scale(part, gain):
    square = lax.optimization_barrier(jnp.mean(part * part, axis=-1, keepdims=True)) + 1e-06
    return (part * lax.rsqrt(square) * gain).astype(jnp.bfloat16)

def absorb(state, query, keys, values, active, scale):
    best, total, acc = state
    scores = jnp.einsum('hqe,hke->hqk', query.astype(jnp.float32), keys.astype(jnp.float32)) * scale
    newbest = jnp.where(active, jnp.maximum(best, lax.optimization_barrier(jnp.max(scores, axis=-1))), best)
    weights = jnp.where(active, jnp.exp(scores - newbest[..., None]), jnp.float32(0.0))
    factor = jnp.exp(best - newbest)
    total = total * factor + lax.optimization_barrier(jnp.sum(weights, axis=-1))
    rounded = weights.astype(jnp.bfloat16).astype(jnp.float32)
    acc = acc * factor[..., None] + jnp.einsum('hqk,hke->hqe', rounded, values.astype(jnp.float32))
    return (newbest, total, acc)

def finish(state):
    best, total, acc = state
    return acc / jnp.maximum(total, jnp.float32(1.0))[..., None]

def reference(latents, norm_gain, qkv_weight, qk_gain, out_weight, intersection):
    normed = normalize(latents, norm_gain)
    qkv = jnp.dot(normed.reshape(LEN * VIEWS, D), qkv_weight.reshape(HEADS * 3 * HD, D).T, preferred_element_type=jnp.float32)
    qkv = qkv.astype(jnp.bfloat16).reshape(LEN, VIEWS, HEADS, 3 * HD).transpose(1, 2, 0, 3)
    query = rms_scale(qkv[..., :HD].astype(jnp.float32), qk_gain[:, 0][None, :, None, :])
    keys = rms_scale(qkv[..., HD:2 * HD].astype(jnp.float32), qk_gain[:, 1][None, :, None, :])
    values = qkv[..., 2 * HD:]
    scale = float(HD) ** (-0.5)
    levels = N_VIEW.bit_length() - 1
    index = jnp.arange(VIEWS, dtype=jnp.int32)
    partners = []
    for step in range(ROUNDS):
        bit = step * (levels - 1) // (ROUNDS - 1)
        partners.append(((index // VIEW_DEV ^ 1 << bit) * VIEW_DEV + index % VIEW_DEV).astype(jnp.int32))
    partners = jnp.stack(partners)

    def per_view(which):
        start = (jnp.full((HEADS, LEN), -1e+30, jnp.float32), jnp.zeros((HEADS, LEN), jnp.float32), jnp.zeros((HEADS, LEN, HD), jnp.float32))
        own = absorb(start, query[which], keys[which], values[which], jnp.bool_(True), scale)
        cross = start
        for step in range(ROUNDS):
            other = partners[step, which]
            cross = absorb(cross, query[which], keys[other], values[other], intersection[step, which] > 0, scale)
        return (finish(own) + finish(cross)).astype(jnp.bfloat16)
    attended = lax.map(per_view, index)
    flat = attended.transpose(2, 0, 1, 3).reshape(LEN * VIEWS, HEADS * HD)
    mixed = jnp.dot(flat, out_weight.reshape(HEADS * HD, D), preferred_element_type=jnp.float32)
    return mixed.astype(jnp.bfloat16).reshape(LEN, VIEWS, D)
```

```python
import functools
import math
import jax
import jax.numpy as jnp
from jax import lax
from jax.experimental import pallas as pl
from jax.experimental.pallas import tpu as pltpu
from jax.sharding import PartitionSpec as P

BLANK = 1e30


def partner(array, bit):
    return lax.ppermute(array, "view", [(i, i ^ 1 << bit) for i in range(lax.axis_size("view"))])


def normalize(latents, norm_gain):
    values = latents.astype(jnp.float32)
    mean = jnp.mean(values, axis=-1, keepdims=True)
    centred = values - mean
    var = jnp.mean(centred * centred, axis=-1, keepdims=True)
    return (centred * lax.rsqrt(var + 1e-06) * norm_gain).astype(jnp.bfloat16)


def gather_tokens(normed):
    heads = lax.axis_size("head")
    copies = jnp.broadcast_to(normed[None], (heads,) + normed.shape)
    rows = lax.all_to_all(copies, "head", split_axis=0, concat_axis=0, tiled=True)
    return rows.reshape(-1, normed.shape[-1])


def rms_rows(part, gain):
    square = jnp.mean(part * part, axis=0, keepdims=True) + 1e-06
    return part * lax.rsqrt(square) * gain


def project_kernel(with_query, rows_ref, weight_ref, gain_ref, *out_refs):
    head_dim = gain_ref.shape[0]
    weight = weight_ref[...]
    flat = lax.dot_general(
        weight, rows_ref[...], (((1,), (1,)), ((), ())), preferred_element_type=jnp.float32
    )
    flat = flat.astype(jnp.bfloat16).astype(jnp.float32)
    if with_query:
        query = rms_rows(flat[:head_dim], gain_ref[:, 0:1])
        out_refs[0][...] = query.T.astype(jnp.bfloat16)
        flat = flat[head_dim:]
    keys = rms_rows(flat[:head_dim], gain_ref[:, 1:2])
    out_refs[-1][...] = jnp.concatenate([keys, flat[head_dim:]], axis=0).astype(jnp.bfloat16)


def project(rows, weight, gain, with_query):
    tokens, width = rows.shape
    head_dim = gain.shape[0]
    out_shape = [jax.ShapeDtypeStruct((2 * head_dim, tokens), jnp.bfloat16)]
    if with_query:
        out_shape = [jax.ShapeDtypeStruct((tokens, head_dim), jnp.bfloat16)] + out_shape
    return pl.pallas_call(
        functools.partial(project_kernel, with_query),
        out_shape=out_shape,
        compiler_params=pltpu.CompilerParams(vmem_limit_bytes=32 << 20),
        cost_estimate=pl.CostEstimate(
            flops=2 * tokens * width * weight.shape[0], bytes_accessed=2 * tokens * width, transcendentals=0
        ),
    )(rows, weight, gain)


def attend_kernel(tile, active_ref, query_ref, own_ref, *refs):
    far_refs, out_ref, values_ref = refs[:-2], refs[-2], refs[-1]
    tokens, head_dim = query_ref.shape
    factor = math.log2(math.e) * float(head_dim) ** (-0.5)
    pair_refs = (own_ref,) + far_refs
    padded = values_ref.shape[-1]
    lane = lax.broadcasted_iota(jnp.int32, (tokens, padded), 1)
    for n, ref in enumerate(pair_refs):
        part = ref[...].astype(jnp.float32)[head_dim:]
        filled = jnp.concatenate([part, jnp.zeros((padded - head_dim, tokens), jnp.float32)], axis=0)
        values_ref[n] = jnp.where(lane == head_dim, 1.0, filled.T).astype(jnp.bfloat16)

    def scores_of(query, ref):
        keys = ref[...][:head_dim]
        return jnp.dot(query, keys, preferred_element_type=jnp.float32) * factor

    def weighted(scores, shift, n):
        weights = jnp.exp2(scores - shift).astype(jnp.bfloat16)
        return jnp.dot(weights, values_ref[n], preferred_element_type=jnp.float32)

    def finish(acc):
        return acc[:, :head_dim] / jnp.maximum(acc[:, head_dim : head_dim + 1], 1.0)

    def step(at, carry):
        rows = pl.ds(pl.multiple_of(at * tile, tile), tile)
        query = query_ref[rows, :]
        scores = scores_of(query, own_ref)
        own = finish(weighted(scores, jnp.max(scores, axis=1, keepdims=True), 0))
        several = [scores_of(query, ref) for ref in far_refs]
        best = jnp.full((tile, 1), -BLANK, jnp.float32)
        for n, scores in enumerate(several):
            most = jnp.max(scores, axis=1, keepdims=True)
            best = jnp.where(active_ref[n] > 0, jnp.maximum(best, most), best)
        acc = jnp.zeros((tile, padded), jnp.float32)
        for n, scores in enumerate(several):
            acc = acc + weighted(scores, jnp.where(active_ref[n] > 0, best, BLANK), n + 1)
        out_ref[rows, :] = (own + finish(acc)).astype(jnp.bfloat16)
        return carry

    lax.fori_loop(0, tokens // tile, step, 0)


def attend(active, query, own, far):
    tokens, head_dim = query.shape
    blocks = 1 + len(far)
    vmem = pl.BlockSpec(memory_space=pltpu.VMEM)
    return pl.pallas_call(
        functools.partial(attend_kernel, 256),
        out_shape=jax.ShapeDtypeStruct((tokens, head_dim), jnp.bfloat16),
        in_specs=[pl.BlockSpec(memory_space=pltpu.SMEM)] + [vmem] * (1 + blocks),
        out_specs=vmem,
        scratch_shapes=[pltpu.VMEM((blocks, tokens, 128), jnp.bfloat16)],
        compiler_params=pltpu.CompilerParams(vmem_limit_bytes=40 << 20),
        cost_estimate=pl.CostEstimate(
            flops=4 * blocks * tokens * tokens * head_dim,
            bytes_accessed=4 * blocks * tokens * head_dim,
            transcendentals=blocks * tokens * tokens,
        ),
    )(active, query, own, *far)


def on_device(latents, norm_gain, qkv_weight, qk_gain, out_weight, intersection):
    loc_len, view_dev, width = latents.shape
    rows = latents.reshape(loc_len, width)
    levels = lax.axis_size("view").bit_length() - 1
    rounds = intersection.shape[0]
    bits = [step * (levels - 1) // (rounds - 1) for step in range(rounds)]
    far_rows = partner(rows, bits[-1])
    gain = qk_gain[0].T
    head_dim = gain.shape[0]
    weight = qkv_weight[0]
    every = gather_tokens(normalize(rows, norm_gain))
    query, own = project(every, weight, gain, True)
    far = [partner(own, bit) for bit in bits[:-1]]
    far_every = gather_tokens(normalize(far_rows, norm_gain))
    far = far + list(project(far_every, weight[head_dim:], gain, False))
    attended = attend(intersection[:, 0], query, own, far)
    token_rows = lax.all_to_all(
        attended.reshape(-1, loc_len, head_dim), "head", split_axis=0, concat_axis=0, tiled=True
    )
    mixed = jnp.einsum(
        "hte,hed->td",
        token_rows,
        lax.all_gather(out_weight, "head", axis=0, tiled=True),
        preferred_element_type=jnp.float32,
    )
    return mixed.astype(jnp.bfloat16).reshape(loc_len, view_dev, width)


def solution(mesh):
    placed = (
        P("head", "view", None),
        P(),
        P("head", None, None),
        P("head", None, None),
        P("head", None, None),
        P(None, "view"),
    )
    return jax.shard_map(
        on_device, mesh=mesh, in_specs=placed, out_specs=P("head", "view", None), check_vma=False
    )
```

```python
import functools
import math
import jax
import jax.numpy as jnp
from jax import lax
from jax.experimental import pallas as pl
from jax.experimental.pallas import tpu as pltpu
from jax.sharding import PartitionSpec as P

BLANK = 1e30


def partner(array, bit):
    return lax.ppermute(array, "view", [(i, i ^ 1 << bit) for i in range(lax.axis_size("view"))])


def normalize_kernel(rows_ref, gain_ref, out_ref):
    values = rows_ref[...].astype(jnp.float32)
    mean = jnp.mean(values, axis=-1, keepdims=True)
    centred = values - mean
    var = jnp.mean(centred * centred, axis=-1, keepdims=True)
    out_ref[...] = (centred * lax.rsqrt(var + 1e-06) * gain_ref[...]).astype(jnp.bfloat16)


def normalize(rows, norm_gain):
    return pl.pallas_call(
        normalize_kernel,
        out_shape=jax.ShapeDtypeStruct(rows.shape, jnp.bfloat16),
        compiler_params=pltpu.CompilerParams(vmem_limit_bytes=16 << 20),
        cost_estimate=pl.CostEstimate(
            flops=8 * rows.size, bytes_accessed=4 * rows.size, transcendentals=0
        ),
    )(rows, norm_gain[None])


def gather_tokens(normed):
    heads = lax.axis_size("head")
    copies = jnp.broadcast_to(normed[None], (heads,) + normed.shape)
    rows = lax.all_to_all(copies, "head", split_axis=0, concat_axis=0, tiled=True)
    return rows.reshape(-1, normed.shape[-1])


def rms_rows(part, gain):
    square = jnp.mean(part * part, axis=0, keepdims=True) + 1e-06
    return part * lax.rsqrt(square) * gain


def project_kernel(with_query, rows_ref, weight_ref, gain_ref, *out_refs):
    head_dim = gain_ref.shape[0]
    weight = weight_ref[...]
    flat = lax.dot_general(
        weight, rows_ref[...], (((1,), (1,)), ((), ())), preferred_element_type=jnp.float32
    )
    flat = flat.astype(jnp.bfloat16).astype(jnp.float32)
    if with_query:
        query = rms_rows(flat[:head_dim], gain_ref[:, 0:1])
        out_refs[0][...] = query.T.astype(jnp.bfloat16)
        flat = flat[head_dim:]
    keys = rms_rows(flat[:head_dim], gain_ref[:, 1:2])
    out_refs[-1][...] = jnp.concatenate([keys, flat[head_dim:]], axis=0).astype(jnp.bfloat16)


def project(rows, weight, gain, with_query):
    tokens, width = rows.shape
    head_dim = gain.shape[0]
    out_shape = [jax.ShapeDtypeStruct((2 * head_dim, tokens), jnp.bfloat16)]
    if with_query:
        out_shape = [jax.ShapeDtypeStruct((tokens, head_dim), jnp.bfloat16)] + out_shape
    return pl.pallas_call(
        functools.partial(project_kernel, with_query),
        out_shape=out_shape,
        compiler_params=pltpu.CompilerParams(vmem_limit_bytes=32 << 20),
        cost_estimate=pl.CostEstimate(
            flops=2 * tokens * width * weight.shape[0], bytes_accessed=2 * tokens * width, transcendentals=0
        ),
    )(rows, weight, gain)


def scores_of(query, pair_ref):
    head_dim = query.shape[1]
    factor = math.log2(math.e) * float(head_dim) ** (-0.5)
    keys = pair_ref[...][:head_dim]
    return jnp.dot(query, keys, preferred_element_type=jnp.float32) * factor


def weighted(scores, shift, values):
    weights = jnp.exp2(scores - shift).astype(jnp.bfloat16)
    return jnp.dot(weights, values, preferred_element_type=jnp.float32)


def finish(acc, head_dim):
    return acc[:, :head_dim] / jnp.maximum(acc[:, head_dim : head_dim + 1], 1.0)


def spread_values(pair_ref, head_dim, padded):
    part = pair_ref[...].astype(jnp.float32)[head_dim:]
    tokens = part.shape[1]
    lane = lax.broadcasted_iota(jnp.int32, (tokens, padded), 1)
    filled = jnp.concatenate([part, jnp.zeros((padded - head_dim, tokens), jnp.float32)], axis=0)
    return jnp.where(lane == head_dim, 1.0, filled.T).astype(jnp.bfloat16)


def cross_update(active_ref, first, query, far_refs, values_ref, slot, best, acc):
    several = [scores_of(query, ref) for ref in far_refs]
    newbest = best
    for n, scores in enumerate(several):
        most = jnp.max(scores, axis=1, keepdims=True)
        newbest = jnp.where(active_ref[first + n] > 0, jnp.maximum(newbest, most), newbest)
    if acc is not None:
        acc = acc * jnp.exp2(best - newbest)
    for n, scores in enumerate(several):
        shift = jnp.where(active_ref[first + n] > 0, newbest, BLANK)
        term = weighted(scores, shift, values_ref[slot + n])
        acc = term if acc is None else acc + term
    return newbest, acc


def near_kernel(tile, active_ref, query_ref, own_ref, *refs):
    far_refs, own_out_ref, state_ref, values_ref = refs[:-3], refs[-3], refs[-2], refs[-1]
    tokens, head_dim = query_ref.shape
    padded = values_ref.shape[-1]
    for n, ref in enumerate((own_ref,) + far_refs):
        values_ref[n] = spread_values(ref, head_dim, padded)

    def step(at, carry):
        rows = pl.ds(pl.multiple_of(at * tile, tile), tile)
        query = query_ref[rows, :]
        scores = scores_of(query, own_ref)
        acc = weighted(scores, jnp.max(scores, axis=1, keepdims=True), values_ref[0])
        own_out_ref[rows, :] = finish(acc, head_dim)
        start = jnp.full((tile, 1), -BLANK, jnp.float32)
        best, acc = cross_update(active_ref, 0, query, far_refs, values_ref, 1, start, None)
        lane = lax.broadcasted_iota(jnp.int32, (tile, padded), 1)
        state_ref[rows, :] = jnp.where(lane == head_dim + 1, best, acc)
        return carry

    lax.fori_loop(0, tokens // tile, step, 0)


def last_kernel(tile, first, active_ref, query_ref, own_in_ref, state_ref, *refs):
    far_refs, out_ref, values_ref = refs[:-2], refs[-2], refs[-1]
    tokens, head_dim = query_ref.shape
    padded = values_ref.shape[-1]
    for n, ref in enumerate(far_refs):
        values_ref[n] = spread_values(ref, head_dim, padded)

    def step(at, carry):
        rows = pl.ds(pl.multiple_of(at * tile, tile), tile)
        query = query_ref[rows, :]
        acc = state_ref[rows, :]
        best = acc[:, head_dim + 1 : head_dim + 2]
        best, acc = cross_update(active_ref, first, query, far_refs, values_ref, 0, best, acc)
        out_ref[rows, :] = (own_in_ref[rows, :] + finish(acc, head_dim)).astype(jnp.bfloat16)
        return carry

    lax.fori_loop(0, tokens // tile, step, 0)


PADDED = 128


def call_attend(kernel, out_shape, blocks, tokens, head_dim, arrays):
    vmem = pl.BlockSpec(memory_space=pltpu.VMEM)
    several = isinstance(out_shape, list)
    return pl.pallas_call(
        kernel,
        out_shape=out_shape,
        in_specs=[pl.BlockSpec(memory_space=pltpu.SMEM)] + [vmem] * (len(arrays) - 1),
        out_specs=[vmem] * len(out_shape) if several else vmem,
        scratch_shapes=[pltpu.VMEM((blocks, tokens, PADDED), jnp.bfloat16)],
        compiler_params=pltpu.CompilerParams(vmem_limit_bytes=40 << 20),
        cost_estimate=pl.CostEstimate(
            flops=4 * blocks * tokens * tokens * 256,
            bytes_accessed=4 * blocks * tokens * head_dim,
            transcendentals=blocks * tokens * tokens,
        ),
    )(*arrays)


def attend_near(active, query, own, far):
    tokens, head_dim = query.shape
    out_shape = [
        jax.ShapeDtypeStruct((tokens, head_dim), jnp.float32),
        jax.ShapeDtypeStruct((tokens, PADDED), jnp.float32),
    ]
    arrays = (active, query, own, *far)
    return call_attend(
        functools.partial(near_kernel, 256), out_shape, 1 + len(far), tokens, head_dim, arrays
    )


def attend_last(active, first, query, own_result, state, far):
    tokens, head_dim = query.shape
    out_shape = jax.ShapeDtypeStruct((tokens, head_dim), jnp.bfloat16)
    arrays = (active, query, own_result, state, *far)
    return call_attend(
        functools.partial(last_kernel, 256, first), out_shape, len(far), tokens, head_dim, arrays
    )


def gather_out_half(out_weight):
    head_dim, width = out_weight.shape
    half = width // 2
    core = lax.axis_index("view") % 2
    mine = lax.dynamic_slice_in_dim(out_weight, core * half, half, axis=1)
    return lax.all_gather(mine, "head", axis=0, tiled=True)


def swap_halves(mine):
    core = lax.axis_index("view") % 2
    other = partner(mine, 0)
    pair = jnp.where(core == 0, jnp.stack([mine, other]), jnp.stack([other, mine]))
    return jnp.concatenate([pair[0], pair[1]], axis=1)


def on_device(latents, norm_gain, qkv_weight, qk_gain, out_weight, intersection):
    loc_len, view_dev, width = latents.shape
    rows = latents.reshape(loc_len, width)
    levels = lax.axis_size("view").bit_length() - 1
    rounds = intersection.shape[0]
    bits = [step * (levels - 1) // (rounds - 1) for step in range(rounds)]
    gain = qk_gain[0].T
    head_dim = gain.shape[0]
    weight = qkv_weight[0]
    active = intersection[:, 0]
    normed = normalize(rows, norm_gain)
    far_normed = partner(normed, bits[-1])
    every = gather_tokens(normed)
    query, own = project(every, weight, gain, True)
    near = [partner(own, bit) for bit in bits[:-1]]
    far_every = gather_tokens(far_normed)
    out_half = gather_out_half(out_weight[0])
    own_result, state = attend_near(active, query, own, near)
    out_half, own_result, state = lax.optimization_barrier((out_half, own_result, state))
    full_out = swap_halves(out_half).reshape(-1, head_dim, width)
    far_every, full_out = lax.optimization_barrier((far_every, full_out))
    far = list(project(far_every, weight[head_dim:], gain, False))
    attended = attend_last(active, rounds - 1, query, own_result, state, far)
    token_rows = lax.all_to_all(
        attended.reshape(-1, loc_len, head_dim), "head", split_axis=0, concat_axis=0, tiled=True
    )
    mixed = jnp.einsum("hte,hed->td", token_rows, full_out, preferred_element_type=jnp.float32)
    return mixed.astype(jnp.bfloat16).reshape(loc_len, view_dev, width)


def solution(mesh):
    placed = (
        P("head", "view", None),
        P(),
        P("head", None, None),
        P("head", None, None),
        P("head", None, None),
        P(None, "view"),
    )
    return jax.shard_map(
        on_device, mesh=mesh, in_specs=placed, out_specs=P("head", "view", None), check_vma=False
    )
```

```python
import functools
import math
import jax
import jax.numpy as jnp
from jax import lax
from jax.experimental import pallas as pl
from jax.experimental.pallas import tpu as pltpu
from jax.sharding import PartitionSpec as P

BLANK = 1e30


def partner(array, bit):
    return lax.ppermute(array, "view", [(i, i ^ 1 << bit) for i in range(lax.axis_size("view"))])


def normalize_kernel(rows_ref, gain_ref, out_ref):
    values = rows_ref[...].astype(jnp.float32)
    mean = jnp.mean(values, axis=-1, keepdims=True)
    centred = values - mean
    var = jnp.mean(centred * centred, axis=-1, keepdims=True)
    out_ref[...] = (centred * lax.rsqrt(var + 1e-06) * gain_ref[...]).astype(jnp.bfloat16)


def normalize(rows, norm_gain):
    return pl.pallas_call(
        normalize_kernel,
        out_shape=jax.ShapeDtypeStruct(rows.shape, jnp.bfloat16),
        compiler_params=pltpu.CompilerParams(vmem_limit_bytes=16 << 20),
        cost_estimate=pl.CostEstimate(
            flops=8 * rows.size, bytes_accessed=4 * rows.size, transcendentals=0
        ),
    )(rows, norm_gain[None])


def gather_tokens(normed):
    heads = lax.axis_size("head")
    copies = jnp.broadcast_to(normed[None], (heads,) + normed.shape)
    rows = lax.all_to_all(copies, "head", split_axis=0, concat_axis=0, tiled=True)
    return rows.reshape(-1, normed.shape[-1])


def rms_rows(part, gain):
    square = jnp.mean(part * part, axis=0, keepdims=True) + 1e-06
    return part * lax.rsqrt(square) * gain


def project_kernel(with_query, rows_ref, weight_ref, gain_ref, *out_refs):
    head_dim = gain_ref.shape[0]
    weight = weight_ref[...]
    flat = lax.dot_general(
        weight, rows_ref[...], (((1,), (1,)), ((), ())), preferred_element_type=jnp.float32
    )
    flat = flat.astype(jnp.bfloat16).astype(jnp.float32)
    if with_query:
        query = rms_rows(flat[:head_dim], gain_ref[:, 0:1])
        out_refs[0][...] = query.T.astype(jnp.bfloat16)
        flat = flat[head_dim:]
    keys = rms_rows(flat[:head_dim], gain_ref[:, 1:2])
    out_refs[-1][...] = jnp.concatenate([keys, flat[head_dim:]], axis=0).astype(jnp.bfloat16)


def project(rows, weight, gain, with_query):
    tokens, width = rows.shape
    head_dim = gain.shape[0]
    out_shape = [jax.ShapeDtypeStruct((2 * head_dim, tokens), jnp.bfloat16)]
    if with_query:
        out_shape = [jax.ShapeDtypeStruct((tokens, head_dim), jnp.bfloat16)] + out_shape
    return pl.pallas_call(
        functools.partial(project_kernel, with_query),
        out_shape=out_shape,
        compiler_params=pltpu.CompilerParams(vmem_limit_bytes=32 << 20),
        cost_estimate=pl.CostEstimate(
            flops=2 * tokens * width * weight.shape[0], bytes_accessed=2 * tokens * width, transcendentals=0
        ),
    )(rows, weight, gain)


def scores_of(query, pair_ref):
    head_dim = query.shape[1]
    factor = math.log2(math.e) * float(head_dim) ** (-0.5)
    keys = pair_ref[...][:head_dim]
    return jnp.dot(query, keys, preferred_element_type=jnp.float32) * factor


def weighted(scores, shift, values):
    weights = jnp.exp2(scores - shift).astype(jnp.bfloat16)
    return jnp.dot(weights, values, preferred_element_type=jnp.float32)


def finish(acc, head_dim):
    return acc[:, :head_dim] / jnp.maximum(acc[:, head_dim : head_dim + 1], 1.0)


def spread_values(pair_ref, head_dim, padded):
    part = pair_ref[...].astype(jnp.float32)[head_dim:]
    tokens = part.shape[1]
    lane = lax.broadcasted_iota(jnp.int32, (tokens, padded), 1)
    filled = jnp.concatenate([part, jnp.zeros((padded - head_dim, tokens), jnp.float32)], axis=0)
    return jnp.where(lane == head_dim, 1.0, filled.T).astype(jnp.bfloat16)


def cross_update(active_ref, first, query, far_refs, values_ref, slot, best, acc):
    several = [scores_of(query, ref) for ref in far_refs]
    newbest = best
    for n, scores in enumerate(several):
        most = jnp.max(scores, axis=1, keepdims=True)
        newbest = jnp.where(active_ref[first + n] > 0, jnp.maximum(newbest, most), newbest)
    if acc is not None:
        acc = acc * jnp.exp2(best - newbest)
    for n, scores in enumerate(several):
        shift = jnp.where(active_ref[first + n] > 0, newbest, BLANK)
        term = weighted(scores, shift, values_ref[slot + n])
        acc = term if acc is None else acc + term
    return newbest, acc


def near_kernel(tile, active_ref, query_ref, own_ref, *refs):
    far_refs, own_out_ref, state_ref, values_ref = refs[:-3], refs[-3], refs[-2], refs[-1]
    tokens, head_dim = query_ref.shape
    padded = values_ref.shape[-1]
    for n, ref in enumerate((own_ref,) + far_refs):
        values_ref[n] = spread_values(ref, head_dim, padded)

    def step(at, carry):
        rows = pl.ds(pl.multiple_of(at * tile, tile), tile)
        query = query_ref[rows, :]
        scores = scores_of(query, own_ref)
        acc = weighted(scores, jnp.max(scores, axis=1, keepdims=True), values_ref[0])
        own_out_ref[rows, :] = finish(acc, head_dim)
        start = jnp.full((tile, 1), -BLANK, jnp.float32)
        best, acc = cross_update(active_ref, 0, query, far_refs, values_ref, 1, start, None)
        lane = lax.broadcasted_iota(jnp.int32, (tile, padded), 1)
        state_ref[rows, :] = jnp.where(lane == head_dim + 1, best, acc)
        return carry

    lax.fori_loop(0, tokens // tile, step, 0)


def last_kernel(tile, first, active_ref, query_ref, own_in_ref, state_ref, *refs):
    far_refs, out_ref, values_ref = refs[:-2], refs[-2], refs[-1]
    tokens, head_dim = query_ref.shape
    padded = values_ref.shape[-1]
    for n, ref in enumerate(far_refs):
        values_ref[n] = spread_values(ref, head_dim, padded)

    def step(at, carry):
        rows = pl.ds(pl.multiple_of(at * tile, tile), tile)
        query = query_ref[rows, :]
        acc = state_ref[rows, :]
        best = acc[:, head_dim + 1 : head_dim + 2]
        best, acc = cross_update(active_ref, first, query, far_refs, values_ref, 0, best, acc)
        out_ref[rows, :] = (own_in_ref[rows, :] + finish(acc, head_dim)).astype(jnp.bfloat16)
        return carry

    lax.fori_loop(0, tokens // tile, step, 0)


PADDED = 128


def call_attend(kernel, out_shape, blocks, tokens, head_dim, arrays):
    vmem = pl.BlockSpec(memory_space=pltpu.VMEM)
    several = isinstance(out_shape, list)
    return pl.pallas_call(
        kernel,
        out_shape=out_shape,
        in_specs=[pl.BlockSpec(memory_space=pltpu.SMEM)] + [vmem] * (len(arrays) - 1),
        out_specs=[vmem] * len(out_shape) if several else vmem,
        scratch_shapes=[pltpu.VMEM((blocks, tokens, PADDED), jnp.bfloat16)],
        compiler_params=pltpu.CompilerParams(vmem_limit_bytes=40 << 20),
        cost_estimate=pl.CostEstimate(
            flops=4 * blocks * tokens * tokens * 256,
            bytes_accessed=4 * blocks * tokens * head_dim,
            transcendentals=blocks * tokens * tokens,
        ),
    )(*arrays)


def attend_near(active, query, own, far):
    tokens, head_dim = query.shape
    out_shape = [
        jax.ShapeDtypeStruct((tokens, head_dim), jnp.float32),
        jax.ShapeDtypeStruct((tokens, PADDED), jnp.float32),
    ]
    arrays = (active, query, own, *far)
    return call_attend(
        functools.partial(near_kernel, 256), out_shape, 1 + len(far), tokens, head_dim, arrays
    )


def attend_last(active, first, query, own_result, state, far):
    tokens, head_dim = query.shape
    out_shape = jax.ShapeDtypeStruct((tokens, head_dim), jnp.bfloat16)
    arrays = (active, query, own_result, state, *far)
    return call_attend(
        functools.partial(last_kernel, 256, first), out_shape, len(far), tokens, head_dim, arrays
    )


def gather_out_half(out_weight):
    head_dim, width = out_weight.shape
    half = width // 2
    core = lax.axis_index("view") % 2
    mine = lax.dynamic_slice_in_dim(out_weight, core * half, half, axis=1)
    return lax.all_gather(mine, "head", axis=0, tiled=True)


def project_out(token_rows, mine):
    core = lax.axis_index("view") % 2
    heads, loc_len, head_dim = token_rows.shape
    mine = mine.reshape(heads, head_dim, -1)
    other = partner(mine, 0)
    halves = [
        jnp.einsum("hte,hed->td", token_rows, part, preferred_element_type=jnp.float32)
        for part in (mine, other)
    ]
    halves = [part.astype(jnp.bfloat16) for part in halves]
    first, second = halves
    return jnp.where(
        core == 0,
        jnp.concatenate([first, second], axis=1),
        jnp.concatenate([second, first], axis=1),
    )


def on_device(latents, norm_gain, qkv_weight, qk_gain, out_weight, intersection):
    loc_len, view_dev, width = latents.shape
    rows = latents.reshape(loc_len, width)
    levels = lax.axis_size("view").bit_length() - 1
    rounds = intersection.shape[0]
    bits = [step * (levels - 1) // (rounds - 1) for step in range(rounds)]
    gain = qk_gain[0].T
    head_dim = gain.shape[0]
    weight = qkv_weight[0]
    active = intersection[:, 0]
    normed = normalize(rows, norm_gain)
    far_normed = partner(normed, bits[-1])
    every = gather_tokens(normed)
    far_every = gather_tokens(far_normed)
    query, own = project(every, weight, gain, True)
    near = [partner(own, bit) for bit in bits[:-1]]
    own_result, state = attend_near(active, query, own, near)
    far_every, own_result, state = lax.optimization_barrier((far_every, own_result, state))
    far = list(project(far_every, weight[head_dim:], gain, False))
    attended = attend_last(active, rounds - 1, query, own_result, state, far)
    out_half, attended = lax.optimization_barrier((gather_out_half(out_weight[0]), attended))
    token_rows = lax.all_to_all(
        attended.reshape(-1, loc_len, head_dim), "head", split_axis=0, concat_axis=0, tiled=True
    )
    mixed = project_out(token_rows, out_half)
    return mixed.reshape(loc_len, view_dev, width)


def solution(mesh):
    placed = (
        P("head", "view", None),
        P(),
        P("head", None, None),
        P("head", None, None),
        P("head", None, None),
        P(None, "view"),
    )
    return jax.shard_map(
        on_device, mesh=mesh, in_specs=placed, out_specs=P("head", "view", None), check_vma=False
    )
```

```python
import functools
import math
import jax
import jax.numpy as jnp
from jax import lax
from jax.experimental import pallas as pl
from jax.experimental.pallas import tpu as pltpu
from jax.sharding import PartitionSpec as P

BLANK = 1e30


def partner(array, bit):
    return lax.ppermute(array, "view", [(i, i ^ 1 << bit) for i in range(lax.axis_size("view"))])


def beside(array):
    return lax.ppermute(array, "head", [(i, i ^ 1) for i in range(lax.axis_size("head"))])


def traded(*arrays):
    views, heads = lax.axis_size("view"), lax.axis_size("head")
    pairs = []
    for view in range(views):
        for head in range(heads):
            if view % 2 != head % 2:
                pairs.append(((view ^ 1) * heads + (head ^ 1), view * heads + head))
    same = lax.axis_index("view") % 2 == lax.axis_index("head") % 2
    return [
        jnp.where(same, array, lax.ppermute(array, ("view", "head"), pairs)) for array in arrays
    ]


def by_core(first, second, axis):
    core = lax.axis_index("view") % 2
    return jnp.where(
        core == 0, jnp.stack([first, second], axis), jnp.stack([second, first], axis)
    )


def normalize_kernel(core_ref, rows_ref, gain_ref, keep_ref, give_ref):
    values = rows_ref[...].astype(jnp.float32)
    mean = jnp.mean(values, axis=-1, keepdims=True)
    centred = values - mean
    var = jnp.mean(centred * centred, axis=-1, keepdims=True)
    normed = centred * lax.rsqrt(var + 1e-06) * gain_ref[...]
    half = normed.shape[0] // 2
    first = core_ref[0] == 0
    keep_ref[...] = jnp.where(first, normed[:half], normed[half:]).astype(jnp.bfloat16)
    give_ref[...] = jnp.where(first, normed[half:], normed[:half]).astype(jnp.bfloat16)


def normalize(core, rows, norm_gain):
    half = jax.ShapeDtypeStruct((rows.shape[0] // 2, rows.shape[1]), jnp.bfloat16)
    vmem = pl.BlockSpec(memory_space=pltpu.VMEM)
    return pl.pallas_call(
        normalize_kernel,
        out_shape=[half, half],
        in_specs=[pl.BlockSpec(memory_space=pltpu.SMEM), vmem, vmem],
        out_specs=[vmem, vmem],
        compiler_params=pltpu.CompilerParams(vmem_limit_bytes=16 << 20),
        cost_estimate=pl.CostEstimate(
            flops=8 * rows.size, bytes_accessed=4 * rows.size, transcendentals=0
        ),
    )(core, rows, norm_gain[None])


def gather_tokens(pair):
    heads = lax.axis_size("head")
    slots = jnp.broadcast_to(pair[None], (heads // 2,) + pair.shape)
    slots = slots.reshape((heads,) + pair.shape[1:])
    rows = lax.all_to_all(slots, "head", split_axis=0, concat_axis=0, tiled=True)
    return rows.reshape(-1, pair.shape[-1])


def rms_rows(part, gain):
    square = jnp.mean(part * part, axis=0, keepdims=True) + 1e-06
    return part * lax.rsqrt(square) * gain


def project_kernel(with_query, mine_ref, other_ref, weight_ref, gain_ref, *out_refs):
    head_dim = gain_ref.shape[0]
    weight = weight_ref[...]
    for n, rows_ref in enumerate((mine_ref, other_ref)):
        tokens = rows_ref.shape[0]
        flat = lax.dot_general(
            weight, rows_ref[...], (((1,), (1,)), ((), ())), preferred_element_type=jnp.float32
        )
        flat = flat.astype(jnp.bfloat16).astype(jnp.float32)
        at = pl.ds(n * tokens, tokens)
        if with_query:
            query = rms_rows(flat[:head_dim], gain_ref[:, 0:1])
            out_refs[0][at, :] = query.T.astype(jnp.bfloat16)
            flat = flat[head_dim:]
        keys = rms_rows(flat[:head_dim], gain_ref[:, 1:2])
        pair = jnp.concatenate([keys, flat[head_dim:]], axis=0)
        out_refs[-1][:, at] = pair.astype(jnp.bfloat16)


def project(mine, other, weight, gain, with_query):
    tokens, width = 2 * mine.shape[0], mine.shape[1]
    head_dim = gain.shape[0]
    out_shape = [jax.ShapeDtypeStruct((2 * head_dim, tokens), jnp.bfloat16)]
    if with_query:
        out_shape = [jax.ShapeDtypeStruct((tokens, head_dim), jnp.bfloat16)] + out_shape
    return pl.pallas_call(
        functools.partial(project_kernel, with_query),
        out_shape=out_shape,
        compiler_params=pltpu.CompilerParams(vmem_limit_bytes=16 << 20),
        cost_estimate=pl.CostEstimate(
            flops=2 * tokens * width * weight.shape[0], bytes_accessed=2 * tokens * width, transcendentals=0
        ),
    )(mine, other, weight, gain)


def scores_of(query, pair_ref):
    head_dim = query.shape[1]
    factor = math.log2(math.e) * float(head_dim) ** (-0.5)
    keys = pair_ref[...][:head_dim]
    return jnp.dot(query, keys, preferred_element_type=jnp.float32) * factor


def weighted(scores, shift, values):
    weights = jnp.exp2(scores - shift).astype(jnp.bfloat16)
    return jnp.dot(weights, values, preferred_element_type=jnp.float32)


def finish(acc, head_dim):
    return acc[:, :head_dim] / jnp.maximum(acc[:, head_dim : head_dim + 1], 1.0)


def spread_values(pair_ref, head_dim, padded):
    part = pair_ref[...].astype(jnp.float32)[head_dim:]
    tokens = part.shape[1]
    lane = lax.broadcasted_iota(jnp.int32, (tokens, padded), 1)
    filled = jnp.concatenate([part, jnp.zeros((padded - head_dim, tokens), jnp.float32)], axis=0)
    return jnp.where(lane == head_dim, 1.0, filled.T).astype(jnp.bfloat16)


def cross_update(active_ref, first, query, far_refs, values_ref, slot, best, acc):
    several = [scores_of(query, ref) for ref in far_refs]
    newbest = best
    for n, scores in enumerate(several):
        most = jnp.max(scores, axis=1, keepdims=True)
        newbest = jnp.where(active_ref[first + n] > 0, jnp.maximum(newbest, most), newbest)
    if acc is not None:
        acc = acc * jnp.exp2(best - newbest)
    for n, scores in enumerate(several):
        shift = jnp.where(active_ref[first + n] > 0, newbest, BLANK)
        term = weighted(scores, shift, values_ref[slot + n])
        acc = term if acc is None else acc + term
    return newbest, acc


def near_kernel(tile, active_ref, query_ref, own_ref, *refs):
    far_refs, own_out_ref, state_ref, values_ref = refs[:-3], refs[-3], refs[-2], refs[-1]
    tokens, head_dim = query_ref.shape
    padded = values_ref.shape[-1]
    for n, ref in enumerate((own_ref,) + far_refs):
        values_ref[n] = spread_values(ref, head_dim, padded)

    def step(at, carry):
        rows = pl.ds(pl.multiple_of(at * tile, tile), tile)
        query = query_ref[rows, :]
        scores = scores_of(query, own_ref)
        acc = weighted(scores, jnp.max(scores, axis=1, keepdims=True), values_ref[0])
        own_out_ref[rows, :] = finish(acc, head_dim)
        start = jnp.full((tile, 1), -BLANK, jnp.float32)
        best, acc = cross_update(active_ref, 0, query, far_refs, values_ref, 1, start, None)
        lane = lax.broadcasted_iota(jnp.int32, (tile, padded), 1)
        state_ref[rows, :] = jnp.where(lane == head_dim + 1, best, acc)
        return carry

    lax.fori_loop(0, tokens // tile, step, 0, unroll=True)


def last_kernel(tile, first, core_ref, active_ref, query_ref, own_in_ref, state_ref, *refs):
    far_refs, out_ref, values_ref = refs[:-2], refs[-2], refs[-1]
    tokens, head_dim = query_ref.shape
    padded = values_ref.shape[-1]
    for n, ref in enumerate(far_refs):
        values_ref[n] = spread_values(ref, head_dim, padded)

    slots, loc_len, _ = out_ref.shape
    half = loc_len // 2
    for at in range(tokens // tile):
        rows = pl.ds(at * tile, tile)
        query = query_ref[rows, :]
        acc = state_ref[rows, :]
        best = acc[:, head_dim + 1 : head_dim + 2]
        best, acc = cross_update(active_ref, first, query, far_refs, values_ref, 0, best, acc)
        result = own_in_ref[rows, :] + finish(acc, head_dim)
        result = result.reshape(tile // half, half, head_dim).astype(jnp.bfloat16)
        second, block = divmod(at * tile // half, slots)
        side = core_ref[0] if second == 0 else 1 - core_ref[0]
        place = pl.ds(pl.multiple_of(side * half, half), half)
        out_ref[pl.ds(block, tile // half), place, :] = result


PADDED = 128


def call_attend(kernel, out_shape, blocks, tokens, head_dim, scalars, arrays):
    smem, vmem = pl.BlockSpec(memory_space=pltpu.SMEM), pl.BlockSpec(memory_space=pltpu.VMEM)
    several = isinstance(out_shape, list)
    return pl.pallas_call(
        kernel,
        out_shape=out_shape,
        in_specs=[smem] * len(scalars) + [vmem] * len(arrays),
        out_specs=[vmem] * len(out_shape) if several else vmem,
        scratch_shapes=[pltpu.VMEM((blocks, tokens, PADDED), jnp.bfloat16)],
        compiler_params=pltpu.CompilerParams(vmem_limit_bytes=24 << 20),
        cost_estimate=pl.CostEstimate(
            flops=blocks * tokens * tokens * head_dim // 4,
            bytes_accessed=4 * blocks * tokens * head_dim,
            transcendentals=0,
        ),
    )(*scalars, *arrays)


def attend_near(active, query, own, far):
    tokens, head_dim = query.shape
    out_shape = [
        jax.ShapeDtypeStruct((tokens, head_dim), jnp.float32),
        jax.ShapeDtypeStruct((tokens, PADDED), jnp.float32),
    ]
    kernel = functools.partial(near_kernel, 256)
    arrays = (query, own, *far)
    return call_attend(kernel, out_shape, 1 + len(far), tokens, head_dim, (active,), arrays)


def attend_last(core, active, first, query, own_result, state, far):
    tokens, head_dim = query.shape
    heads = lax.axis_size("head")
    out_shape = jax.ShapeDtypeStruct((heads, tokens // heads, head_dim), jnp.bfloat16)
    kernel = functools.partial(last_kernel, 256, first)
    arrays = (query, own_result, state, *far)
    return call_attend(kernel, out_shape, len(far), tokens, head_dim, (core, active), arrays)


def return_tokens(attended):
    heads, loc_len, head_dim = attended.shape
    core = lax.axis_index("view") % 2
    came = lax.all_to_all(attended, "head", split_axis=0, concat_axis=0, tiled=True)
    came = came.reshape(heads // 2, 2, loc_len, head_dim)
    mine = jnp.where(core == 0, came[:, 0], came[:, 1])
    other = partner(jnp.where(core == 0, came[:, 1], came[:, 0]), 0)
    return by_core(mine, other, 1).reshape(heads, loc_len, head_dim)


def on_device(latents, norm_gain, qkv_weight, qk_gain, out_weight, intersection):
    loc_len, view_dev, width = latents.shape
    rows = latents.reshape(loc_len, width)
    levels = lax.axis_size("view").bit_length() - 1
    rounds = intersection.shape[0]
    bits = [step * (levels - 1) // (rounds - 1) for step in range(rounds)]
    head_dim = qk_gain.shape[-1]
    core = (lax.axis_index("view") % 2).astype(jnp.int32)[None]
    flags = jnp.broadcast_to(intersection.astype(jnp.float32), (rounds, head_dim))
    weight, small = traded(qkv_weight[0], jnp.concatenate([qk_gain[0], flags], axis=0))
    keep, give = normalize(core, rows, norm_gain)
    pair = by_core(keep, partner(give, 0), 0)
    far_pair = partner(pair, bits[-1])
    mine = gather_tokens(pair)
    mine, far_pair, weight, small = lax.optimization_barrier((mine, far_pair, weight, small))
    gain, active = small[:2].T, small[2:, 0].astype(jnp.int32)
    far_mine = gather_tokens(far_pair)
    query, own = project(mine, partner(mine, 0), weight, gain, True)
    near = beside(own)
    middle = [partner(own, bit) for bit in bits[1:-1]]
    own_result, state = attend_near(active, query, own, [near])
    far_mine, own_result, state, middle = lax.optimization_barrier(
        (far_mine, own_result, state, middle)
    )
    far = list(project(far_mine, partner(far_mine, 0), weight[head_dim:], gain, False))
    attended = attend_last(core, active, 1, query, own_result, state, middle + far)
    full_out = lax.all_gather(out_weight, "head", axis=0, tiled=True)
    full_out, attended = lax.optimization_barrier((full_out, attended))
    token_rows = return_tokens(attended)
    mixed = jnp.einsum("hte,hed->td", token_rows, full_out, preferred_element_type=jnp.float32)
    return mixed.astype(jnp.bfloat16).reshape(loc_len, view_dev, width)


def solution(mesh):
    placed = (
        P("head", "view", None),
        P(),
        P("head", None, None),
        P("head", None, None),
        P("head", None, None),
        P(None, "view"),
    )
    return jax.shard_map(
        on_device, mesh=mesh, in_specs=placed, out_specs=P("head", "view", None), check_vma=False
    )
```

```python
import functools
import math
import jax
import jax.numpy as jnp
from jax import lax
from jax.experimental import pallas as pl
from jax.experimental.pallas import tpu as pltpu
from jax.sharding import PartitionSpec as P

BLANK = 1e30


def partner(array, bit):
    return lax.ppermute(array, "view", [(i, i ^ 1 << bit) for i in range(lax.axis_size("view"))])


def normalize_kernel(rows_ref, gain_ref, out_ref):
    values = rows_ref[...].astype(jnp.float32)
    mean = jnp.mean(values, axis=-1, keepdims=True)
    centred = values - mean
    var = jnp.mean(centred * centred, axis=-1, keepdims=True)
    out_ref[...] = (centred * lax.rsqrt(var + 1e-06) * gain_ref[...]).astype(jnp.bfloat16)


def normalize(rows, norm_gain):
    return pl.pallas_call(
        normalize_kernel,
        out_shape=jax.ShapeDtypeStruct(rows.shape, jnp.bfloat16),
        compiler_params=pltpu.CompilerParams(vmem_limit_bytes=16 << 20),
        cost_estimate=pl.CostEstimate(
            flops=8 * rows.size, bytes_accessed=4 * rows.size, transcendentals=0
        ),
    )(rows, norm_gain[None])


def groups(which):
    heads = lax.axis_size("head")
    side = math.isqrt(heads)
    table = [[side * i + j for j in range(side)] for i in range(side)]
    return table if which == 0 else [list(column) for column in zip(*table)]


def exchange(slots, which):
    return lax.all_to_all(
        slots, "head", split_axis=0, concat_axis=0, tiled=True, axis_index_groups=groups(which)
    )


def gather_tokens(normed):
    side = len(groups(0))
    copies = jnp.broadcast_to(normed[None], (side,) + normed.shape)
    return exchange(copies, 0).reshape(-1, normed.shape[-1])


def gather_weights(weight):
    views, heads = lax.axis_size("view"), lax.axis_size("head")
    side = len(groups(0))
    core = lax.axis_index("view") % 2
    rows = weight.shape[0]
    part = (rows // 2 + 15) // 16 * 16
    pairs = []
    for view in range(views):
        step = side if view % 2 == 0 else -side
        for head in range(heads):
            pairs.append((view * heads + (head + step) % heads, view * heads + head))
    nearby = lax.ppermute(weight, ("view", "head"), pairs)
    sent = jnp.where(core == 0, weight[:part], weight[rows - part :])
    across = [(head, (head + heads // 2) % heads) for head in range(heads)]
    return jnp.concatenate([nearby, lax.ppermute(sent, "head", across)], axis=0)


def rms_rows(part, gain):
    square = jnp.mean(part * part, axis=0, keepdims=True) + 1e-06
    return part * lax.rsqrt(square) * gain


def project_kernel(skip, place_ref, rows_ref, weight_ref, mine_ref, other_ref, out_ref):
    tokens = rows_ref[...]
    rows = weight_ref.shape[0]
    part = mine_ref.shape[0] - rows

    def product(weight):
        return lax.dot_general(
            weight, tokens, (((1,), (1,)), ((), ())), preferred_element_type=jnp.float32
        )

    mine, other = product(mine_ref[...]), product(other_ref[...])
    own = product(weight_ref[...])
    first = place_ref[4] == 0
    low = jnp.where(first, mine[rows:], other[rows:])
    high = jnp.where(first, other[rows:], mine[rows:])
    far = jnp.concatenate([low[: rows - part], high], axis=0)
    for n, flat in enumerate((own, mine[:rows], other[:rows], far)):
        out_ref[place_ref[n]] = flat[skip:].astype(jnp.bfloat16)


def project(place, tokens, weight, mine, other, skip):
    rows, width = weight.shape
    side = len(groups(0))
    smem, vmem = pl.BlockSpec(memory_space=pltpu.SMEM), pl.BlockSpec(memory_space=pltpu.VMEM)
    return pl.pallas_call(
        functools.partial(project_kernel, skip),
        out_shape=jax.ShapeDtypeStruct((side, rows - skip, tokens.shape[0]), jnp.bfloat16),
        in_specs=[smem] + [vmem] * 4,
        out_specs=vmem,
        compiler_params=pltpu.CompilerParams(vmem_limit_bytes=16 << 20),
        cost_estimate=pl.CostEstimate(
            flops=2 * side * rows * width * tokens.shape[0], bytes_accessed=4 * rows * width, transcendentals=0
        ),
    )(place, tokens, weight, mine, other)


def settle_kernel(with_query, parts_ref, gain_ref, *out_refs):
    head_dim = gain_ref.shape[0]
    blocks, _, tokens = parts_ref.shape
    for n in range(blocks):
        flat = parts_ref[n].astype(jnp.float32)
        at = pl.ds(n * tokens, tokens)
        if with_query:
            query = rms_rows(flat[:head_dim], gain_ref[:, 0:1])
            out_refs[0][at, :] = query.T.astype(jnp.bfloat16)
            flat = flat[head_dim:]
        keys = rms_rows(flat[:head_dim], gain_ref[:, 1:2])
        pair = jnp.concatenate([keys, flat[head_dim:]], axis=0)
        out_refs[-1][:, at] = pair.astype(jnp.bfloat16)


def settle(parts, gain, with_query):
    head_dim = gain.shape[0]
    tokens = parts.shape[0] * parts.shape[2]
    out_shape = [jax.ShapeDtypeStruct((2 * head_dim, tokens), jnp.bfloat16)]
    if with_query:
        out_shape = [jax.ShapeDtypeStruct((tokens, head_dim), jnp.bfloat16)] + out_shape
    return pl.pallas_call(
        functools.partial(settle_kernel, with_query),
        out_shape=out_shape,
        compiler_params=pltpu.CompilerParams(vmem_limit_bytes=16 << 20),
        cost_estimate=pl.CostEstimate(
            flops=8 * parts.size, bytes_accessed=4 * parts.size, transcendentals=0
        ),
    )(parts, gain)


def scores_of(query, pair_ref):
    head_dim = query.shape[1]
    factor = math.log2(math.e) * float(head_dim) ** (-0.5)
    keys = pair_ref[...][:head_dim]
    return jnp.dot(query, keys, preferred_element_type=jnp.float32) * factor


def weighted(scores, shift, values):
    weights = jnp.exp2(scores - shift).astype(jnp.bfloat16)
    return jnp.dot(weights, values, preferred_element_type=jnp.float32)


def finish(acc, head_dim):
    return acc[:, :head_dim] / jnp.maximum(acc[:, head_dim : head_dim + 1], 1.0)


def spread_values(pair_ref, head_dim, padded):
    part = pair_ref[...].astype(jnp.float32)[head_dim:]
    tokens = part.shape[1]
    lane = lax.broadcasted_iota(jnp.int32, (tokens, padded), 1)
    filled = jnp.concatenate([part, jnp.zeros((padded - head_dim, tokens), jnp.float32)], axis=0)
    return jnp.where(lane == head_dim, 1.0, filled.T).astype(jnp.bfloat16)


def cross_update(active_ref, first, query, far_refs, values_ref, slot, best, acc):
    several = [scores_of(query, ref) for ref in far_refs]
    newbest = best
    for n, scores in enumerate(several):
        most = jnp.max(scores, axis=1, keepdims=True)
        newbest = jnp.where(active_ref[first + n] > 0, jnp.maximum(newbest, most), newbest)
    if acc is not None:
        acc = acc * jnp.exp2(best - newbest)
    for n, scores in enumerate(several):
        shift = jnp.where(active_ref[first + n] > 0, newbest, BLANK)
        term = weighted(scores, shift, values_ref[slot + n])
        acc = term if acc is None else acc + term
    return newbest, acc


def near_kernel(tile, active_ref, query_ref, own_ref, *refs):
    far_refs, own_out_ref, state_ref, values_ref = refs[:-3], refs[-3], refs[-2], refs[-1]
    tokens, head_dim = query_ref.shape
    padded = values_ref.shape[-1]
    for n, ref in enumerate((own_ref,) + far_refs):
        values_ref[n] = spread_values(ref, head_dim, padded)

    def step(at, carry):
        rows = pl.ds(pl.multiple_of(at * tile, tile), tile)
        query = query_ref[rows, :]
        scores = scores_of(query, own_ref)
        acc = weighted(scores, jnp.max(scores, axis=1, keepdims=True), values_ref[0])
        own_out_ref[rows, :] = finish(acc, head_dim)
        start = jnp.full((tile, 1), -BLANK, jnp.float32)
        best, acc = cross_update(active_ref, 0, query, far_refs, values_ref, 1, start, None)
        lane = lax.broadcasted_iota(jnp.int32, (tile, padded), 1)
        state_ref[rows, :] = jnp.where(lane == head_dim + 1, best, acc)
        return carry

    lax.fori_loop(0, tokens // tile, step, 0, unroll=True)


def last_kernel(tile, first, active_ref, query_ref, own_in_ref, state_ref, *refs):
    far_refs, out_ref, values_ref = refs[:-2], refs[-2], refs[-1]
    tokens, head_dim = query_ref.shape
    padded = values_ref.shape[-1]
    for n, ref in enumerate(far_refs):
        values_ref[n] = spread_values(ref, head_dim, padded)

    def step(at, carry):
        rows = pl.ds(pl.multiple_of(at * tile, tile), tile)
        query = query_ref[rows, :]
        acc = state_ref[rows, :]
        best = acc[:, head_dim + 1 : head_dim + 2]
        best, acc = cross_update(active_ref, first, query, far_refs, values_ref, 0, best, acc)
        out_ref[rows, :] = (own_in_ref[rows, :] + finish(acc, head_dim)).astype(jnp.bfloat16)
        return carry

    lax.fori_loop(0, tokens // tile, step, 0, unroll=True)


PADDED = 128


def call_attend(kernel, out_shape, blocks, tokens, head_dim, arrays):
    vmem = pl.BlockSpec(memory_space=pltpu.VMEM)
    several = isinstance(out_shape, list)
    return pl.pallas_call(
        kernel,
        out_shape=out_shape,
        in_specs=[pl.BlockSpec(memory_space=pltpu.SMEM)] + [vmem] * (len(arrays) - 1),
        out_specs=[vmem] * len(out_shape) if several else vmem,
        scratch_shapes=[pltpu.VMEM((blocks, tokens, PADDED), jnp.bfloat16)],
        compiler_params=pltpu.CompilerParams(vmem_limit_bytes=20 << 20),
        cost_estimate=pl.CostEstimate(
            flops=4 * blocks * tokens * tokens * 256,
            bytes_accessed=4 * blocks * tokens * head_dim,
            transcendentals=blocks * tokens * tokens,
        ),
    )(*arrays)


def attend_near(active, query, own, far):
    tokens, head_dim = query.shape
    out_shape = [
        jax.ShapeDtypeStruct((tokens, head_dim), jnp.float32),
        jax.ShapeDtypeStruct((tokens, PADDED), jnp.float32),
    ]
    arrays = (active, query, own, *far)
    return call_attend(
        functools.partial(near_kernel, 256), out_shape, 1 + len(far), tokens, head_dim, arrays
    )


def attend_last(active, first, query, own_result, state, far):
    tokens, head_dim = query.shape
    out_shape = jax.ShapeDtypeStruct((tokens, head_dim), jnp.bfloat16)
    arrays = (active, query, own_result, state, *far)
    return call_attend(
        functools.partial(last_kernel, 256, first), out_shape, len(far), tokens, head_dim, arrays
    )


def gather_out_half(out_weight):
    head_dim, width = out_weight.shape
    half = width // 2
    core = lax.axis_index("view") % 2
    mine = lax.dynamic_slice_in_dim(out_weight, core * half, half, axis=1)
    return lax.all_gather(mine, "head", axis=0, tiled=True)


def project_out(token_rows, mine):
    core = lax.axis_index("view") % 2
    heads, loc_len, head_dim = token_rows.shape
    mine = mine.reshape(heads, head_dim, -1)
    other = partner(mine, 0)
    halves = [
        jnp.einsum("hte,hed->td", token_rows, part, preferred_element_type=jnp.float32)
        for part in (mine, other)
    ]
    halves = [part.astype(jnp.bfloat16) for part in halves]
    first, second = halves
    return jnp.where(
        core == 0,
        jnp.concatenate([first, second], axis=1),
        jnp.concatenate([second, first], axis=1),
    )


def on_device(latents, norm_gain, qkv_weight, qk_gain, out_weight, intersection):
    loc_len, view_dev, width = latents.shape
    rows = latents.reshape(loc_len, width)
    levels = lax.axis_size("view").bit_length() - 1
    rounds = intersection.shape[0]
    bits = [step * (levels - 1) // (rounds - 1) for step in range(rounds)]
    gain = qk_gain[0].T
    head_dim = gain.shape[0]
    weight = qkv_weight[0]
    active = intersection[:, 0]
    core = lax.axis_index("view") % 2
    heads, side = lax.axis_size("head"), len(groups(0))
    line = lax.axis_index("head") // side
    turn = jnp.where(core == 0, 1, side - 1)
    place = jnp.stack([line, line + turn, line + side - turn, line + side // 2]) % side
    place = jnp.concatenate([place, core[None]]).astype(jnp.int32)
    mine_weight = gather_weights(weight)
    normed = normalize(rows, norm_gain)
    far_normed = partner(normed, bits[-1])
    tokens, mine_weight, far_normed = lax.optimization_barrier(
        (gather_tokens(normed), mine_weight, far_normed)
    )
    other_weight = partner(mine_weight, 0)
    parts = exchange(project(place, tokens, weight, mine_weight, other_weight, 0), 1)
    query, own = settle(parts, gain, True)
    near = partner(own, bits[0])
    middle = [partner(own, bit) for bit in bits[1:-1]]
    far_normed, query, own = lax.optimization_barrier((far_normed, query, own))
    far_tokens = gather_tokens(far_normed)
    far_parts = project(place, far_tokens, weight, mine_weight, other_weight, head_dim)
    far_parts = exchange(far_parts, 1)
    own_result, state = attend_near(active, query, own, [near])
    far_parts, own_result, state, middle = lax.optimization_barrier(
        (far_parts, own_result, state, middle)
    )
    far = list(settle(far_parts, gain, False))
    attended = attend_last(active, 1, query, own_result, state, middle + far)
    out_half, attended = lax.optimization_barrier((gather_out_half(out_weight[0]), attended))
    token_rows = lax.all_to_all(
        attended.reshape(-1, loc_len, head_dim), "head", split_axis=0, concat_axis=0, tiled=True
    )
    mixed = project_out(token_rows, out_half)
    return mixed.reshape(loc_len, view_dev, width)


def solution(mesh):
    placed = (
        P("head", "view", None),
        P(),
        P("head", None, None),
        P("head", None, None),
        P("head", None, None),
        P(None, "view"),
    )
    return jax.shard_map(
        on_device, mesh=mesh, in_specs=placed, out_specs=P("head", "view", None), check_vma=False
    )
```

```python
import functools
import math
import jax
import jax.numpy as jnp
from jax import lax
from jax.experimental import pallas as pl
from jax.experimental.pallas import tpu as pltpu
from jax.sharding import PartitionSpec as P

BLANK = 1e30


def partner(array, bit):
    return lax.ppermute(array, "view", [(i, i ^ 1 << bit) for i in range(lax.axis_size("view"))])


def normalize_kernel(rows_ref, gain_ref, out_ref):
    values = rows_ref[...].astype(jnp.float32)
    mean = jnp.mean(values, axis=-1, keepdims=True)
    centred = values - mean
    var = jnp.mean(centred * centred, axis=-1, keepdims=True)
    out_ref[...] = (centred * lax.rsqrt(var + 1e-06) * gain_ref[...]).astype(jnp.bfloat16)


def normalize(rows, norm_gain):
    return pl.pallas_call(
        normalize_kernel,
        out_shape=jax.ShapeDtypeStruct(rows.shape, jnp.bfloat16),
        compiler_params=pltpu.CompilerParams(vmem_limit_bytes=16 << 20),
        cost_estimate=pl.CostEstimate(
            flops=8 * rows.size, bytes_accessed=4 * rows.size, transcendentals=0
        ),
    )(rows, norm_gain[None])


def gather_tokens(normed):
    heads = lax.axis_size("head")
    copies = jnp.broadcast_to(normed[None], (heads,) + normed.shape)
    rows = lax.all_to_all(copies, "head", split_axis=0, concat_axis=0, tiled=True)
    return rows.reshape(-1, normed.shape[-1])


def rms_rows(part, gain):
    square = jnp.mean(part * part, axis=0, keepdims=True) + 1e-06
    return part * lax.rsqrt(square) * gain


def project_kernel(with_query, rows_ref, weight_ref, gain_ref, *out_refs):
    head_dim = gain_ref.shape[0]
    weight = weight_ref[...]
    flat = lax.dot_general(
        weight, rows_ref[...], (((1,), (1,)), ((), ())), preferred_element_type=jnp.float32
    )
    flat = flat.astype(jnp.bfloat16).astype(jnp.float32)
    if with_query:
        query = rms_rows(flat[:head_dim], gain_ref[:, 0:1])
        out_refs[0][...] = query.T.astype(jnp.bfloat16)
        flat = flat[head_dim:]
    keys = rms_rows(flat[:head_dim], gain_ref[:, 1:2])
    out_refs[-1][...] = jnp.concatenate([keys, flat[head_dim:]], axis=0).astype(jnp.bfloat16)


def project(rows, weight, gain, with_query):
    tokens, width = rows.shape
    head_dim = gain.shape[0]
    out_shape = [jax.ShapeDtypeStruct((2 * head_dim, tokens), jnp.bfloat16)]
    if with_query:
        out_shape = [jax.ShapeDtypeStruct((tokens, head_dim), jnp.bfloat16)] + out_shape
    return pl.pallas_call(
        functools.partial(project_kernel, with_query),
        out_shape=out_shape,
        compiler_params=pltpu.CompilerParams(vmem_limit_bytes=16 << 20),
        cost_estimate=pl.CostEstimate(
            flops=2 * tokens * width * weight.shape[0], bytes_accessed=2 * tokens * width, transcendentals=0
        ),
    )(rows, weight, gain)


def scores_of(query, pair_ref):
    head_dim = query.shape[1]
    factor = math.log2(math.e) * float(head_dim) ** (-0.5)
    keys = pair_ref[...][:head_dim]
    return jnp.dot(query, keys, preferred_element_type=jnp.float32) * factor


def weighted(scores, shift, values):
    weights = jnp.exp2(scores - shift).astype(jnp.bfloat16)
    return jnp.dot(weights, values, preferred_element_type=jnp.float32)


def finish(acc, head_dim):
    return acc[:, :head_dim] / jnp.maximum(acc[:, head_dim : head_dim + 1], 1.0)


def spread_values(pair_ref, head_dim, padded):
    part = pair_ref[...].astype(jnp.float32)[head_dim:]
    tokens = part.shape[1]
    lane = lax.broadcasted_iota(jnp.int32, (tokens, padded), 1)
    filled = jnp.concatenate([part, jnp.zeros((padded - head_dim, tokens), jnp.float32)], axis=0)
    return jnp.where(lane == head_dim, 1.0, filled.T).astype(jnp.bfloat16)


def cross_update(active_ref, first, query, far_refs, values_ref, slot, best, acc):
    several = [scores_of(query, ref) for ref in far_refs]
    newbest = best
    for n, scores in enumerate(several):
        most = jnp.max(scores, axis=1, keepdims=True)
        newbest = jnp.where(active_ref[first + n] > 0, jnp.maximum(newbest, most), newbest)
    if acc is not None:
        acc = acc * jnp.exp2(best - newbest)
    for n, scores in enumerate(several):
        shift = jnp.where(active_ref[first + n] > 0, newbest, BLANK)
        term = weighted(scores, shift, values_ref[slot + n])
        acc = term if acc is None else acc + term
    return newbest, acc


def near_kernel(tile, active_ref, query_ref, own_ref, *refs):
    far_refs, own_out_ref, state_ref, values_ref = refs[:-3], refs[-3], refs[-2], refs[-1]
    tokens, head_dim = query_ref.shape
    padded = values_ref.shape[-1]
    for n, ref in enumerate((own_ref,) + far_refs):
        values_ref[n] = spread_values(ref, head_dim, padded)

    def step(at, carry):
        rows = pl.ds(pl.multiple_of(at * tile, tile), tile)
        query = query_ref[rows, :]
        scores = scores_of(query, own_ref)
        acc = weighted(scores, jnp.max(scores, axis=1, keepdims=True), values_ref[0])
        own_out_ref[rows, :] = finish(acc, head_dim)
        start = jnp.full((tile, 1), -BLANK, jnp.float32)
        best, acc = cross_update(active_ref, 0, query, far_refs, values_ref, 1, start, None)
        lane = lax.broadcasted_iota(jnp.int32, (tile, padded), 1)
        state_ref[rows, :] = jnp.where(lane == head_dim + 1, best, acc)
        return carry

    lax.fori_loop(0, tokens // tile, step, 0, unroll=True)


def last_kernel(tile, first, active_ref, query_ref, own_in_ref, state_ref, *refs):
    far_refs, out_ref, values_ref = refs[:-2], refs[-2], refs[-1]
    tokens, head_dim = query_ref.shape
    padded = values_ref.shape[-1]
    for n, ref in enumerate(far_refs):
        values_ref[n] = spread_values(ref, head_dim, padded)

    for at in range(tokens // tile):
        rows = pl.ds(at * tile, tile)
        query = query_ref[rows, :]
        acc = state_ref[rows, :]
        best = acc[:, head_dim + 1 : head_dim + 2]
        best, acc = cross_update(active_ref, first, query, far_refs, values_ref, 0, best, acc)
        result = own_in_ref[rows, :] + finish(acc, head_dim)
        out_ref[at] = result.T.astype(jnp.bfloat16)


PADDED = 128


def call_attend(kernel, out_shape, blocks, tokens, head_dim, arrays):
    vmem = pl.BlockSpec(memory_space=pltpu.VMEM)
    several = isinstance(out_shape, list)
    return pl.pallas_call(
        kernel,
        out_shape=out_shape,
        in_specs=[pl.BlockSpec(memory_space=pltpu.SMEM)] + [vmem] * (len(arrays) - 1),
        out_specs=[vmem] * len(out_shape) if several else vmem,
        scratch_shapes=[pltpu.VMEM((blocks, tokens, PADDED), jnp.bfloat16)],
        compiler_params=pltpu.CompilerParams(vmem_limit_bytes=20 << 20),
        cost_estimate=pl.CostEstimate(
            flops=4 * blocks * tokens * tokens * 256,
            bytes_accessed=4 * blocks * tokens * head_dim,
            transcendentals=blocks * tokens * tokens,
        ),
    )(*arrays)


def attend_near(active, query, own, far):
    tokens, head_dim = query.shape
    out_shape = [
        jax.ShapeDtypeStruct((tokens, head_dim), jnp.float32),
        jax.ShapeDtypeStruct((tokens, PADDED), jnp.float32),
    ]
    arrays = (active, query, own, *far)
    return call_attend(
        functools.partial(near_kernel, 256), out_shape, 1 + len(far), tokens, head_dim, arrays
    )


def attend_last(active, first, query, own_result, state, far):
    tokens, head_dim = query.shape
    side = len(groups(0))
    out_shape = jax.ShapeDtypeStruct((side, head_dim, tokens // side), jnp.bfloat16)
    arrays = (active, query, own_result, state, *far)
    return call_attend(
        functools.partial(last_kernel, tokens // side, first), out_shape, len(far), tokens, head_dim, arrays
    )


def groups(which):
    heads = lax.axis_size("head")
    side = math.isqrt(heads)
    table = [[side * i + j for j in range(side)] for i in range(side)]
    return table if which == 0 else [list(column) for column in zip(*table)]


def exchange(slots, which):
    return lax.all_to_all(
        slots, "head", split_axis=0, concat_axis=0, tiled=True, axis_index_groups=groups(which)
    )


def column_weights(weight):
    heads = lax.axis_size("head")
    side = len(groups(0))
    return [
        lax.ppermute(weight, "head", [((head + step * side) % heads, head) for head in range(heads)])
        for step in range(1, side)
    ]


def project_out_kernel(line_ref, parts_ref, *refs):
    weight_refs, out_ref = refs[:-1], refs[-1]
    side = len(weight_refs)
    total = None
    for step, weight_ref in enumerate(weight_refs):
        part = parts_ref[lax.rem(line_ref[0] + step, side)]
        term = lax.dot_general(
            part, weight_ref[...], (((0,), (0,)), ((), ())), preferred_element_type=jnp.float32
        )
        total = term if total is None else total + term
    out_ref[...] = total.reshape(out_ref.shape).astype(jnp.bfloat16)


def project_out(parts, weights):
    side, head_dim, tokens = parts.shape
    width = weights[0].shape[1]
    line = (lax.axis_index("head") // side).astype(jnp.int32)[None]
    smem, vmem = pl.BlockSpec(memory_space=pltpu.SMEM), pl.BlockSpec(memory_space=pltpu.VMEM)
    partial = pl.pallas_call(
        project_out_kernel,
        out_shape=jax.ShapeDtypeStruct((side, tokens // side, width), jnp.bfloat16),
        in_specs=[smem] + [vmem] * (1 + len(weights)),
        out_specs=vmem,
        compiler_params=pltpu.CompilerParams(vmem_limit_bytes=16 << 20),
        cost_estimate=pl.CostEstimate(
            flops=2 * parts.size * width, bytes_accessed=2 * (side * head_dim + tokens) * width, transcendentals=0
        ),
    )(line, parts, *weights)
    partial = exchange(partial, 0)
    return jnp.sum(partial.astype(jnp.float32), axis=0).astype(jnp.bfloat16)


def on_device(latents, norm_gain, qkv_weight, qk_gain, out_weight, intersection):
    loc_len, view_dev, width = latents.shape
    rows = latents.reshape(loc_len, width)
    levels = lax.axis_size("view").bit_length() - 1
    rounds = intersection.shape[0]
    bits = [step * (levels - 1) // (rounds - 1) for step in range(rounds)]
    gain = qk_gain[0].T
    head_dim = gain.shape[0]
    weight = qkv_weight[0]
    active = intersection[:, 0]
    normed = normalize(rows, norm_gain)
    far_normed = partner(normed, bits[-1])
    far_normed, out_weights = lax.optimization_barrier(
        (far_normed, column_weights(out_weight[0]))
    )
    every = gather_tokens(normed)
    far_every = gather_tokens(far_normed)
    query, own = project(every, weight, gain, True)
    near = [partner(own, bit) for bit in bits[:-1]]
    own_result, state = attend_near(active, query, own, near)
    far_every, own_result, state = lax.optimization_barrier((far_every, own_result, state))
    far = list(project(far_every, weight[head_dim:], gain, False))
    attended = attend_last(active, rounds - 1, query, own_result, state, far)
    mixed = project_out(exchange(attended, 1), [out_weight[0]] + out_weights)
    return mixed.reshape(loc_len, view_dev, width)


def solution(mesh):
    placed = (
        P("head", "view", None),
        P(),
        P("head", None, None),
        P("head", None, None),
        P("head", None, None),
        P(None, "view"),
    )
    return jax.shard_map(
        on_device, mesh=mesh, in_specs=placed, out_specs=P("head", "view", None), check_vma=False
    )
```

```python
import functools
import math
import jax
import jax.numpy as jnp
from jax import lax
from jax.experimental import pallas as pl
from jax.experimental.pallas import tpu as pltpu
from jax.sharding import PartitionSpec as P

BLANK = 1e30


def partner(array, bit):
    return lax.ppermute(array, "view", [(i, i ^ 1 << bit) for i in range(lax.axis_size("view"))])


def spread(source_ref, slots_ref, sems):
    copies = [
        pltpu.make_async_copy(source_ref, slots_ref.at[n], sems.at[n]) for n in range(slots_ref.shape[0])
    ]
    for copy in copies:
        copy.start()
    for copy in copies:
        copy.wait()


def normalize_kernel(rows_ref, gain_ref, out_ref, slots_ref, sems):
    values = rows_ref[...].astype(jnp.float32)
    mean = jnp.mean(values, axis=-1, keepdims=True)
    centred = values - mean
    var = jnp.mean(centred * centred, axis=-1, keepdims=True)
    gain = gain_ref[...].reshape(1, -1)
    out_ref[...] = (centred * lax.rsqrt(var + 1e-06) * gain).astype(jnp.bfloat16)
    spread(out_ref, slots_ref, sems)


def normalize(rows, norm_gain, slots):
    vmem = pl.BlockSpec(memory_space=pltpu.VMEM)
    return pl.pallas_call(
        normalize_kernel,
        out_shape=[
            jax.ShapeDtypeStruct(rows.shape, jnp.bfloat16),
            pltpu.HBM((slots,) + rows.shape, jnp.bfloat16),
        ],
        in_specs=[vmem, vmem],
        out_specs=[vmem, pl.BlockSpec(memory_space=pltpu.HBM)],
        scratch_shapes=[pltpu.SemaphoreType.DMA((slots,))],
        compiler_params=pltpu.CompilerParams(vmem_limit_bytes=16 << 20),
        cost_estimate=pl.CostEstimate(
            flops=8 * rows.size, bytes_accessed=2 * slots * rows.size, transcendentals=0
        ),
    )(rows, norm_gain)


def copies_of(rows, slots):
    return pl.pallas_call(
        spread,
        out_shape=pltpu.HBM((slots,) + rows.shape, rows.dtype),
        in_specs=[pl.BlockSpec(memory_space=pltpu.VMEM)],
        out_specs=pl.BlockSpec(memory_space=pltpu.HBM),
        scratch_shapes=[pltpu.SemaphoreType.DMA((slots,))],
        compiler_params=pltpu.CompilerParams(vmem_limit_bytes=16 << 20),
        cost_estimate=pl.CostEstimate(flops=0, bytes_accessed=2 * slots * rows.size, transcendentals=0),
    )(rows)


def gather_tokens(slots):
    rows = lax.all_to_all(slots, "head", split_axis=0, concat_axis=0, tiled=True)
    return rows.reshape(-1, slots.shape[-1])


def rms_rows(part, gain):
    square = jnp.mean(part * part, axis=0, keepdims=True) + 1e-06
    return part * lax.rsqrt(square) * gain


def project_kernel(with_query, rows_ref, weight_ref, gain_ref, *out_refs):
    head_dim = gain_ref.shape[0]
    weight = weight_ref[...]
    flat = lax.dot_general(
        weight, rows_ref[...], (((1,), (1,)), ((), ())), preferred_element_type=jnp.float32
    )
    flat = flat.astype(jnp.bfloat16).astype(jnp.float32)
    if with_query:
        query = rms_rows(flat[:head_dim], gain_ref[:, 0:1])
        out_refs[0][...] = query.T.astype(jnp.bfloat16)
        flat = flat[head_dim:]
    keys = rms_rows(flat[:head_dim], gain_ref[:, 1:2])
    out_refs[-1][...] = jnp.concatenate([keys, flat[head_dim:]], axis=0).astype(jnp.bfloat16)


def project(rows, weight, gain, with_query):
    tokens, width = rows.shape
    head_dim = gain.shape[0]
    block = tokens if with_query else tokens // 4
    out_shape = [jax.ShapeDtypeStruct((2 * head_dim, tokens), jnp.bfloat16)]
    out_specs = [pl.BlockSpec((2 * head_dim, block), lambda n: (0, n))]
    if with_query:
        out_shape = [jax.ShapeDtypeStruct((tokens, head_dim), jnp.bfloat16)] + out_shape
        out_specs = [pl.BlockSpec((block, head_dim), lambda n: (n, 0))] + out_specs
    return pl.pallas_call(
        functools.partial(project_kernel, with_query),
        grid=(tokens // block,),
        out_shape=out_shape,
        in_specs=[
            pl.BlockSpec((block, width), lambda n: (n, 0)),
            pl.BlockSpec(weight.shape, lambda n: (0, 0)),
            pl.BlockSpec(gain.shape, lambda n: (0, 0)),
        ],
        out_specs=out_specs,
        compiler_params=pltpu.CompilerParams(vmem_limit_bytes=20 << 20),
        cost_estimate=pl.CostEstimate(
            flops=2 * tokens * width * weight.shape[0], bytes_accessed=2 * tokens * width, transcendentals=0
        ),
    )(rows, weight, gain)


def scores_of(query, pair_ref):
    head_dim = query.shape[1]
    factor = math.log2(math.e) * float(head_dim) ** (-0.5)
    keys = pair_ref[...][:head_dim]
    return jnp.dot(query, keys, preferred_element_type=jnp.float32) * factor


def weighted(scores, shift, values):
    weights = jnp.exp2(scores - shift).astype(jnp.bfloat16)
    return jnp.dot(weights, values, preferred_element_type=jnp.float32)


def finish(acc, head_dim):
    return acc[:, :head_dim] / jnp.maximum(acc[:, head_dim : head_dim + 1], 1.0)


def spread_values(pair_ref, head_dim, padded):
    part = pair_ref[...].astype(jnp.float32)[head_dim:]
    tokens = part.shape[1]
    lane = lax.broadcasted_iota(jnp.int32, (tokens, padded), 1)
    filled = jnp.concatenate([part, jnp.zeros((padded - head_dim, tokens), jnp.float32)], axis=0)
    return jnp.where(lane == head_dim, 1.0, filled.T).astype(jnp.bfloat16)


def cross_update(active_ref, first, query, far_refs, values_ref, slot, best, acc):
    several = [scores_of(query, ref) for ref in far_refs]
    newbest = best
    for n, scores in enumerate(several):
        most = jnp.max(scores, axis=1, keepdims=True)
        newbest = jnp.where(active_ref[first + n] > 0, jnp.maximum(newbest, most), newbest)
    if acc is not None:
        acc = acc * jnp.exp2(best - newbest)
    for n, scores in enumerate(several):
        shift = jnp.where(active_ref[first + n] > 0, newbest, BLANK)
        term = weighted(scores, shift, values_ref[slot + n])
        acc = term if acc is None else acc + term
    return newbest, acc


def near_kernel(tile, active_ref, query_ref, own_ref, *refs):
    far_refs, own_out_ref, state_ref, values_ref = refs[:-3], refs[-3], refs[-2], refs[-1]
    tokens, head_dim = query_ref.shape
    padded = values_ref.shape[-1]
    for n, ref in enumerate((own_ref,) + far_refs):
        values_ref[n] = spread_values(ref, head_dim, padded)

    def step(at, carry):
        rows = pl.ds(pl.multiple_of(at * tile, tile), tile)
        query = query_ref[rows, :]
        scores = scores_of(query, own_ref)
        acc = weighted(scores, jnp.max(scores, axis=1, keepdims=True), values_ref[0])
        own_out_ref[rows, :] = finish(acc, head_dim)
        start = jnp.full((tile, 1), -BLANK, jnp.float32)
        best, acc = cross_update(active_ref, 0, query, far_refs, values_ref, 1, start, None)
        lane = lax.broadcasted_iota(jnp.int32, (tile, padded), 1)
        state_ref[rows, :] = jnp.where(lane == head_dim + 1, best, acc)
        return carry

    lax.fori_loop(0, tokens // tile, step, 0, unroll=True)


def last_kernel(tile, first, active_ref, query_ref, own_in_ref, state_ref, *refs):
    far_refs, out_ref, values_ref = refs[:-2], refs[-2], refs[-1]
    tokens, head_dim = query_ref.shape
    padded = values_ref.shape[-1]
    for n, ref in enumerate(far_refs):
        values_ref[n] = spread_values(ref, head_dim, padded)

    for at in range(tokens // tile):
        rows = pl.ds(at * tile, tile)
        query = query_ref[rows, :]
        acc = state_ref[rows, :]
        best = acc[:, head_dim + 1 : head_dim + 2]
        best, acc = cross_update(active_ref, first, query, far_refs, values_ref, 0, best, acc)
        result = own_in_ref[rows, :] + finish(acc, head_dim)
        out_ref[at] = result.T.astype(jnp.bfloat16)


PADDED = 128


def call_attend(kernel, out_shape, blocks, tokens, head_dim, arrays):
    vmem = pl.BlockSpec(memory_space=pltpu.VMEM)
    several = isinstance(out_shape, list)
    return pl.pallas_call(
        kernel,
        out_shape=out_shape,
        in_specs=[pl.BlockSpec(memory_space=pltpu.SMEM)] + [vmem] * (len(arrays) - 1),
        out_specs=[vmem] * len(out_shape) if several else vmem,
        scratch_shapes=[pltpu.VMEM((blocks, tokens, PADDED), jnp.bfloat16)],
        compiler_params=pltpu.CompilerParams(vmem_limit_bytes=20 << 20),
        cost_estimate=pl.CostEstimate(
            flops=4 * blocks * tokens * tokens * 256,
            bytes_accessed=4 * blocks * tokens * head_dim,
            transcendentals=blocks * tokens * tokens,
        ),
    )(*arrays)


def attend_near(active, query, own, far):
    tokens, head_dim = query.shape
    out_shape = [
        jax.ShapeDtypeStruct((tokens, head_dim), jnp.float32),
        jax.ShapeDtypeStruct((tokens, PADDED), jnp.float32),
    ]
    arrays = (active, query, own, *far)
    return call_attend(
        functools.partial(near_kernel, 256), out_shape, 1 + len(far), tokens, head_dim, arrays
    )


def attend_last(active, first, query, own_result, state, far):
    tokens, head_dim = query.shape
    side = len(groups(0))
    out_shape = jax.ShapeDtypeStruct((side, head_dim, tokens // side), jnp.bfloat16)
    arrays = (active, query, own_result, state, *far)
    return call_attend(
        functools.partial(last_kernel, tokens // side, first), out_shape, len(far), tokens, head_dim, arrays
    )


def groups(which):
    heads = lax.axis_size("head")
    side = math.isqrt(heads)
    table = [[side * i + j for j in range(side)] for i in range(side)]
    return table if which == 0 else [list(column) for column in zip(*table)]


def exchange(slots, which):
    return lax.all_to_all(
        slots, "head", split_axis=0, concat_axis=0, tiled=True, axis_index_groups=groups(which)
    )


def column_weights(weight):
    views, heads = lax.axis_size("view"), lax.axis_size("head")
    side = len(groups(0))
    core = lax.axis_index("view") % 2
    width = weight.shape[1]
    part = (width // 2 + 127) // 128 * 128
    pairs = []
    for view in range(views):
        step = side if view % 2 == 0 else -side
        for head in range(heads):
            pairs.append((view * heads + (head + step) % heads, view * heads + head))
    beside = lax.ppermute(weight, ("view", "head"), pairs)
    sent = jnp.where(core == 0, weight[:, :part], weight[:, width - part :])
    across = [(head, (head + heads // 2) % heads) for head in range(heads)]
    mine = jnp.concatenate([beside, lax.ppermute(sent, "head", across)], axis=1)
    return mine, partner(mine, 0)


def project_out_kernel(place_ref, parts_ref, weight_ref, mine_ref, other_ref, out_ref):
    side = parts_ref.shape[0]
    line, core = place_ref[0], place_ref[1]
    width = weight_ref.shape[1]
    part = mine_ref.shape[1] - width

    def product(step, weight):
        rows = parts_ref[lax.rem(line + step, side)]
        return lax.dot_general(
            rows, weight, (((0,), (0,)), ((), ())), preferred_element_type=jnp.float32
        )

    turn = jnp.where(core == 0, 1, side - 1)
    total = product(0, weight_ref[...])
    total = total + product(turn, mine_ref[:, :width])
    total = total + product(side - turn, other_ref[:, :width])
    mine, other = product(side // 2, mine_ref[:, width:]), product(side // 2, other_ref[:, width:])
    low, high = jnp.where(core == 0, mine, other), jnp.where(core == 0, other, mine)
    total = total + jnp.concatenate([low[:, : width - part], high], axis=1)
    out_ref[...] = total.reshape(out_ref.shape).astype(jnp.bfloat16)


def project_out(parts, weight, mine, other):
    side, head_dim, tokens = parts.shape
    width = weight.shape[1]
    line, core = lax.axis_index("head") // side, lax.axis_index("view") % 2
    place = jnp.stack([line, core]).astype(jnp.int32)
    smem, vmem = pl.BlockSpec(memory_space=pltpu.SMEM), pl.BlockSpec(memory_space=pltpu.VMEM)
    partial = pl.pallas_call(
        project_out_kernel,
        out_shape=jax.ShapeDtypeStruct((side, tokens // side, width), jnp.bfloat16),
        in_specs=[smem] + [vmem] * 4,
        out_specs=vmem,
        compiler_params=pltpu.CompilerParams(vmem_limit_bytes=16 << 20),
        cost_estimate=pl.CostEstimate(
            flops=2 * parts.size * width, bytes_accessed=2 * (side * head_dim + tokens) * width, transcendentals=0
        ),
    )(place, parts, weight, mine, other)
    partial = exchange(partial, 0)
    return jnp.sum(partial.astype(jnp.float32), axis=0).astype(jnp.bfloat16)


def on_device(latents, norm_gain, qkv_weight, qk_gain, out_weight, intersection):
    loc_len, view_dev, width = latents.shape
    rows = latents.reshape(loc_len, width)
    levels = lax.axis_size("view").bit_length() - 1
    rounds = intersection.shape[0]
    bits = [step * (levels - 1) // (rounds - 1) for step in range(rounds)]
    gain = qk_gain[0].T
    head_dim = gain.shape[0]
    weight = qkv_weight[0]
    active = intersection[:, 0]
    heads = lax.axis_size("head")
    normed, slots = normalize(rows, norm_gain, heads)
    far_slots = copies_of(partner(normed, bits[-1]), heads)
    every, far_slots = lax.optimization_barrier((gather_tokens(slots), far_slots))
    far_every = gather_tokens(far_slots)
    query, own = project(every, weight, gain, True)
    near = [partner(own, bit) for bit in bits[:-1]]
    near[0], out_rows = lax.optimization_barrier((near[0], out_weight[0]))
    mine, other = column_weights(out_rows)
    own_result, state = attend_near(active, query, own, near)
    far_every, own_result, state, mine, other = lax.optimization_barrier(
        (far_every, own_result, state, mine, other)
    )
    far_every = pltpu.with_memory_space_constraint(far_every, pltpu.HBM)
    far = list(project(far_every, weight[head_dim:], gain, False))
    attended = attend_last(active, rounds - 1, query, own_result, state, far)
    mixed = project_out(exchange(attended, 1), out_weight[0], mine, other)
    return mixed.reshape(loc_len, view_dev, width)


def solution(mesh):
    placed = (
        P("head", "view", None),
        P(),
        P("head", None, None),
        P("head", None, None),
        P("head", None, None),
        P(None, "view"),
    )
    return jax.shard_map(
        on_device, mesh=mesh, in_specs=placed, out_specs=P("head", "view", None), check_vma=False
    )
```

```python
import functools
import math
import jax
import jax.numpy as jnp
from jax import lax
from jax.experimental import pallas as pl
from jax.experimental.pallas import tpu as pltpu
from jax.sharding import PartitionSpec as P

BLANK = 1e30


def partner(array, bit):
    return lax.ppermute(array, "view", [(i, i ^ 1 << bit) for i in range(lax.axis_size("view"))])


def spread(source_ref, slots_ref, sems):
    copies = [
        pltpu.make_async_copy(source_ref, slots_ref.at[n], sems.at[n]) for n in range(slots_ref.shape[0])
    ]
    for copy in copies:
        copy.start()
    for copy in copies:
        copy.wait()


def normalize_kernel(rows_ref, gain_ref, out_ref, slots_ref, sems):
    values = rows_ref[...].astype(jnp.float32)
    mean = jnp.mean(values, axis=-1, keepdims=True)
    centred = values - mean
    var = jnp.mean(centred * centred, axis=-1, keepdims=True)
    gain = gain_ref[...].reshape(1, -1)
    out_ref[...] = (centred * lax.rsqrt(var + 1e-06) * gain).astype(jnp.bfloat16)
    spread(out_ref, slots_ref, sems)


def normalize(rows, norm_gain, slots):
    vmem = pl.BlockSpec(memory_space=pltpu.VMEM)
    return pl.pallas_call(
        normalize_kernel,
        out_shape=[
            jax.ShapeDtypeStruct(rows.shape, jnp.bfloat16),
            pltpu.HBM((slots,) + rows.shape, jnp.bfloat16),
        ],
        in_specs=[vmem, vmem],
        out_specs=[vmem, pl.BlockSpec(memory_space=pltpu.HBM)],
        scratch_shapes=[pltpu.SemaphoreType.DMA((slots,))],
        compiler_params=pltpu.CompilerParams(vmem_limit_bytes=16 << 20),
        cost_estimate=pl.CostEstimate(
            flops=8 * rows.size, bytes_accessed=2 * slots * rows.size, transcendentals=0
        ),
    )(rows, norm_gain)


def copies_of(rows, slots):
    return pl.pallas_call(
        spread,
        out_shape=pltpu.HBM((slots,) + rows.shape, rows.dtype),
        in_specs=[pl.BlockSpec(memory_space=pltpu.VMEM)],
        out_specs=pl.BlockSpec(memory_space=pltpu.HBM),
        scratch_shapes=[pltpu.SemaphoreType.DMA((slots,))],
        compiler_params=pltpu.CompilerParams(vmem_limit_bytes=16 << 20),
        cost_estimate=pl.CostEstimate(flops=0, bytes_accessed=2 * slots * rows.size, transcendentals=0),
    )(rows)


def gather_tokens(slots):
    rows = lax.all_to_all(slots, "head", split_axis=0, concat_axis=0, tiled=True)
    return rows.reshape(-1, slots.shape[-1])


def rms_rows(part, gain):
    square = jnp.mean(part * part, axis=0, keepdims=True) + 1e-06
    return part * lax.rsqrt(square) * gain


def project_kernel(rows_ref, weight_ref, gain_ref, query_ref, pair_ref):
    head_dim = gain_ref.shape[0]
    flat = lax.dot_general(
        weight_ref[...], rows_ref[...], (((1,), (1,)), ((), ())), preferred_element_type=jnp.float32
    )
    flat = flat.astype(jnp.bfloat16).astype(jnp.float32)
    query_ref[...] = rms_rows(flat[:head_dim], gain_ref[:, 0:1]).T.astype(jnp.bfloat16)
    keys = rms_rows(flat[head_dim : 2 * head_dim], gain_ref[:, 1:2])
    pair = jnp.concatenate([keys, flat[2 * head_dim :]], axis=0)
    pair_ref[...] = pair.astype(jnp.bfloat16)


def project_far_kernel(rows_ref, weight_ref, gain_ref, pair_ref, held_ref, sems):
    head_dim = gain_ref.shape[0]
    skip = head_dim // 16 * 16
    blocks, block = held_ref.shape[:2]
    copies = [
        pltpu.make_async_copy(rows_ref.at[pl.ds(n * block, block)], held_ref.at[n], sems.at[n])
        for n in range(blocks)
    ]
    for copy in copies:
        copy.start()
    for n in range(blocks):
        copies[n].wait()
        flat = lax.dot_general(
            weight_ref[skip:], held_ref[n], (((1,), (1,)), ((), ())), preferred_element_type=jnp.float32
        )
        flat = flat[head_dim - skip :].astype(jnp.bfloat16).astype(jnp.float32)
        keys = rms_rows(flat[:head_dim], gain_ref[:, 1:2])
        pair = jnp.concatenate([keys, flat[head_dim:]], axis=0)
        pair_ref[:, pl.ds(n * block, block)] = pair.astype(jnp.bfloat16)


def project(rows, weight, gain):
    tokens, width = rows.shape
    head_dim = gain.shape[0]
    return pl.pallas_call(
        project_kernel,
        out_shape=[
            jax.ShapeDtypeStruct((tokens, head_dim), jnp.bfloat16),
            jax.ShapeDtypeStruct((2 * head_dim, tokens), jnp.bfloat16),
        ],
        compiler_params=pltpu.CompilerParams(vmem_limit_bytes=16 << 20),
        cost_estimate=pl.CostEstimate(
            flops=2 * tokens * width * weight.shape[0], bytes_accessed=2 * tokens * width, transcendentals=0
        ),
    )(rows, weight, gain)


def project_far(rows, weight, gain):
    tokens, width = rows.shape
    head_dim = gain.shape[0]
    blocks = 2
    vmem = pl.BlockSpec(memory_space=pltpu.VMEM)
    rows = pltpu.with_memory_space_constraint(rows, pltpu.HBM)
    return pl.pallas_call(
        project_far_kernel,
        out_shape=jax.ShapeDtypeStruct((2 * head_dim, tokens), jnp.bfloat16),
        in_specs=[pl.BlockSpec(memory_space=pltpu.HBM), vmem, vmem],
        out_specs=vmem,
        scratch_shapes=[
            pltpu.VMEM((blocks, tokens // blocks, width), jnp.bfloat16),
            pltpu.SemaphoreType.DMA((blocks,)),
        ],
        compiler_params=pltpu.CompilerParams(vmem_limit_bytes=20 << 20),
        cost_estimate=pl.CostEstimate(
            flops=2 * tokens * width * weight.shape[0], bytes_accessed=2 * tokens * width, transcendentals=0
        ),
    )(rows, weight, gain)


def scores_of(query, pair_ref):
    head_dim = query.shape[1]
    factor = math.log2(math.e) * float(head_dim) ** (-0.5)
    keys = pair_ref[...][:head_dim]
    return jnp.dot(query, keys, preferred_element_type=jnp.float32) * factor


def weighted(scores, shift, values):
    weights = jnp.exp2(scores - shift).astype(jnp.bfloat16)
    return jnp.dot(weights, values, preferred_element_type=jnp.float32)


def finish(acc, head_dim):
    return acc[:, :head_dim] / jnp.maximum(acc[:, head_dim : head_dim + 1], 1.0)


def spread_values(pair_ref, head_dim, padded):
    part = pair_ref[...].astype(jnp.float32)[head_dim:]
    tokens = part.shape[1]
    lane = lax.broadcasted_iota(jnp.int32, (tokens, padded), 1)
    filled = jnp.concatenate([part, jnp.zeros((padded - head_dim, tokens), jnp.float32)], axis=0)
    return jnp.where(lane == head_dim, 1.0, filled.T).astype(jnp.bfloat16)


def cross_update(active_ref, first, query, far_refs, values_ref, slot, best, acc):
    several = [scores_of(query, ref) for ref in far_refs]
    newbest = best
    for n, scores in enumerate(several):
        most = jnp.max(scores, axis=1, keepdims=True)
        newbest = jnp.where(active_ref[first + n] > 0, jnp.maximum(newbest, most), newbest)
    if acc is not None:
        acc = acc * jnp.exp2(best - newbest)
    for n, scores in enumerate(several):
        shift = jnp.where(active_ref[first + n] > 0, newbest, BLANK)
        term = weighted(scores, shift, values_ref[slot + n])
        acc = term if acc is None else acc + term
    return newbest, acc


def near_kernel(tile, active_ref, query_ref, own_ref, *refs):
    far_refs, own_out_ref, state_ref, values_ref = refs[:-3], refs[-3], refs[-2], refs[-1]
    tokens, head_dim = query_ref.shape
    padded = values_ref.shape[-1]
    for n, ref in enumerate((own_ref,) + far_refs):
        values_ref[n] = spread_values(ref, head_dim, padded)

    def step(at, carry):
        rows = pl.ds(pl.multiple_of(at * tile, tile), tile)
        query = query_ref[rows, :]
        scores = scores_of(query, own_ref)
        acc = weighted(scores, jnp.max(scores, axis=1, keepdims=True), values_ref[0])
        own_out_ref[rows, :] = finish(acc, head_dim)
        start = jnp.full((tile, 1), -BLANK, jnp.float32)
        best, acc = cross_update(active_ref, 0, query, far_refs, values_ref, 1, start, None)
        lane = lax.broadcasted_iota(jnp.int32, (tile, padded), 1)
        state_ref[rows, :] = jnp.where(lane == head_dim + 1, best, acc)
        return carry

    lax.fori_loop(0, tokens // tile, step, 0, unroll=True)


def middle_kernel(tile, first, active_ref, query_ref, state_ref, *refs):
    far_refs, out_ref, values_ref = refs[:-2], refs[-2], refs[-1]
    tokens, head_dim = query_ref.shape
    padded = values_ref.shape[-1]
    for n, ref in enumerate(far_refs):
        values_ref[n] = spread_values(ref, head_dim, padded)
    lane = lax.broadcasted_iota(jnp.int32, (tile, padded), 1)
    for at in range(tokens // tile):
        rows = pl.ds(at * tile, tile)
        acc = state_ref[rows, :]
        best = acc[:, head_dim + 1 : head_dim + 2]
        best, acc = cross_update(
            active_ref, first, query_ref[rows, :], far_refs, values_ref, 0, best, acc
        )
        out_ref[rows, :] = jnp.where(lane == head_dim + 1, best, acc)


def last_kernel(tile, first, active_ref, query_ref, own_in_ref, state_ref, *refs):
    far_refs, out_ref, values_ref = refs[:-2], refs[-2], refs[-1]
    tokens, head_dim = query_ref.shape
    padded = values_ref.shape[-1]
    for n, ref in enumerate(far_refs):
        values_ref[n] = spread_values(ref, head_dim, padded)

    for at in range(tokens // tile):
        rows = pl.ds(at * tile, tile)
        query = query_ref[rows, :]
        acc = state_ref[rows, :]
        best = acc[:, head_dim + 1 : head_dim + 2]
        best, acc = cross_update(active_ref, first, query, far_refs, values_ref, 0, best, acc)
        result = own_in_ref[rows, :] + finish(acc, head_dim)
        out_ref[at] = result.T.astype(jnp.bfloat16)


PADDED = 128


def call_attend(kernel, out_shape, blocks, tokens, head_dim, arrays):
    vmem = pl.BlockSpec(memory_space=pltpu.VMEM)
    several = isinstance(out_shape, list)
    return pl.pallas_call(
        kernel,
        out_shape=out_shape,
        in_specs=[pl.BlockSpec(memory_space=pltpu.SMEM)] + [vmem] * (len(arrays) - 1),
        out_specs=[vmem] * len(out_shape) if several else vmem,
        scratch_shapes=[pltpu.VMEM((blocks, tokens, PADDED), jnp.bfloat16)],
        compiler_params=pltpu.CompilerParams(vmem_limit_bytes=20 << 20),
        cost_estimate=pl.CostEstimate(
            flops=4 * blocks * tokens * tokens * 256,
            bytes_accessed=4 * blocks * tokens * head_dim,
            transcendentals=blocks * tokens * tokens,
        ),
    )(*arrays)


def attend_near(active, query, own, far):
    tokens, head_dim = query.shape
    out_shape = [
        jax.ShapeDtypeStruct((tokens, head_dim), jnp.float32),
        jax.ShapeDtypeStruct((tokens, PADDED), jnp.float32),
    ]
    arrays = (active, query, own, *far)
    return call_attend(
        functools.partial(near_kernel, 256), out_shape, 1 + len(far), tokens, head_dim, arrays
    )


def attend_middle(active, first, query, state, far):
    tokens, head_dim = query.shape
    out_shape = jax.ShapeDtypeStruct((tokens, PADDED), jnp.float32)
    arrays = (active, query, state, *far)
    return call_attend(
        functools.partial(middle_kernel, 256, first), out_shape, len(far), tokens, head_dim, arrays
    )


def attend_last(active, first, query, own_result, state, far):
    tokens, head_dim = query.shape
    side = len(groups(0))
    out_shape = jax.ShapeDtypeStruct((side, head_dim, tokens // side), jnp.bfloat16)
    arrays = (active, query, own_result, state, *far)
    return call_attend(
        functools.partial(last_kernel, tokens // side, first), out_shape, len(far), tokens, head_dim, arrays
    )


def groups(which):
    heads = lax.axis_size("head")
    side = math.isqrt(heads)
    table = [[side * i + j for j in range(side)] for i in range(side)]
    return table if which == 0 else [list(column) for column in zip(*table)]


def exchange(slots, which):
    return lax.all_to_all(
        slots, "head", split_axis=0, concat_axis=0, tiled=True, axis_index_groups=groups(which)
    )


def column_weights(weight):
    views, heads = lax.axis_size("view"), lax.axis_size("head")
    side = len(groups(0))
    core = lax.axis_index("view") % 2
    width = weight.shape[1]
    part = (width // 2 + 127) // 128 * 128
    pairs = []
    for view in range(views):
        step = side if view % 2 == 0 else -side
        for head in range(heads):
            pairs.append((view * heads + (head + step) % heads, view * heads + head))
    beside = lax.ppermute(weight, ("view", "head"), pairs)
    sent = jnp.where(core == 0, weight[:, :part], weight[:, width - part :])
    across = [(head, (head + heads // 2) % heads) for head in range(heads)]
    return jnp.concatenate([beside, lax.ppermute(sent, "head", across)], axis=1)


def project_out_kernel(place_ref, parts_ref, weight_ref, mine_ref, other_ref, out_ref):
    side = parts_ref.shape[0]
    line, core = place_ref[0], place_ref[1]
    width = weight_ref.shape[1]
    part = mine_ref.shape[1] - width

    def product(step, weight):
        rows = parts_ref[lax.rem(line + step, side)]
        return lax.dot_general(
            rows, weight, (((0,), (0,)), ((), ())), preferred_element_type=jnp.float32
        )

    turn = jnp.where(core == 0, 1, side - 1)
    total = product(0, weight_ref[...])
    total = total + product(turn, mine_ref[:, :width])
    total = total + product(side - turn, other_ref[:, :width])
    mine, other = product(side // 2, mine_ref[:, width:]), product(side // 2, other_ref[:, width:])
    low, high = jnp.where(core == 0, mine, other), jnp.where(core == 0, other, mine)
    total = total + jnp.concatenate([low[:, : width - part], high], axis=1)
    out_ref[...] = total.reshape(out_ref.shape).astype(jnp.bfloat16)


def project_out(parts, weight, mine, other):
    side, head_dim, tokens = parts.shape
    width = weight.shape[1]
    line, core = lax.axis_index("head") // side, lax.axis_index("view") % 2
    place = jnp.stack([line, core]).astype(jnp.int32)
    smem, vmem = pl.BlockSpec(memory_space=pltpu.SMEM), pl.BlockSpec(memory_space=pltpu.VMEM)
    partial = pl.pallas_call(
        project_out_kernel,
        out_shape=jax.ShapeDtypeStruct((side, tokens // side, width), jnp.bfloat16),
        in_specs=[smem] + [vmem] * 4,
        out_specs=vmem,
        compiler_params=pltpu.CompilerParams(vmem_limit_bytes=16 << 20),
        cost_estimate=pl.CostEstimate(
            flops=2 * parts.size * width, bytes_accessed=2 * (side * head_dim + tokens) * width, transcendentals=0
        ),
    )(place, parts, weight, mine, other)
    partial = exchange(partial, 0)
    return jnp.sum(partial.astype(jnp.float32), axis=0).astype(jnp.bfloat16)


def on_device(latents, norm_gain, qkv_weight, qk_gain, out_weight, intersection):
    loc_len, view_dev, width = latents.shape
    rows = latents.reshape(loc_len, width)
    levels = lax.axis_size("view").bit_length() - 1
    rounds = intersection.shape[0]
    bits = [step * (levels - 1) // (rounds - 1) for step in range(rounds)]
    gain = qk_gain[0].T
    head_dim = gain.shape[0]
    weight = qkv_weight[0]
    active = intersection[:, 0]
    heads = lax.axis_size("head")
    normed, slots = normalize(rows, norm_gain, heads)
    far_normed, mine, gain, active = lax.optimization_barrier(
        (partner(normed, bits[-1]), column_weights(out_weight[0]), gain, active)
    )
    far_slots = copies_of(far_normed, heads)
    every, far_slots = lax.optimization_barrier((gather_tokens(slots), far_slots))
    far_every = gather_tokens(far_slots)
    query, own = project(every, weight, gain)
    near = [partner(own, bit) for bit in bits[:-1]]
    near[0], mine = lax.optimization_barrier((near[0], mine))
    other = partner(mine, 0)
    own_result, state = attend_near(active, query, own, near[:1])
    state = attend_middle(active, 1, query, state, near[1:])
    far_every, own_result, state, other = lax.optimization_barrier(
        (far_every, own_result, state, other)
    )
    far = [project_far(far_every, weight, gain)]
    attended = attend_last(active, rounds - 1, query, own_result, state, far)
    mixed = project_out(exchange(attended, 1), out_weight[0], mine, other)
    return mixed.reshape(loc_len, view_dev, width)


def solution(mesh):
    placed = (
        P("head", "view", None),
        P(),
        P("head", None, None),
        P("head", None, None),
        P("head", None, None),
        P(None, "view"),
    )
    return jax.shard_map(
        on_device, mesh=mesh, in_specs=placed, out_specs=P("head", "view", None), check_vma=False
    )
```

```python
import functools
import math
import jax
import jax.numpy as jnp
from jax import lax
from jax.experimental import pallas as pl
from jax.experimental.pallas import tpu as pltpu
from jax.sharding import PartitionSpec as P

BLANK = 1e30


def partner(array, bit):
    return lax.ppermute(array, "view", [(i, i ^ 1 << bit) for i in range(lax.axis_size("view"))])


def spread(source_ref, slots_ref, sems):
    copies = [
        pltpu.make_async_copy(source_ref, slots_ref.at[n], sems.at[n]) for n in range(slots_ref.shape[0])
    ]
    for copy in copies:
        copy.start()
    for copy in copies:
        copy.wait()


def normalize_kernel(rows_ref, gain_ref, out_ref, slots_ref, held_ref, held_gain_ref, read_sems, sems):
    reads = [
        pltpu.make_async_copy(rows_ref, held_ref, read_sems.at[0]),
        pltpu.make_async_copy(gain_ref, held_gain_ref, read_sems.at[1]),
    ]
    for read in reads:
        read.start()
    for read in reads:
        read.wait()
    values = held_ref[...].astype(jnp.float32)
    mean = jnp.mean(values, axis=-1, keepdims=True)
    centred = values - mean
    var = jnp.mean(centred * centred, axis=-1, keepdims=True)
    gain = held_gain_ref[...].reshape(1, -1)
    out_ref[...] = (centred * lax.rsqrt(var + 1e-06) * gain).astype(jnp.bfloat16)
    spread(out_ref, slots_ref, sems)


def normalize(rows, norm_gain, slots):
    vmem, hbm = pl.BlockSpec(memory_space=pltpu.VMEM), pl.BlockSpec(memory_space=pltpu.HBM)
    rows = pltpu.with_memory_space_constraint(rows, pltpu.HBM)
    norm_gain = pltpu.with_memory_space_constraint(norm_gain, pltpu.HBM)
    return pl.pallas_call(
        normalize_kernel,
        out_shape=[
            jax.ShapeDtypeStruct(rows.shape, jnp.bfloat16),
            pltpu.HBM((slots,) + rows.shape, jnp.bfloat16),
        ],
        in_specs=[hbm, hbm],
        out_specs=[vmem, hbm],
        scratch_shapes=[
            pltpu.VMEM(rows.shape, rows.dtype),
            pltpu.VMEM(norm_gain.shape, norm_gain.dtype),
            pltpu.SemaphoreType.DMA((2,)),
            pltpu.SemaphoreType.DMA((slots,)),
        ],
        compiler_params=pltpu.CompilerParams(vmem_limit_bytes=16 << 20),
        cost_estimate=pl.CostEstimate(
            flops=8 * rows.size, bytes_accessed=2 * slots * rows.size, transcendentals=0
        ),
    )(rows, norm_gain)


def copies_of(rows, slots):
    return pl.pallas_call(
        spread,
        out_shape=pltpu.HBM((slots,) + rows.shape, rows.dtype),
        in_specs=[pl.BlockSpec(memory_space=pltpu.VMEM)],
        out_specs=pl.BlockSpec(memory_space=pltpu.HBM),
        scratch_shapes=[pltpu.SemaphoreType.DMA((slots,))],
        compiler_params=pltpu.CompilerParams(vmem_limit_bytes=16 << 20),
        cost_estimate=pl.CostEstimate(flops=0, bytes_accessed=2 * slots * rows.size, transcendentals=0),
    )(rows)


def gather_tokens(slots):
    rows = lax.all_to_all(slots, "head", split_axis=0, concat_axis=0, tiled=True)
    return rows.reshape(-1, slots.shape[-1])


def rms_rows(part, gain):
    square = jnp.mean(part * part, axis=0, keepdims=True) + 1e-06
    return part * lax.rsqrt(square) * gain


def project_kernel(rows_ref, weight_ref, gain_ref, query_ref, pair_ref):
    head_dim = gain_ref.shape[0]
    flat = lax.dot_general(
        weight_ref[...], rows_ref[...], (((1,), (1,)), ((), ())), preferred_element_type=jnp.float32
    )
    flat = flat.astype(jnp.bfloat16).astype(jnp.float32)
    query_ref[...] = rms_rows(flat[:head_dim], gain_ref[:, 0:1]).T.astype(jnp.bfloat16)
    keys = rms_rows(flat[head_dim : 2 * head_dim], gain_ref[:, 1:2])
    pair = jnp.concatenate([keys, flat[2 * head_dim :]], axis=0)
    pair_ref[...] = pair.astype(jnp.bfloat16)


def project(rows, weight, gain):
    tokens, width = rows.shape
    head_dim = gain.shape[0]
    return pl.pallas_call(
        project_kernel,
        out_shape=[
            jax.ShapeDtypeStruct((tokens, head_dim), jnp.bfloat16),
            jax.ShapeDtypeStruct((2 * head_dim, tokens), jnp.bfloat16),
        ],
        compiler_params=pltpu.CompilerParams(vmem_limit_bytes=16 << 20),
        cost_estimate=pl.CostEstimate(
            flops=2 * tokens * width * weight.shape[0], bytes_accessed=2 * tokens * width, transcendentals=0
        ),
    )(rows, weight, gain)


def scores_of(query, pair_ref):
    head_dim = query.shape[1]
    factor = math.log2(math.e) * float(head_dim) ** (-0.5)
    keys = pair_ref[...][:head_dim]
    return jnp.dot(query, keys, preferred_element_type=jnp.float32) * factor


def weighted(scores, shift, values):
    weights = jnp.exp2(scores - shift).astype(jnp.bfloat16)
    return jnp.dot(weights, values, preferred_element_type=jnp.float32)


def finish(acc, head_dim):
    return acc[:, :head_dim] / jnp.maximum(acc[:, head_dim : head_dim + 1], 1.0)


def spread_values(pair_ref, head_dim, padded):
    part = pair_ref[...].astype(jnp.float32)[head_dim:]
    tokens = part.shape[1]
    lane = lax.broadcasted_iota(jnp.int32, (tokens, padded), 1)
    filled = jnp.concatenate([part, jnp.zeros((padded - head_dim, tokens), jnp.float32)], axis=0)
    return jnp.where(lane == head_dim, 1.0, filled.T).astype(jnp.bfloat16)


def cross_update(active_ref, first, query, far_refs, values_ref, slot, best, acc):
    several = [scores_of(query, ref) for ref in far_refs]
    newbest = best
    for n, scores in enumerate(several):
        most = jnp.max(scores, axis=1, keepdims=True)
        newbest = jnp.where(active_ref[first + n] > 0, jnp.maximum(newbest, most), newbest)
    if acc is not None:
        acc = acc * jnp.exp2(best - newbest)
    for n, scores in enumerate(several):
        shift = jnp.where(active_ref[first + n] > 0, newbest, BLANK)
        term = weighted(scores, shift, values_ref[slot + n])
        acc = term if acc is None else acc + term
    return newbest, acc


def near_kernel(tile, active_ref, query_ref, own_ref, *refs):
    far_refs, own_out_ref, state_ref, values_ref = refs[:-3], refs[-3], refs[-2], refs[-1]
    tokens, head_dim = query_ref.shape
    padded = values_ref.shape[-1]
    for n, ref in enumerate((own_ref,) + far_refs):
        values_ref[n] = spread_values(ref, head_dim, padded)

    def step(at, carry):
        rows = pl.ds(pl.multiple_of(at * tile, tile), tile)
        query = query_ref[rows, :]
        scores = scores_of(query, own_ref)
        acc = weighted(scores, jnp.max(scores, axis=1, keepdims=True), values_ref[0])
        own_out_ref[rows, :] = finish(acc, head_dim)
        start = jnp.full((tile, 1), -BLANK, jnp.float32)
        best, acc = cross_update(active_ref, 0, query, far_refs, values_ref, 1, start, None)
        lane = lax.broadcasted_iota(jnp.int32, (tile, padded), 1)
        state_ref[rows, :] = jnp.where(lane == head_dim + 1, best, acc)
        return carry

    lax.fori_loop(0, tokens // tile, step, 0, unroll=True)


def middle_kernel(tile, first, active_ref, query_ref, state_ref, *refs):
    far_refs, out_ref, values_ref = refs[:-2], refs[-2], refs[-1]
    tokens, head_dim = query_ref.shape
    padded = values_ref.shape[-1]
    for n, ref in enumerate(far_refs):
        values_ref[n] = spread_values(ref, head_dim, padded)
    lane = lax.broadcasted_iota(jnp.int32, (tile, padded), 1)
    for at in range(tokens // tile):
        rows = pl.ds(at * tile, tile)
        acc = state_ref[rows, :]
        best = acc[:, head_dim + 1 : head_dim + 2]
        best, acc = cross_update(
            active_ref, first, query_ref[rows, :], far_refs, values_ref, 0, best, acc
        )
        out_ref[rows, :] = jnp.where(lane == head_dim + 1, best, acc)


def last_kernel(
    tile, which, active_ref, query_ref, own_in_ref, state_ref, rows_ref, weight_ref, gain_ref,
    out_ref, held_ref, keys_ref, values_ref, sems,
):
    tokens, head_dim = query_ref.shape
    padded = values_ref.shape[-1]
    blocks, block, width = held_ref.shape
    copies = [
        pltpu.make_async_copy(rows_ref.at[pl.ds(n * block, block)], held_ref.at[n], sems.at[n])
        for n in range(blocks)
    ]
    for copy in copies:
        copy.start()
    even = head_dim // 16 * 16
    value_weight = weight_ref[2 * head_dim :].astype(jnp.float32)
    blank = jnp.zeros((padded - head_dim, width), jnp.float32)
    value_weight = jnp.concatenate([value_weight, blank], axis=0).astype(jnp.bfloat16)
    lane = lax.broadcasted_iota(jnp.int32, (block, padded), 1)
    across = (((1,), (1,)), ((), ()))
    for n in range(blocks):
        copies[n].wait()
        at = pl.ds(n * block, block)
        rows = held_ref[n]
        keys = lax.dot_general(
            weight_ref[even : 2 * head_dim], rows, across, preferred_element_type=jnp.float32
        )
        keys = keys[head_dim - even :].astype(jnp.bfloat16).astype(jnp.float32)
        keys_ref[:, at] = rms_rows(keys, gain_ref[:, 1:2]).astype(jnp.bfloat16)
        values = lax.dot_general(rows, value_weight, across, preferred_element_type=jnp.float32)
        values_ref[at, :] = jnp.where(lane == head_dim, 1.0, values).astype(jnp.bfloat16)
    for at in range(tokens // tile):
        rows = pl.ds(at * tile, tile)
        acc = state_ref[rows, :]
        best = acc[:, head_dim + 1 : head_dim + 2]
        factor = math.log2(math.e) * float(head_dim) ** (-0.5)
        scores = jnp.dot(query_ref[rows, :], keys_ref[...], preferred_element_type=jnp.float32) * factor
        most = jnp.maximum(best, jnp.max(scores, axis=1, keepdims=True))
        newbest = jnp.where(active_ref[which] > 0, most, best)
        shift = jnp.where(active_ref[which] > 0, newbest, BLANK)
        acc = acc * jnp.exp2(best - newbest) + weighted(scores, shift, values_ref[...])
        result = own_in_ref[rows, :] + finish(acc, head_dim)
        out_ref[at] = result.T.astype(jnp.bfloat16)


PADDED = 128


def call_attend(kernel, out_shape, blocks, tokens, head_dim, arrays):
    vmem = pl.BlockSpec(memory_space=pltpu.VMEM)
    several = isinstance(out_shape, list)
    return pl.pallas_call(
        kernel,
        out_shape=out_shape,
        in_specs=[pl.BlockSpec(memory_space=pltpu.SMEM)] + [vmem] * (len(arrays) - 1),
        out_specs=[vmem] * len(out_shape) if several else vmem,
        scratch_shapes=[pltpu.VMEM((blocks, tokens, PADDED), jnp.bfloat16)],
        compiler_params=pltpu.CompilerParams(vmem_limit_bytes=20 << 20),
        cost_estimate=pl.CostEstimate(
            flops=4 * blocks * tokens * tokens * 256,
            bytes_accessed=4 * blocks * tokens * head_dim,
            transcendentals=blocks * tokens * tokens,
        ),
    )(*arrays)


def attend_near(active, query, own, far):
    tokens, head_dim = query.shape
    out_shape = [
        jax.ShapeDtypeStruct((tokens, head_dim), jnp.float32),
        jax.ShapeDtypeStruct((tokens, PADDED), jnp.float32),
    ]
    arrays = (active, query, own, *far)
    return call_attend(
        functools.partial(near_kernel, 256), out_shape, 1 + len(far), tokens, head_dim, arrays
    )


def attend_middle(active, first, query, state, far):
    tokens, head_dim = query.shape
    out_shape = jax.ShapeDtypeStruct((tokens, PADDED), jnp.float32)
    arrays = (active, query, state, *far)
    return call_attend(
        functools.partial(middle_kernel, 256, first), out_shape, len(far), tokens, head_dim, arrays
    )


def attend_last(active, which, query, own_result, state, rows, weight, gain):
    tokens, head_dim = query.shape
    width = rows.shape[1]
    side = len(groups(0))
    blocks = 2
    smem, vmem = pl.BlockSpec(memory_space=pltpu.SMEM), pl.BlockSpec(memory_space=pltpu.VMEM)
    rows = pltpu.with_memory_space_constraint(rows, pltpu.HBM)
    return pl.pallas_call(
        functools.partial(last_kernel, tokens // side, which),
        out_shape=jax.ShapeDtypeStruct((side, head_dim, tokens // side), jnp.bfloat16),
        in_specs=[smem] + [vmem] * 3 + [pl.BlockSpec(memory_space=pltpu.HBM)] + [vmem] * 2,
        out_specs=vmem,
        scratch_shapes=[
            pltpu.VMEM((blocks, tokens // blocks, width), jnp.bfloat16),
            pltpu.VMEM((head_dim, tokens), jnp.bfloat16),
            pltpu.VMEM((tokens, PADDED), jnp.bfloat16),
            pltpu.SemaphoreType.DMA((blocks,)),
        ],
        compiler_params=pltpu.CompilerParams(vmem_limit_bytes=24 << 20),
        cost_estimate=pl.CostEstimate(
            flops=2 * tokens * width * weight.shape[0] + 4 * tokens * tokens * 256,
            bytes_accessed=2 * tokens * width,
            transcendentals=tokens * tokens,
        ),
    )(active, query, own_result, state, rows, weight, gain)


def groups(which):
    heads = lax.axis_size("head")
    side = math.isqrt(heads)
    table = [[side * i + j for j in range(side)] for i in range(side)]
    return table if which == 0 else [list(column) for column in zip(*table)]


def exchange(slots, which):
    return lax.all_to_all(
        slots, "head", split_axis=0, concat_axis=0, tiled=True, axis_index_groups=groups(which)
    )


def column_weights(weight):
    views, heads = lax.axis_size("view"), lax.axis_size("head")
    side = len(groups(0))
    core = lax.axis_index("view") % 2
    width = weight.shape[1]
    part = (width // 2 + 127) // 128 * 128
    pairs = []
    for view in range(views):
        step = side if view % 2 == 0 else -side
        for head in range(heads):
            pairs.append((view * heads + (head + step) % heads, view * heads + head))
    beside = lax.ppermute(weight, ("view", "head"), pairs)
    sent = jnp.where(core == 0, weight[:, :part], weight[:, width - part :])
    across = [(head, (head + heads // 2) % heads) for head in range(heads)]
    return jnp.concatenate([beside, lax.ppermute(sent, "head", across)], axis=1)


def project_out_kernel(place_ref, parts_ref, weight_ref, mine_ref, other_ref, out_ref):
    side = parts_ref.shape[0]
    line, core = place_ref[0], place_ref[1]
    width = weight_ref.shape[1]
    part = mine_ref.shape[1] - width

    def product(step, weight):
        rows = parts_ref[lax.rem(line + step, side)]
        return lax.dot_general(
            rows, weight, (((0,), (0,)), ((), ())), preferred_element_type=jnp.float32
        )

    turn = jnp.where(core == 0, 1, side - 1)
    total = product(0, weight_ref[...])
    total = total + product(turn, mine_ref[:, :width])
    total = total + product(side - turn, other_ref[:, :width])
    mine, other = product(side // 2, mine_ref[:, width:]), product(side // 2, other_ref[:, width:])
    low, high = jnp.where(core == 0, mine, other), jnp.where(core == 0, other, mine)
    total = total + jnp.concatenate([low[:, : width - part], high], axis=1)
    out_ref[...] = total.reshape(out_ref.shape).astype(jnp.bfloat16)


def project_out(parts, weight, mine, other):
    side, head_dim, tokens = parts.shape
    width = weight.shape[1]
    line, core = lax.axis_index("head") // side, lax.axis_index("view") % 2
    place = jnp.stack([line, core]).astype(jnp.int32)
    smem, vmem = pl.BlockSpec(memory_space=pltpu.SMEM), pl.BlockSpec(memory_space=pltpu.VMEM)
    partial = pl.pallas_call(
        project_out_kernel,
        out_shape=jax.ShapeDtypeStruct((side, tokens // side, width), jnp.bfloat16),
        in_specs=[smem] + [vmem] * 4,
        out_specs=vmem,
        compiler_params=pltpu.CompilerParams(vmem_limit_bytes=16 << 20),
        cost_estimate=pl.CostEstimate(
            flops=2 * parts.size * width, bytes_accessed=2 * (side * head_dim + tokens) * width, transcendentals=0
        ),
    )(place, parts, weight, mine, other)
    partial = exchange(partial, 0)
    return jnp.sum(partial.astype(jnp.float32), axis=0).astype(jnp.bfloat16)


def on_device(latents, norm_gain, qkv_weight, qk_gain, out_weight, intersection):
    loc_len, view_dev, width = latents.shape
    rows = latents.reshape(loc_len, width)
    levels = lax.axis_size("view").bit_length() - 1
    rounds = intersection.shape[0]
    bits = [step * (levels - 1) // (rounds - 1) for step in range(rounds)]
    gain = qk_gain[0].T
    head_dim = gain.shape[0]
    weight = qkv_weight[0]
    active = intersection[:, 0]
    heads = lax.axis_size("head")
    normed, slots = normalize(rows, norm_gain, heads)
    far_normed, gain, active = lax.optimization_barrier((partner(normed, bits[-1]), gain, active))
    far_slots = copies_of(far_normed, heads)
    every, far_slots = lax.optimization_barrier((gather_tokens(slots), far_slots))
    far_every = gather_tokens(far_slots)
    query, own = project(every, weight, gain)
    near = [partner(own, bit) for bit in bits[:-1]]
    near[0], out_rows = lax.optimization_barrier((near[0], out_weight[0]))
    mine = column_weights(out_rows)
    own_result, state = attend_near(active, query, own, near[:1])
    state = attend_middle(active, 1, query, state, near[1:])
    state, mine = lax.optimization_barrier((state, mine))
    other = partner(mine, 0)
    far_every, own_result, state = lax.optimization_barrier((far_every, own_result, state))
    attended = attend_last(active, rounds - 1, query, own_result, state, far_every, weight, gain)
    mixed = project_out(exchange(attended, 1), out_weight[0], mine, other)
    return mixed.reshape(loc_len, view_dev, width)


def solution(mesh):
    placed = (
        P("head", "view", None),
        P(),
        P("head", None, None),
        P("head", None, None),
        P("head", None, None),
        P(None, "view"),
    )
    return jax.shard_map(
        on_device, mesh=mesh, in_specs=placed, out_specs=P("head", "view", None), check_vma=False
    )
```

```python
import functools
import math
import jax
import jax.numpy as jnp
from jax import lax
from jax.experimental import pallas as pl
from jax.experimental.pallas import tpu as pltpu
from jax.sharding import PartitionSpec as P

BLANK = 1e30


def partner(array, bit):
    return lax.ppermute(array, "view", [(i, i ^ 1 << bit) for i in range(lax.axis_size("view"))])


def spread(source_ref, slots_ref, sems):
    copies = [
        pltpu.make_async_copy(source_ref, slots_ref.at[n], sems.at[n]) for n in range(slots_ref.shape[0])
    ]
    for copy in copies:
        copy.start()
    for copy in copies:
        copy.wait()


def normalize_kernel(rows_ref, gain_ref, out_ref, slots_ref, held_ref, held_gain_ref, read_sems, sems):
    reads = [
        pltpu.make_async_copy(rows_ref, held_ref, read_sems.at[0]),
        pltpu.make_async_copy(gain_ref, held_gain_ref, read_sems.at[1]),
    ]
    for read in reads:
        read.start()
    for read in reads:
        read.wait()
    values = held_ref[...].astype(jnp.float32)
    mean = jnp.mean(values, axis=-1, keepdims=True)
    centred = values - mean
    var = jnp.mean(centred * centred, axis=-1, keepdims=True)
    gain = held_gain_ref[...].reshape(1, -1)
    out_ref[...] = (centred * lax.rsqrt(var + 1e-06) * gain).astype(jnp.bfloat16)
    spread(out_ref, slots_ref, sems)


def normalize(rows, norm_gain, slots):
    vmem, hbm = pl.BlockSpec(memory_space=pltpu.VMEM), pl.BlockSpec(memory_space=pltpu.HBM)
    rows = pltpu.with_memory_space_constraint(rows, pltpu.HBM)
    norm_gain = pltpu.with_memory_space_constraint(norm_gain, pltpu.HBM)
    return pl.pallas_call(
        normalize_kernel,
        out_shape=[
            jax.ShapeDtypeStruct(rows.shape, jnp.bfloat16),
            pltpu.HBM((slots,) + rows.shape, jnp.bfloat16),
        ],
        in_specs=[hbm, hbm],
        out_specs=[vmem, hbm],
        scratch_shapes=[
            pltpu.VMEM(rows.shape, rows.dtype),
            pltpu.VMEM(norm_gain.shape, norm_gain.dtype),
            pltpu.SemaphoreType.DMA((2,)),
            pltpu.SemaphoreType.DMA((slots,)),
        ],
        compiler_params=pltpu.CompilerParams(vmem_limit_bytes=16 << 20),
        cost_estimate=pl.CostEstimate(
            flops=8 * rows.size, bytes_accessed=2 * slots * rows.size, transcendentals=0
        ),
    )(rows, norm_gain)


def copies_of(rows, slots):
    return pl.pallas_call(
        spread,
        out_shape=pltpu.HBM((slots,) + rows.shape, rows.dtype),
        in_specs=[pl.BlockSpec(memory_space=pltpu.VMEM)],
        out_specs=pl.BlockSpec(memory_space=pltpu.HBM),
        scratch_shapes=[pltpu.SemaphoreType.DMA((slots,))],
        compiler_params=pltpu.CompilerParams(vmem_limit_bytes=16 << 20),
        cost_estimate=pl.CostEstimate(flops=0, bytes_accessed=2 * slots * rows.size, transcendentals=0),
    )(rows)


def gather_tokens(slots):
    rows = lax.all_to_all(slots, "head", split_axis=0, concat_axis=0, tiled=True)
    return rows.reshape(-1, slots.shape[-1])


def rms_rows(part, gain):
    square = jnp.mean(part * part, axis=0, keepdims=True) + 1e-06
    return part * lax.rsqrt(square) * gain


def project_kernel(rows_ref, weight_ref, gain_ref, query_ref, pair_ref):
    head_dim = gain_ref.shape[0]
    flat = lax.dot_general(
        weight_ref[...], rows_ref[...], (((1,), (1,)), ((), ())), preferred_element_type=jnp.float32
    )
    flat = flat.astype(jnp.bfloat16).astype(jnp.float32)
    query_ref[...] = rms_rows(flat[:head_dim], gain_ref[:, 0:1]).T.astype(jnp.bfloat16)
    keys = rms_rows(flat[head_dim : 2 * head_dim], gain_ref[:, 1:2])
    pair = jnp.concatenate([keys, flat[2 * head_dim :]], axis=0)
    pair_ref[...] = pair.astype(jnp.bfloat16)


def project_far_kernel(rows_ref, weight_ref, gain_ref, pair_ref, held_ref, sems):
    head_dim = gain_ref.shape[0]
    skip = head_dim // 16 * 16
    blocks, block = held_ref.shape[:2]
    copies = [
        pltpu.make_async_copy(rows_ref.at[pl.ds(n * block, block)], held_ref.at[n], sems.at[n])
        for n in range(blocks)
    ]
    for copy in copies:
        copy.start()
    for n in range(blocks):
        copies[n].wait()
        flat = lax.dot_general(
            weight_ref[skip:], held_ref[n], (((1,), (1,)), ((), ())), preferred_element_type=jnp.float32
        )
        flat = flat[head_dim - skip :].astype(jnp.bfloat16).astype(jnp.float32)
        keys = rms_rows(flat[:head_dim], gain_ref[:, 1:2])
        pair = jnp.concatenate([keys, flat[head_dim:]], axis=0)
        pair_ref[:, pl.ds(n * block, block)] = pair.astype(jnp.bfloat16)


def project(rows, weight, gain):
    tokens, width = rows.shape
    head_dim = gain.shape[0]
    return pl.pallas_call(
        project_kernel,
        out_shape=[
            jax.ShapeDtypeStruct((tokens, head_dim), jnp.bfloat16),
            jax.ShapeDtypeStruct((2 * head_dim, tokens), jnp.bfloat16),
        ],
        compiler_params=pltpu.CompilerParams(vmem_limit_bytes=16 << 20),
        cost_estimate=pl.CostEstimate(
            flops=2 * tokens * width * weight.shape[0], bytes_accessed=2 * tokens * width, transcendentals=0
        ),
    )(rows, weight, gain)


def project_far(rows, weight, gain):
    tokens, width = rows.shape
    head_dim = gain.shape[0]
    blocks = 2
    vmem = pl.BlockSpec(memory_space=pltpu.VMEM)
    rows = pltpu.with_memory_space_constraint(rows, pltpu.HBM)
    return pl.pallas_call(
        project_far_kernel,
        out_shape=jax.ShapeDtypeStruct((2 * head_dim, tokens), jnp.bfloat16),
        in_specs=[pl.BlockSpec(memory_space=pltpu.HBM), vmem, vmem],
        out_specs=vmem,
        scratch_shapes=[
            pltpu.VMEM((blocks, tokens // blocks, width), jnp.bfloat16),
            pltpu.SemaphoreType.DMA((blocks,)),
        ],
        compiler_params=pltpu.CompilerParams(vmem_limit_bytes=20 << 20),
        cost_estimate=pl.CostEstimate(
            flops=2 * tokens * width * weight.shape[0], bytes_accessed=2 * tokens * width, transcendentals=0
        ),
    )(rows, weight, gain)


def scores_of(query, pair_ref):
    head_dim = query.shape[1]
    factor = math.log2(math.e) * float(head_dim) ** (-0.5)
    keys = pair_ref[...][:head_dim]
    return jnp.dot(query, keys, preferred_element_type=jnp.float32) * factor


def weighted(scores, shift, values):
    weights = jnp.exp2(scores - shift).astype(jnp.bfloat16)
    return jnp.dot(weights, values, preferred_element_type=jnp.float32)


def finish(acc, head_dim):
    return acc[:, :head_dim] / jnp.maximum(acc[:, head_dim : head_dim + 1], 1.0)


def spread_values(pair_ref, head_dim, padded):
    part = pair_ref[...].astype(jnp.float32)[head_dim:]
    tokens = part.shape[1]
    lane = lax.broadcasted_iota(jnp.int32, (tokens, padded), 1)
    filled = jnp.concatenate([part, jnp.zeros((padded - head_dim, tokens), jnp.float32)], axis=0)
    return jnp.where(lane == head_dim, 1.0, filled.T).astype(jnp.bfloat16)


def cross_update(active_ref, first, query, far_refs, values_ref, slot, best, acc):
    several = [scores_of(query, ref) for ref in far_refs]
    newbest = best
    for n, scores in enumerate(several):
        most = jnp.max(scores, axis=1, keepdims=True)
        newbest = jnp.where(active_ref[first + n] > 0, jnp.maximum(newbest, most), newbest)
    if acc is not None:
        acc = acc * jnp.exp2(best - newbest)
    for n, scores in enumerate(several):
        shift = jnp.where(active_ref[first + n] > 0, newbest, BLANK)
        term = weighted(scores, shift, values_ref[slot + n])
        acc = term if acc is None else acc + term
    return newbest, acc


def near_kernel(tile, active_ref, query_ref, own_ref, *refs):
    far_refs, own_out_ref, state_ref, values_ref = refs[:-3], refs[-3], refs[-2], refs[-1]
    tokens, head_dim = query_ref.shape
    padded = values_ref.shape[-1]
    for n, ref in enumerate((own_ref,) + far_refs):
        values_ref[n] = spread_values(ref, head_dim, padded)

    def step(at, carry):
        rows = pl.ds(pl.multiple_of(at * tile, tile), tile)
        query = query_ref[rows, :]
        scores = scores_of(query, own_ref)
        acc = weighted(scores, jnp.max(scores, axis=1, keepdims=True), values_ref[0])
        own_out_ref[rows, :] = finish(acc, head_dim)
        start = jnp.full((tile, 1), -BLANK, jnp.float32)
        best, acc = cross_update(active_ref, 0, query, far_refs, values_ref, 1, start, None)
        lane = lax.broadcasted_iota(jnp.int32, (tile, padded), 1)
        state_ref[rows, :] = jnp.where(lane == head_dim + 1, best, acc)
        return carry

    lax.fori_loop(0, tokens // tile, step, 0, unroll=True)


def middle_kernel(tile, first, active_ref, query_ref, state_ref, *refs):
    far_refs, out_ref, values_ref = refs[:-2], refs[-2], refs[-1]
    tokens, head_dim = query_ref.shape
    padded = values_ref.shape[-1]
    for n, ref in enumerate(far_refs):
        values_ref[n] = spread_values(ref, head_dim, padded)
    lane = lax.broadcasted_iota(jnp.int32, (tile, padded), 1)
    for at in range(tokens // tile):
        rows = pl.ds(at * tile, tile)
        acc = state_ref[rows, :]
        best = acc[:, head_dim + 1 : head_dim + 2]
        best, acc = cross_update(
            active_ref, first, query_ref[rows, :], far_refs, values_ref, 0, best, acc
        )
        out_ref[rows, :] = jnp.where(lane == head_dim + 1, best, acc)


def last_kernel(tile, first, active_ref, query_ref, own_in_ref, state_ref, *refs):
    far_refs, out_ref, values_ref = refs[:-2], refs[-2], refs[-1]
    tokens, head_dim = query_ref.shape
    padded = values_ref.shape[-1]
    for n, ref in enumerate(far_refs):
        values_ref[n] = spread_values(ref, head_dim, padded)

    for at in range(tokens // tile):
        rows = pl.ds(at * tile, tile)
        query = query_ref[rows, :]
        acc = state_ref[rows, :]
        best = acc[:, head_dim + 1 : head_dim + 2]
        best, acc = cross_update(active_ref, first, query, far_refs, values_ref, 0, best, acc)
        result = own_in_ref[rows, :] + finish(acc, head_dim)
        out_ref[at] = result.T.astype(jnp.bfloat16)


PADDED = 128


def call_attend(kernel, out_shape, blocks, tokens, head_dim, arrays):
    vmem = pl.BlockSpec(memory_space=pltpu.VMEM)
    several = isinstance(out_shape, list)
    return pl.pallas_call(
        kernel,
        out_shape=out_shape,
        in_specs=[pl.BlockSpec(memory_space=pltpu.SMEM)] + [vmem] * (len(arrays) - 1),
        out_specs=[vmem] * len(out_shape) if several else vmem,
        scratch_shapes=[pltpu.VMEM((blocks, tokens, PADDED), jnp.bfloat16)],
        compiler_params=pltpu.CompilerParams(vmem_limit_bytes=20 << 20),
        cost_estimate=pl.CostEstimate(
            flops=4 * blocks * tokens * tokens * 256,
            bytes_accessed=4 * blocks * tokens * head_dim,
            transcendentals=blocks * tokens * tokens,
        ),
    )(*arrays)


def attend_near(active, query, own, far):
    tokens, head_dim = query.shape
    out_shape = [
        jax.ShapeDtypeStruct((tokens, head_dim), jnp.float32),
        jax.ShapeDtypeStruct((tokens, PADDED), jnp.float32),
    ]
    arrays = (active, query, own, *far)
    return call_attend(
        functools.partial(near_kernel, 256), out_shape, 1 + len(far), tokens, head_dim, arrays
    )


def attend_middle(active, first, query, state, far):
    tokens, head_dim = query.shape
    out_shape = jax.ShapeDtypeStruct((tokens, PADDED), jnp.float32)
    arrays = (active, query, state, *far)
    return call_attend(
        functools.partial(middle_kernel, 256, first), out_shape, len(far), tokens, head_dim, arrays
    )


def attend_last(active, first, query, own_result, state, far):
    tokens, head_dim = query.shape
    side = len(groups(0))
    out_shape = jax.ShapeDtypeStruct((side, head_dim, tokens // side), jnp.bfloat16)
    arrays = (active, query, own_result, state, *far)
    return call_attend(
        functools.partial(last_kernel, tokens // side, first), out_shape, len(far), tokens, head_dim, arrays
    )


def groups(which):
    heads = lax.axis_size("head")
    side = math.isqrt(heads)
    table = [[side * i + j for j in range(side)] for i in range(side)]
    return table if which == 0 else [list(column) for column in zip(*table)]


def exchange(slots, which):
    return lax.all_to_all(
        slots, "head", split_axis=0, concat_axis=0, tiled=True, axis_index_groups=groups(which)
    )


def column_weights(weight):
    heads = lax.axis_size("head")
    side = len(groups(0))
    return [
        lax.ppermute(weight, "head", [((head + step * side) % heads, head) for head in range(heads)])
        for step in range(1, side)
    ]


def project_out_kernel(line_ref, parts_ref, *refs):
    weight_refs, out_ref = refs[:-1], refs[-1]
    side = len(weight_refs)
    total = None
    for step, weight_ref in enumerate(weight_refs):
        part = parts_ref[lax.rem(line_ref[0] + step, side)]
        term = lax.dot_general(
            part, weight_ref[...], (((0,), (0,)), ((), ())), preferred_element_type=jnp.float32
        )
        total = term if total is None else total + term
    out_ref[...] = total.reshape(out_ref.shape).astype(jnp.bfloat16)


def project_out(parts, weights):
    side, head_dim, tokens = parts.shape
    width = weights[0].shape[1]
    line = (lax.axis_index("head") // side).astype(jnp.int32)[None]
    smem, vmem = pl.BlockSpec(memory_space=pltpu.SMEM), pl.BlockSpec(memory_space=pltpu.VMEM)
    partial = pl.pallas_call(
        project_out_kernel,
        out_shape=jax.ShapeDtypeStruct((side, tokens // side, width), jnp.bfloat16),
        in_specs=[smem] + [vmem] * (1 + len(weights)),
        out_specs=vmem,
        compiler_params=pltpu.CompilerParams(vmem_limit_bytes=16 << 20),
        cost_estimate=pl.CostEstimate(
            flops=2 * parts.size * width, bytes_accessed=2 * (side * head_dim + tokens) * width, transcendentals=0
        ),
    )(line, parts, *weights)
    partial = exchange(partial, 0)
    return jnp.sum(partial.astype(jnp.float32), axis=0).astype(jnp.bfloat16)


def on_device(latents, norm_gain, qkv_weight, qk_gain, out_weight, intersection):
    loc_len, view_dev, width = latents.shape
    rows = latents.reshape(loc_len, width)
    levels = lax.axis_size("view").bit_length() - 1
    rounds = intersection.shape[0]
    bits = [step * (levels - 1) // (rounds - 1) for step in range(rounds)]
    gain = qk_gain[0].T
    head_dim = gain.shape[0]
    weight = qkv_weight[0]
    active = intersection[:, 0]
    heads = lax.axis_size("head")
    normed, slots = normalize(rows, norm_gain, heads)
    far_normed, gain, active = lax.optimization_barrier((partner(normed, bits[-1]), gain, active))
    far_slots = copies_of(far_normed, heads)
    every, far_slots = lax.optimization_barrier((gather_tokens(slots), far_slots))
    far_every = gather_tokens(far_slots)
    query, own = project(every, weight, gain)
    near = [partner(own, bit) for bit in bits[:-1]]
    near[0], out_rows = lax.optimization_barrier((near[0], out_weight[0]))
    out_weights = [out_weight[0]] + column_weights(out_rows)
    own_result, state = attend_near(active, query, own, near[:1])
    state = attend_middle(active, 1, query, state, near[1:])
    far_every, own_result, state = lax.optimization_barrier((far_every, own_result, state))
    far = [project_far(far_every, weight, gain)]
    attended = attend_last(active, rounds - 1, query, own_result, state, far)
    mixed = project_out(exchange(attended, 1), out_weights)
    return mixed.reshape(loc_len, view_dev, width)


def solution(mesh):
    placed = (
        P("head", "view", None),
        P(),
        P("head", None, None),
        P("head", None, None),
        P("head", None, None),
        P(None, "view"),
    )
    return jax.shard_map(
        on_device, mesh=mesh, in_specs=placed, out_specs=P("head", "view", None), check_vma=False
    )
```

```python
import functools
import math
import jax
import jax.numpy as jnp
from jax import lax
from jax.experimental import pallas as pl
from jax.experimental.pallas import tpu as pltpu
from jax.sharding import PartitionSpec as P

BLANK = 1e30


def partner(array, bit):
    return lax.ppermute(array, "view", [(i, i ^ 1 << bit) for i in range(lax.axis_size("view"))])


def spread(source_ref, slots_ref, sems):
    copies = [
        pltpu.make_async_copy(source_ref, slots_ref.at[n], sems.at[n]) for n in range(slots_ref.shape[0])
    ]
    for copy in copies:
        copy.start()
    for copy in copies:
        copy.wait()


def normalize_kernel(rows_ref, gain_ref, out_ref, slots_ref, held_ref, held_gain_ref, read_sems, sems):
    reads = [
        pltpu.make_async_copy(rows_ref, held_ref, read_sems.at[0]),
        pltpu.make_async_copy(gain_ref, held_gain_ref, read_sems.at[1]),
    ]
    for read in reads:
        read.start()
    for read in reads:
        read.wait()
    values = held_ref[...].astype(jnp.float32)
    mean = jnp.mean(values, axis=-1, keepdims=True)
    centred = values - mean
    var = jnp.mean(centred * centred, axis=-1, keepdims=True)
    gain = held_gain_ref[...].reshape(1, -1)
    out_ref[...] = (centred * lax.rsqrt(var + 1e-06) * gain).astype(jnp.bfloat16)
    spread(out_ref, slots_ref, sems)


def normalize(rows, norm_gain, slots):
    vmem, hbm = pl.BlockSpec(memory_space=pltpu.VMEM), pl.BlockSpec(memory_space=pltpu.HBM)
    rows = pltpu.with_memory_space_constraint(rows, pltpu.HBM)
    norm_gain = pltpu.with_memory_space_constraint(norm_gain, pltpu.HBM)
    return pl.pallas_call(
        normalize_kernel,
        out_shape=[
            jax.ShapeDtypeStruct(rows.shape, jnp.bfloat16),
            pltpu.HBM((slots,) + rows.shape, jnp.bfloat16),
        ],
        in_specs=[hbm, hbm],
        out_specs=[vmem, hbm],
        scratch_shapes=[
            pltpu.VMEM(rows.shape, rows.dtype),
            pltpu.VMEM(norm_gain.shape, norm_gain.dtype),
            pltpu.SemaphoreType.DMA((2,)),
            pltpu.SemaphoreType.DMA((slots,)),
        ],
        compiler_params=pltpu.CompilerParams(vmem_limit_bytes=16 << 20),
        cost_estimate=pl.CostEstimate(
            flops=8 * rows.size, bytes_accessed=2 * slots * rows.size, transcendentals=0
        ),
    )(rows, norm_gain)


def copies_of(rows, slots):
    return pl.pallas_call(
        spread,
        out_shape=pltpu.HBM((slots,) + rows.shape, rows.dtype),
        in_specs=[pl.BlockSpec(memory_space=pltpu.VMEM)],
        out_specs=pl.BlockSpec(memory_space=pltpu.HBM),
        scratch_shapes=[pltpu.SemaphoreType.DMA((slots,))],
        compiler_params=pltpu.CompilerParams(vmem_limit_bytes=16 << 20),
        cost_estimate=pl.CostEstimate(flops=0, bytes_accessed=2 * slots * rows.size, transcendentals=0),
    )(rows)


def gather_tokens(slots):
    rows = lax.all_to_all(slots, "head", split_axis=0, concat_axis=0, tiled=True)
    return rows.reshape(-1, slots.shape[-1])


def rms_rows(part, gain):
    square = jnp.mean(part * part, axis=0, keepdims=True) + 1e-06
    return part * lax.rsqrt(square) * gain


def project_kernel(rows_ref, weight_ref, gain_ref, query_ref, pair_ref):
    head_dim = gain_ref.shape[0]
    flat = lax.dot_general(
        weight_ref[...], rows_ref[...], (((1,), (1,)), ((), ())), preferred_element_type=jnp.float32
    )
    flat = flat.astype(jnp.bfloat16).astype(jnp.float32)
    query_ref[...] = rms_rows(flat[:head_dim], gain_ref[:, 0:1]).astype(jnp.bfloat16)
    keys = rms_rows(flat[head_dim : 2 * head_dim], gain_ref[:, 1:2])
    pair = jnp.concatenate([keys, flat[2 * head_dim :]], axis=0)
    pair_ref[...] = pair.astype(jnp.bfloat16)


def project_far_kernel(rows_ref, weight_ref, gain_ref, pair_ref, held_ref, sems):
    head_dim = gain_ref.shape[0]
    skip = head_dim // 16 * 16
    blocks, block = held_ref.shape[:2]
    copies = [
        pltpu.make_async_copy(rows_ref.at[pl.ds(n * block, block)], held_ref.at[n], sems.at[n])
        for n in range(blocks)
    ]
    for copy in copies:
        copy.start()
    for n in range(blocks):
        copies[n].wait()
        flat = lax.dot_general(
            weight_ref[skip:], held_ref[n], (((1,), (1,)), ((), ())), preferred_element_type=jnp.float32
        )
        flat = flat[head_dim - skip :].astype(jnp.bfloat16).astype(jnp.float32)
        keys = rms_rows(flat[:head_dim], gain_ref[:, 1:2])
        pair = jnp.concatenate([keys, flat[head_dim:]], axis=0)
        pair_ref[:, pl.ds(n * block, block)] = pair.astype(jnp.bfloat16)


def project(rows, weight, gain):
    tokens, width = rows.shape
    head_dim = gain.shape[0]
    return pl.pallas_call(
        project_kernel,
        out_shape=[
            jax.ShapeDtypeStruct((head_dim, tokens), jnp.bfloat16),
            jax.ShapeDtypeStruct((2 * head_dim, tokens), jnp.bfloat16),
        ],
        compiler_params=pltpu.CompilerParams(vmem_limit_bytes=16 << 20),
        cost_estimate=pl.CostEstimate(
            flops=2 * tokens * width * weight.shape[0], bytes_accessed=2 * tokens * width, transcendentals=0
        ),
    )(rows, weight, gain)


def project_far(rows, weight, gain):
    tokens, width = rows.shape
    head_dim = gain.shape[0]
    blocks = 2
    vmem = pl.BlockSpec(memory_space=pltpu.VMEM)
    rows = pltpu.with_memory_space_constraint(rows, pltpu.HBM)
    return pl.pallas_call(
        project_far_kernel,
        out_shape=jax.ShapeDtypeStruct((2 * head_dim, tokens), jnp.bfloat16),
        in_specs=[pl.BlockSpec(memory_space=pltpu.HBM), vmem, vmem],
        out_specs=vmem,
        scratch_shapes=[
            pltpu.VMEM((blocks, tokens // blocks, width), jnp.bfloat16),
            pltpu.SemaphoreType.DMA((blocks,)),
        ],
        compiler_params=pltpu.CompilerParams(vmem_limit_bytes=20 << 20),
        cost_estimate=pl.CostEstimate(
            flops=2 * tokens * width * weight.shape[0], bytes_accessed=2 * tokens * width, transcendentals=0
        ),
    )(rows, weight, gain)


def spread_pair(pair_ref, keys_ref, values_ref):
    head_dim = keys_ref.shape[1]
    pair = pair_ref[...].astype(jnp.float32)
    ones = jnp.ones((values_ref.shape[0] - head_dim, pair.shape[1]), jnp.float32)
    keys_ref[...] = pair[:head_dim].T.astype(jnp.bfloat16)
    values_ref[...] = jnp.concatenate([pair[head_dim:], ones], axis=0).astype(jnp.bfloat16)


def scores_of(keys, query):
    factor = math.log2(math.e) * float(query.shape[0]) ** (-0.5)
    return jnp.dot(keys, query, preferred_element_type=jnp.float32) * factor


def weighted(scores, shift, values):
    weights = jnp.exp2(scores - shift).astype(jnp.bfloat16)
    return jnp.dot(values, weights, preferred_element_type=jnp.float32)


def cross_update(on, scores, values, best):
    most = jnp.maximum(best, jnp.max(scores, axis=0, keepdims=True))
    newbest = jnp.where(on, most, best)
    shift = jnp.where(on, newbest, BLANK)
    return newbest, jnp.exp2(best - newbest), weighted(scores, shift, values)


def finish(acc, head_dim):
    return acc[:head_dim] / jnp.maximum(acc[head_dim : head_dim + 1], 1.0)


def near_kernel(
    tile, active_ref, query_ref, own_ref, far_ref, own_out_ref, state_ref, best_ref, keys_ref, values_ref
):
    head_dim, tokens = query_ref.shape
    for n, ref in enumerate((own_ref, far_ref)):
        spread_pair(ref, keys_ref.at[n], values_ref.at[n])
    for at in range(tokens // tile):
        columns = pl.ds(at * tile, tile)
        query = query_ref[:, columns]
        scores = scores_of(keys_ref[0], query)
        acc = weighted(scores, jnp.max(scores, axis=0, keepdims=True), values_ref[0])
        own_out_ref[:, columns] = finish(acc, head_dim)
        start = jnp.full((1, tile), -BLANK, jnp.float32)
        scores = scores_of(keys_ref[1], query)
        best, _, acc = cross_update(active_ref[0] > 0, scores, values_ref[1], start)
        state_ref[:, columns] = acc
        best_ref[:, columns] = best


def middle_kernel(
    tile, which, active_ref, query_ref, state_ref, best_ref, far_ref, state_out_ref, best_out_ref,
    keys_ref, values_ref,
):
    tokens = query_ref.shape[1]
    spread_pair(far_ref, keys_ref, values_ref)
    for at in range(tokens // tile):
        columns = pl.ds(at * tile, tile)
        scores = scores_of(keys_ref[...], query_ref[:, columns])
        on = active_ref[which] > 0
        best, factor, term = cross_update(on, scores, values_ref[...], best_ref[:, columns])
        state_out_ref[:, columns] = state_ref[:, columns] * factor + term
        best_out_ref[:, columns] = best


def last_kernel(
    tile, which, active_ref, query_ref, own_in_ref, state_ref, best_ref, far_ref, out_ref,
    keys_ref, values_ref,
):
    head_dim, tokens = query_ref.shape
    block = out_ref.shape[-1]
    spread_pair(far_ref, keys_ref, values_ref)
    for at in range(tokens // tile):
        columns = pl.ds(at * tile, tile)
        scores = scores_of(keys_ref[...], query_ref[:, columns])
        on = active_ref[which] > 0
        _, factor, term = cross_update(on, scores, values_ref[...], best_ref[:, columns])
        cross = finish(state_ref[:, columns] * factor + term, head_dim)
        result = (own_in_ref[:, columns] + cross).astype(jnp.bfloat16)
        for n in range(tile // block):
            out_ref[at * (tile // block) + n] = result[:, n * block : (n + 1) * block]


ONES = 8


def call_attend(kernel, out_shape, blocks, arrays):
    head_dim, tokens = arrays[1].shape
    lead = () if blocks == 1 else (blocks,)
    smem, vmem = pl.BlockSpec(memory_space=pltpu.SMEM), pl.BlockSpec(memory_space=pltpu.VMEM)
    several = isinstance(out_shape, list)
    return pl.pallas_call(
        kernel,
        out_shape=out_shape,
        in_specs=[smem] + [vmem] * (len(arrays) - 1),
        out_specs=[vmem] * len(out_shape) if several else vmem,
        scratch_shapes=[
            pltpu.VMEM(lead + (tokens, head_dim), jnp.bfloat16),
            pltpu.VMEM(lead + (head_dim + ONES, tokens), jnp.bfloat16),
        ],
        compiler_params=pltpu.CompilerParams(vmem_limit_bytes=24 << 20),
        cost_estimate=pl.CostEstimate(
            flops=4 * blocks * tokens * tokens * 256,
            bytes_accessed=4 * blocks * tokens * head_dim,
            transcendentals=blocks * tokens * tokens,
        ),
    )(*arrays)


def attend_near(active, query, own, far):
    head_dim, tokens = query.shape
    out_shape = [
        jax.ShapeDtypeStruct((rows, tokens), jnp.float32) for rows in (head_dim, head_dim + ONES, 1)
    ]
    kernel = functools.partial(near_kernel, tokens // 2)
    return call_attend(kernel, out_shape, 2, (active, query, own, far))


def attend_middle(active, which, query, state, best, far):
    out_shape = [jax.ShapeDtypeStruct(array.shape, jnp.float32) for array in (state, best)]
    kernel = functools.partial(middle_kernel, query.shape[1] // 2, which)
    return call_attend(kernel, out_shape, 1, (active, query, state, best, far))


def attend_last(active, which, query, own_result, state, best, far):
    head_dim, tokens = query.shape
    side = len(groups(0))
    out_shape = jax.ShapeDtypeStruct((side, head_dim, tokens // side), jnp.bfloat16)
    kernel = functools.partial(last_kernel, tokens // 2, which)
    return call_attend(kernel, out_shape, 1, (active, query, own_result, state, best, far))


def groups(which):
    heads = lax.axis_size("head")
    side = math.isqrt(heads)
    table = [[side * i + j for j in range(side)] for i in range(side)]
    return table if which == 0 else [list(column) for column in zip(*table)]


def exchange(slots, which):
    return lax.all_to_all(
        slots, "head", split_axis=0, concat_axis=0, tiled=True, axis_index_groups=groups(which)
    )


def column_weights(weight):
    heads = lax.axis_size("head")
    side = len(groups(0))
    return [
        lax.ppermute(weight, "head", [((head + step * side) % heads, head) for head in range(heads)])
        for step in range(1, side)
    ]


def project_out_kernel(line_ref, parts_ref, *refs):
    weight_refs, out_ref = refs[:-1], refs[-1]
    side = len(weight_refs)
    total = None
    for step, weight_ref in enumerate(weight_refs):
        part = parts_ref[lax.rem(line_ref[0] + step, side)]
        term = lax.dot_general(
            part, weight_ref[...], (((0,), (0,)), ((), ())), preferred_element_type=jnp.float32
        )
        total = term if total is None else total + term
    out_ref[...] = total.reshape(out_ref.shape).astype(jnp.bfloat16)


def project_out(parts, weights):
    side, head_dim, tokens = parts.shape
    width = weights[0].shape[1]
    line = (lax.axis_index("head") // side).astype(jnp.int32)[None]
    smem, vmem = pl.BlockSpec(memory_space=pltpu.SMEM), pl.BlockSpec(memory_space=pltpu.VMEM)
    partial = pl.pallas_call(
        project_out_kernel,
        out_shape=jax.ShapeDtypeStruct((side, tokens // side, width), jnp.bfloat16),
        in_specs=[smem] + [vmem] * (1 + len(weights)),
        out_specs=vmem,
        compiler_params=pltpu.CompilerParams(vmem_limit_bytes=16 << 20),
        cost_estimate=pl.CostEstimate(
            flops=2 * parts.size * width, bytes_accessed=2 * (side * head_dim + tokens) * width, transcendentals=0
        ),
    )(line, parts, *weights)
    partial = exchange(partial, 0)
    return jnp.sum(partial.astype(jnp.float32), axis=0).astype(jnp.bfloat16)


def on_device(latents, norm_gain, qkv_weight, qk_gain, out_weight, intersection):
    loc_len, view_dev, width = latents.shape
    rows = latents.reshape(loc_len, width)
    levels = lax.axis_size("view").bit_length() - 1
    rounds = intersection.shape[0]
    bits = [step * (levels - 1) // (rounds - 1) for step in range(rounds)]
    gain = qk_gain[0].T
    head_dim = gain.shape[0]
    weight = qkv_weight[0]
    active = intersection[:, 0]
    heads = lax.axis_size("head")
    normed, slots = normalize(rows, norm_gain, heads)
    far_normed, gain, active = lax.optimization_barrier((partner(normed, bits[-1]), gain, active))
    far_slots = copies_of(far_normed, heads)
    every, far_slots = lax.optimization_barrier((gather_tokens(slots), far_slots))
    far_every = gather_tokens(far_slots)
    query, own = project(every, weight, gain)
    near = [partner(own, bit) for bit in bits[:-1]]
    near[0], out_rows = lax.optimization_barrier((near[0], out_weight[0]))
    out_weights = [out_weight[0]] + column_weights(out_rows)
    own_result, state, best = attend_near(active, query, own, near[0])
    state, best = attend_middle(active, 1, query, state, best, near[1])
    far_every, own_result, state, best = lax.optimization_barrier(
        (far_every, own_result, state, best)
    )
    far = project_far(far_every, weight, gain)
    attended = attend_last(active, rounds - 1, query, own_result, state, best, far)
    mixed = project_out(exchange(attended, 1), out_weights)
    return mixed.reshape(loc_len, view_dev, width)


def solution(mesh):
    placed = (
        P("head", "view", None),
        P(),
        P("head", None, None),
        P("head", None, None),
        P("head", None, None),
        P(None, "view"),
    )
    return jax.shard_map(
        on_device, mesh=mesh, in_specs=placed, out_specs=P("head", "view", None), check_vma=False
    )
```

```python
import functools
import math
import jax
import jax.numpy as jnp
from jax import lax
from jax.experimental import pallas as pl
from jax.experimental.pallas import tpu as pltpu
from jax.sharding import PartitionSpec as P

BLANK = 1e30


def partner(array, bit):
    return lax.ppermute(array, "view", [(i, i ^ 1 << bit) for i in range(lax.axis_size("view"))])


def traded(array):
    views, heads = lax.axis_size("view"), lax.axis_size("head")
    pairs = []
    for view in range(views):
        for head in range(heads):
            if view % 2 != head % 2:
                pairs.append(((view ^ 1) * heads + (head ^ 1), view * heads + head))
    return lax.ppermute(array, ("view", "head"), pairs)


def beside(array):
    return lax.ppermute(array, "head", [(i, i ^ 1) for i in range(lax.axis_size("head"))])


def normalize_kernel(core_ref, rows_ref, gain_ref, keep_ref, give_ref, held_ref, held_gain_ref, read_sems):
    reads = [
        pltpu.make_async_copy(rows_ref, held_ref, read_sems.at[0]),
        pltpu.make_async_copy(gain_ref, held_gain_ref, read_sems.at[1]),
    ]
    for read in reads:
        read.start()
    for read in reads:
        read.wait()
    values = held_ref[...].astype(jnp.float32)
    mean = jnp.mean(values, axis=-1, keepdims=True)
    centred = values - mean
    var = jnp.mean(centred * centred, axis=-1, keepdims=True)
    gain = held_gain_ref[...].reshape(1, -1)
    normed = centred * lax.rsqrt(var + 1e-06) * gain
    half = normed.shape[0] // 2
    first = core_ref[0] == 0
    keep_ref[...] = jnp.where(first, normed[:half], normed[half:]).astype(jnp.bfloat16)
    give_ref[...] = jnp.where(first, normed[half:], normed[:half]).astype(jnp.bfloat16)


def normalize(core, rows, norm_gain):
    smem, vmem = pl.BlockSpec(memory_space=pltpu.SMEM), pl.BlockSpec(memory_space=pltpu.VMEM)
    hbm = pl.BlockSpec(memory_space=pltpu.HBM)
    half = jax.ShapeDtypeStruct((rows.shape[0] // 2, rows.shape[1]), jnp.bfloat16)
    rows = pltpu.with_memory_space_constraint(rows, pltpu.HBM)
    norm_gain = pltpu.with_memory_space_constraint(norm_gain, pltpu.HBM)
    return pl.pallas_call(
        normalize_kernel,
        out_shape=[half, half],
        in_specs=[smem, hbm, hbm],
        out_specs=[vmem, vmem],
        scratch_shapes=[
            pltpu.VMEM(rows.shape, rows.dtype),
            pltpu.VMEM(norm_gain.shape, norm_gain.dtype),
            pltpu.SemaphoreType.DMA((2,)),
        ],
        compiler_params=pltpu.CompilerParams(vmem_limit_bytes=16 << 20),
        cost_estimate=pl.CostEstimate(
            flops=8 * rows.size, bytes_accessed=4 * rows.size, transcendentals=0
        ),
    )(core, rows, norm_gain)


def deal_kernel(pair_ref, slots_ref, sems):
    copies = [
        pltpu.make_async_copy(pair_ref.at[n % 2], slots_ref.at[n], sems.at[n])
        for n in range(slots_ref.shape[0])
    ]
    for copy in copies:
        copy.start()
    for copy in copies:
        copy.wait()


def pair_kernel(core_ref, keep_ref, took_ref, pair_ref, slots_ref, sems):
    first = core_ref[0] == 0
    keep, took = keep_ref[...].astype(jnp.float32), took_ref[...].astype(jnp.float32)
    pair_ref[0] = jnp.where(first, keep, took).astype(jnp.bfloat16)
    pair_ref[1] = jnp.where(first, took, keep).astype(jnp.bfloat16)
    deal_kernel(pair_ref, slots_ref, sems)


def pair_up(core, keep, took, slots):
    smem, vmem = pl.BlockSpec(memory_space=pltpu.SMEM), pl.BlockSpec(memory_space=pltpu.VMEM)
    return pl.pallas_call(
        pair_kernel,
        out_shape=[
            jax.ShapeDtypeStruct((2,) + keep.shape, keep.dtype),
            pltpu.HBM((slots,) + keep.shape, keep.dtype),
        ],
        in_specs=[smem, vmem, vmem],
        out_specs=[vmem, pl.BlockSpec(memory_space=pltpu.HBM)],
        scratch_shapes=[pltpu.SemaphoreType.DMA((slots,))],
        compiler_params=pltpu.CompilerParams(vmem_limit_bytes=16 << 20),
        cost_estimate=pl.CostEstimate(flops=0, bytes_accessed=2 * slots * keep.size, transcendentals=0),
    )(core, keep, took)


def deal(pair, slots):
    return pl.pallas_call(
        deal_kernel,
        out_shape=pltpu.HBM((slots,) + pair.shape[1:], pair.dtype),
        in_specs=[pl.BlockSpec(memory_space=pltpu.VMEM)],
        out_specs=pl.BlockSpec(memory_space=pltpu.HBM),
        scratch_shapes=[pltpu.SemaphoreType.DMA((slots,))],
        compiler_params=pltpu.CompilerParams(vmem_limit_bytes=16 << 20),
        cost_estimate=pl.CostEstimate(flops=0, bytes_accessed=0, transcendentals=0),
    )(pair)


def gather_tokens(slots):
    rows = lax.all_to_all(slots, "head", split_axis=0, concat_axis=0, tiled=True)
    return rows.reshape(-1, slots.shape[-1])


def rms_rows(part, gain):
    square = jnp.mean(part * part, axis=0, keepdims=True) + 1e-06
    return part * lax.rsqrt(square) * gain


def project_kernel(mine_ref, other_ref, weight_ref, gain_ref, query_ref, pair_ref):
    head_dim = gain_ref.shape[0]
    for n, rows_ref in enumerate((mine_ref, other_ref)):
        block = rows_ref.shape[0]
        at = pl.ds(n * block, block)
        flat = lax.dot_general(
            weight_ref[...], rows_ref[...], (((1,), (1,)), ((), ())), preferred_element_type=jnp.float32
        )
        flat = flat.astype(jnp.bfloat16).astype(jnp.float32)
        query_ref[:, at] = rms_rows(flat[:head_dim], gain_ref[:, 0:1]).astype(jnp.bfloat16)
        keys = rms_rows(flat[head_dim : 2 * head_dim], gain_ref[:, 1:2])
        pair = jnp.concatenate([keys, flat[2 * head_dim :]], axis=0)
        pair_ref[:, at] = pair.astype(jnp.bfloat16)


def project_far_kernel(mine_ref, other_ref, weight_ref, gain_ref, pair_ref):
    head_dim = gain_ref.shape[0]
    skip = head_dim // 16 * 16
    for n, rows_ref in enumerate((mine_ref, other_ref)):
        block = rows_ref.shape[0]
        flat = lax.dot_general(
            weight_ref[skip:], rows_ref[...], (((1,), (1,)), ((), ())), preferred_element_type=jnp.float32
        )
        flat = flat[head_dim - skip :].astype(jnp.bfloat16).astype(jnp.float32)
        keys = rms_rows(flat[:head_dim], gain_ref[:, 1:2])
        pair = jnp.concatenate([keys, flat[head_dim:]], axis=0)
        pair_ref[:, pl.ds(n * block, block)] = pair.astype(jnp.bfloat16)


def project(mine, other, weight, gain, with_query):
    tokens, width = 2 * mine.shape[0], mine.shape[1]
    head_dim = gain.shape[0]
    pair = jax.ShapeDtypeStruct((2 * head_dim, tokens), jnp.bfloat16)
    query = jax.ShapeDtypeStruct((head_dim, tokens), jnp.bfloat16)
    return pl.pallas_call(
        project_kernel if with_query else project_far_kernel,
        out_shape=[query, pair] if with_query else pair,
        compiler_params=pltpu.CompilerParams(vmem_limit_bytes=16 << 20),
        cost_estimate=pl.CostEstimate(
            flops=(100 if with_query else 2) * tokens * width * weight.shape[0],
            bytes_accessed=2 * tokens * width,
            transcendentals=0,
        ),
    )(mine, other, weight, gain)


def spread_pair(pair_ref, keys_ref, values_ref):
    head_dim = keys_ref.shape[1]
    pair = pair_ref[...].astype(jnp.float32)
    ones = jnp.ones((values_ref.shape[0] - head_dim, pair.shape[1]), jnp.float32)
    keys_ref[...] = pair[:head_dim].T.astype(jnp.bfloat16)
    values_ref[...] = jnp.concatenate([pair[head_dim:], ones], axis=0).astype(jnp.bfloat16)


def scores_of(keys, query):
    factor = math.log2(math.e) * float(query.shape[0]) ** (-0.5)
    return jnp.dot(keys, query, preferred_element_type=jnp.float32) * factor


def weighted(scores, shift, values):
    weights = jnp.exp2(scores - shift).astype(jnp.bfloat16)
    return jnp.dot(values, weights, preferred_element_type=jnp.float32)


def cross_update(on, scores, values, best):
    most = jnp.maximum(best, jnp.max(scores, axis=0, keepdims=True))
    newbest = jnp.where(on, most, best)
    shift = jnp.where(on, newbest, BLANK)
    return newbest, jnp.exp2(best - newbest), weighted(scores, shift, values)


def finish(acc, head_dim):
    return acc[:head_dim] / jnp.maximum(acc[head_dim : head_dim + 1], 1.0)


def own_kernel(tile, query_ref, own_ref, own_out_ref, keys_ref, values_ref):
    head_dim, tokens = query_ref.shape
    spread_pair(own_ref, keys_ref, values_ref)
    for at in range(tokens // tile):
        columns = pl.ds(at * tile, tile)
        scores = scores_of(keys_ref[...], query_ref[:, columns])
        acc = weighted(scores, jnp.max(scores, axis=0, keepdims=True), values_ref[...])
        own_out_ref[:, columns] = finish(acc, head_dim)


def middle_kernel(
    tile, which, active_ref, query_ref, state_ref, best_ref, far_ref, state_out_ref, best_out_ref,
    keys_ref, values_ref,
):
    tokens = query_ref.shape[1]
    spread_pair(far_ref, keys_ref, values_ref)
    for at in range(tokens // tile):
        columns = pl.ds(at * tile, tile)
        scores = scores_of(keys_ref[...], query_ref[:, columns])
        on = active_ref[which] > 0
        best, factor, term = cross_update(on, scores, values_ref[...], best_ref[:, columns])
        state_out_ref[:, columns] = state_ref[:, columns] * factor + term
        best_out_ref[:, columns] = best


def last_kernel(
    tile, which, active_ref, query_ref, own_in_ref, state_ref, best_ref, far_ref, out_ref,
    keys_ref, values_ref,
):
    head_dim, tokens = query_ref.shape
    slots, _, block = out_ref.shape
    part = tile // slots
    spread_pair(far_ref, keys_ref, values_ref)
    for at in range(tokens // tile):
        columns = pl.ds(at * tile, tile)
        scores = scores_of(keys_ref[...], query_ref[:, columns])
        on = active_ref[which] > 0
        _, factor, term = cross_update(on, scores, values_ref[...], best_ref[:, columns])
        cross = finish(state_ref[:, columns] * factor + term, head_dim)
        result = (own_in_ref[:, columns] + cross).astype(jnp.bfloat16)
        for n in range(slots):
            out_ref[n, :, at * part : (at + 1) * part] = result[:, n * part : (n + 1) * part]


ONES = 8


def call_attend(kernel, out_shape, scalars, arrays):
    head_dim, tokens = arrays[0].shape
    smem, vmem = pl.BlockSpec(memory_space=pltpu.SMEM), pl.BlockSpec(memory_space=pltpu.VMEM)
    several = isinstance(out_shape, list)
    return pl.pallas_call(
        kernel,
        out_shape=out_shape,
        in_specs=[smem] * len(scalars) + [vmem] * len(arrays),
        out_specs=[vmem] * len(out_shape) if several else vmem,
        scratch_shapes=[
            pltpu.VMEM((tokens, head_dim), jnp.bfloat16),
            pltpu.VMEM((head_dim + ONES, tokens), jnp.bfloat16),
        ],
        compiler_params=pltpu.CompilerParams(vmem_limit_bytes=24 << 20),
        cost_estimate=pl.CostEstimate(
            flops=4 * tokens * tokens * 256,
            bytes_accessed=4 * tokens * head_dim,
            transcendentals=tokens * tokens,
        ),
    )(*scalars, *arrays)


def attend_own(query, own):
    out_shape = jax.ShapeDtypeStruct(query.shape, jnp.float32)
    return call_attend(
        functools.partial(own_kernel, query.shape[1] // 2), out_shape, (), (query, own)
    )


def attend_middle(active, which, query, state, best, far):
    out_shape = [jax.ShapeDtypeStruct(array.shape, jnp.float32) for array in (state, best)]
    kernel = functools.partial(middle_kernel, query.shape[1] // 2, which)
    return call_attend(kernel, out_shape, (active,), (query, state, best, far))


def attend_last(active, which, query, own_result, state, best, far):
    head_dim, tokens = query.shape
    side = len(groups(0))
    out_shape = jax.ShapeDtypeStruct((side, head_dim, tokens // side), jnp.bfloat16)
    kernel = functools.partial(last_kernel, tokens // 2, which)
    return call_attend(kernel, out_shape, (active,), (query, own_result, state, best, far))


def groups(which):
    heads = lax.axis_size("head")
    side = math.isqrt(heads)
    table = [[side * i + j for j in range(side)] for i in range(side)]
    return table if which == 0 else [list(column) for column in zip(*table)]


def exchange(slots, which):
    return lax.all_to_all(
        slots, "head", split_axis=0, concat_axis=0, tiled=True, axis_index_groups=groups(which)
    )


def column_weights(weight):
    heads = lax.axis_size("head")
    side = len(groups(0))
    return [
        lax.ppermute(weight, "head", [((head + step * side) % heads, head) for head in range(heads)])
        for step in range(1, side)
    ]


def project_out_kernel(line_ref, parts_ref, *refs):
    weight_refs, out_ref = refs[:-1], refs[-1]
    side = len(weight_refs)
    total = None
    for step, weight_ref in enumerate(weight_refs):
        part = parts_ref[lax.rem(line_ref[0] + step, side)]
        term = lax.dot_general(
            part, weight_ref[...], (((0,), (0,)), ((), ())), preferred_element_type=jnp.float32
        )
        total = term if total is None else total + term
    blocks, loc_len, width = out_ref.shape
    half = loc_len // 2
    for n in range(2):
        part = total[n * blocks * half : (n + 1) * blocks * half].reshape(blocks, half, width)
        place = line_ref[1] if n == 0 else 1 - line_ref[1]
        place = pl.ds(pl.multiple_of(place * half, half), half)
        out_ref[:, place, :] = part.astype(jnp.bfloat16)


def project_out(parts, weights):
    side, head_dim, tokens = parts.shape
    width = weights[0].shape[1]
    core = lax.axis_index("view") % 2
    line = jnp.stack([lax.axis_index("head") // side, core]).astype(jnp.int32)
    smem, vmem = pl.BlockSpec(memory_space=pltpu.SMEM), pl.BlockSpec(memory_space=pltpu.VMEM)
    partial = pl.pallas_call(
        project_out_kernel,
        out_shape=jax.ShapeDtypeStruct((side, tokens // side, width), jnp.bfloat16),
        in_specs=[smem] + [vmem] * (1 + len(weights)),
        out_specs=vmem,
        compiler_params=pltpu.CompilerParams(vmem_limit_bytes=16 << 20),
        cost_estimate=pl.CostEstimate(
            flops=2 * parts.size * width, bytes_accessed=2 * (side * head_dim + tokens) * width, transcendentals=0
        ),
    )(line, parts, *weights)
    partial = partial.astype(jnp.float32) + partner(partial, 0).astype(jnp.float32)
    partial = exchange(partial.astype(jnp.bfloat16), 0).astype(jnp.float32)
    first = sum(partial[n] for n in range(0, side, 2))
    second = sum(partial[n] for n in range(1, side, 2))
    return jnp.where(core == 0, first, second).astype(jnp.bfloat16)


def on_device(latents, norm_gain, qkv_weight, qk_gain, out_weight, intersection):
    loc_len, view_dev, width = latents.shape
    rows = latents.reshape(loc_len, width)
    levels = lax.axis_size("view").bit_length() - 1
    rounds = intersection.shape[0]
    bits = [step * (levels - 1) // (rounds - 1) for step in range(rounds)]
    head_dim, heads = qk_gain.shape[-1], lax.axis_size("head")
    core = lax.axis_index("view") % 2
    same = core == lax.axis_index("head") % 2
    keep, give = normalize(core.astype(jnp.int32)[None], rows, norm_gain)
    pair, slots = pair_up(core.astype(jnp.int32)[None], keep, partner(give, 0), heads)
    parts, left = [], qk_gain[0]
    for _ in range(3):
        parts.append(lax.reduce_precision(left, 8, 7))
        left = left - parts[-1]
    small = jnp.concatenate(parts + [jnp.broadcast_to(intersection, (rounds, head_dim)).astype(jnp.float32)])
    small = jnp.pad(small, ((0, 16 - small.shape[0]), (0, width - head_dim))).astype(jnp.bfloat16)
    packed = jnp.concatenate([qkv_weight[0], out_weight[0], small], axis=0)
    packed, pair = lax.optimization_barrier((packed, pair))
    came = traded(packed)
    far_slots = deal(partner(pair, bits[-1]), heads)
    mine, far_slots, came = lax.optimization_barrier((gather_tokens(slots), far_slots, came))
    weight = jnp.where(same, qkv_weight[0], came[: 3 * head_dim])
    out_rows = jnp.where(same, out_weight[0], came[3 * head_dim : 4 * head_dim])
    small = jnp.where(same, small, came[4 * head_dim :])[:, :head_dim].astype(jnp.float32)
    gain = (small[0:2] + (small[2:4] + small[4:6])).T
    active = small[6 : 6 + rounds, 0].astype(jnp.int32)
    far_mine = gather_tokens(far_slots)
    query, own = project(mine, partner(mine, 0), weight, gain, True)
    middle, near = partner(own, bits[1]), beside(own)
    own_result, out_rows = lax.optimization_barrier((attend_own(query, own), out_rows))
    out_weights = [out_rows] + column_weights(out_rows)
    state = jnp.zeros((head_dim + ONES, query.shape[1]), jnp.float32)
    best = jnp.full((1, query.shape[1]), -BLANK, jnp.float32)
    state, best = attend_middle(active, 0, query, state, best, near)
    far_mine, own_result, state, best, middle, out_weights = lax.optimization_barrier(
        (far_mine, own_result, state, best, middle, out_weights)
    )
    far = project(far_mine, partner(far_mine, 0), weight, gain, False)
    state, best = attend_middle(active, rounds - 1, query, state, best, far)
    attended = attend_last(active, 1, query, own_result, state, best, middle)
    mixed = project_out(exchange(attended, 1), out_weights)
    return mixed.reshape(loc_len, view_dev, width)


def solution(mesh):
    placed = (
        P("head", "view", None),
        P(),
        P("head", None, None),
        P("head", None, None),
        P("head", None, None),
        P(None, "view"),
    )
    return jax.shard_map(
        on_device, mesh=mesh, in_specs=placed, out_specs=P("head", "view", None), check_vma=False
    )
```

```python
import functools
import math
import jax
import jax.numpy as jnp
from jax import lax
from jax.experimental import pallas as pl
from jax.experimental.pallas import tpu as pltpu
from jax.sharding import PartitionSpec as P

BLANK = 1e30


def partner(array, bit):
    return lax.ppermute(array, "view", [(i, i ^ 1 << bit) for i in range(lax.axis_size("view"))])


def spread(source_ref, slots_ref, sems):
    copies = [
        pltpu.make_async_copy(source_ref, slots_ref.at[n], sems.at[n]) for n in range(slots_ref.shape[0])
    ]
    for copy in copies:
        copy.start()
    for copy in copies:
        copy.wait()


def normalize_kernel(rows_ref, gain_ref, out_ref, slots_ref, held_ref, held_gain_ref, read_sems, sems):
    reads = [
        pltpu.make_async_copy(rows_ref, held_ref, read_sems.at[0]),
        pltpu.make_async_copy(gain_ref, held_gain_ref, read_sems.at[1]),
    ]
    for read in reads:
        read.start()
    for read in reads:
        read.wait()
    values = held_ref[...].astype(jnp.float32)
    mean = jnp.mean(values, axis=-1, keepdims=True)
    centred = values - mean
    var = jnp.mean(centred * centred, axis=-1, keepdims=True)
    gain = held_gain_ref[...].reshape(1, -1)
    out_ref[...] = (centred * lax.rsqrt(var + 1e-06) * gain).astype(jnp.bfloat16)
    spread(out_ref, slots_ref, sems)


def normalize(rows, norm_gain, slots):
    vmem, hbm = pl.BlockSpec(memory_space=pltpu.VMEM), pl.BlockSpec(memory_space=pltpu.HBM)
    rows = pltpu.with_memory_space_constraint(rows, pltpu.HBM)
    norm_gain = pltpu.with_memory_space_constraint(norm_gain, pltpu.HBM)
    return pl.pallas_call(
        normalize_kernel,
        out_shape=[
            jax.ShapeDtypeStruct(rows.shape, jnp.bfloat16),
            pltpu.HBM((slots,) + rows.shape, jnp.bfloat16),
        ],
        in_specs=[hbm, hbm],
        out_specs=[vmem, hbm],
        scratch_shapes=[
            pltpu.VMEM(rows.shape, rows.dtype),
            pltpu.VMEM(norm_gain.shape, norm_gain.dtype),
            pltpu.SemaphoreType.DMA((2,)),
            pltpu.SemaphoreType.DMA((slots,)),
        ],
        compiler_params=pltpu.CompilerParams(vmem_limit_bytes=16 << 20),
        cost_estimate=pl.CostEstimate(
            flops=8 * rows.size, bytes_accessed=2 * slots * rows.size, transcendentals=0
        ),
    )(rows, norm_gain)


def copies_of(rows, slots):
    return pl.pallas_call(
        spread,
        out_shape=pltpu.HBM((slots,) + rows.shape, rows.dtype),
        in_specs=[pl.BlockSpec(memory_space=pltpu.VMEM)],
        out_specs=pl.BlockSpec(memory_space=pltpu.HBM),
        scratch_shapes=[pltpu.SemaphoreType.DMA((slots,))],
        compiler_params=pltpu.CompilerParams(vmem_limit_bytes=16 << 20),
        cost_estimate=pl.CostEstimate(flops=0, bytes_accessed=2 * slots * rows.size, transcendentals=0),
    )(rows)


def gather_tokens(slots):
    rows = lax.all_to_all(slots, "head", split_axis=0, concat_axis=0, tiled=True)
    return rows.reshape(-1, slots.shape[-1])


def rms_rows(part, gain):
    square = jnp.mean(part * part, axis=0, keepdims=True) + 1e-06
    return part * lax.rsqrt(square) * gain


def project_kernel(rows_ref, weight_ref, gain_ref, query_ref, pair_ref):
    head_dim = gain_ref.shape[0]
    flat = lax.dot_general(
        weight_ref[...], rows_ref[...], (((1,), (1,)), ((), ())), preferred_element_type=jnp.float32
    )
    flat = flat.astype(jnp.bfloat16).astype(jnp.float32)
    query_ref[...] = rms_rows(flat[:head_dim], gain_ref[:, 0:1]).astype(jnp.bfloat16)
    keys = rms_rows(flat[head_dim : 2 * head_dim], gain_ref[:, 1:2])
    pair = jnp.concatenate([keys, flat[2 * head_dim :]], axis=0)
    pair_ref[...] = pair.astype(jnp.bfloat16)


def project(rows, weight, gain):
    tokens, width = rows.shape
    head_dim = gain.shape[0]
    return pl.pallas_call(
        project_kernel,
        out_shape=[
            jax.ShapeDtypeStruct((head_dim, tokens), jnp.bfloat16),
            jax.ShapeDtypeStruct((2 * head_dim, tokens), jnp.bfloat16),
        ],
        compiler_params=pltpu.CompilerParams(vmem_limit_bytes=16 << 20),
        cost_estimate=pl.CostEstimate(
            flops=2 * tokens * width * weight.shape[0], bytes_accessed=2 * tokens * width, transcendentals=0
        ),
    )(rows, weight, gain)


def project_far_kernel(place_ref, rows_ref, weight_ref, mine_ref, other_ref, out_ref):
    tokens = rows_ref[...]
    wide = out_ref.shape[1]
    size = mine_ref.shape[0] - COLUMN
    start = weight_ref.shape[0] - wide
    even = start // 16 * 16

    def product(rows):
        return lax.dot_general(
            rows, tokens, (((1,), (1,)), ((), ())), preferred_element_type=jnp.float32
        )

    own = product(weight_ref[even:])[start - even :]
    skip = size - PAD - wide
    mine, other = product(mine_ref[COLUMN - size : COLUMN]), product(other_ref[COLUMN - size : COLUMN])
    first, second = product(mine_ref[COLUMN:]), product(other_ref[COLUMN:])
    far = jnp.where(place_ref[4] == 0, second, first)
    out_ref[place_ref[0]] = own.astype(jnp.bfloat16)
    for n, flat in enumerate((mine, other, far)):
        out_ref[place_ref[1 + n]] = flat[skip : skip + wide].astype(jnp.bfloat16)


PAD = 8
COLUMN = 304


def project_far(place, rows, weight, mine, other, head_dim):
    side = len(groups(0))
    smem, vmem = pl.BlockSpec(memory_space=pltpu.SMEM), pl.BlockSpec(memory_space=pltpu.VMEM)
    return pl.pallas_call(
        project_far_kernel,
        out_shape=jax.ShapeDtypeStruct((side, 2 * head_dim, rows.shape[0]), jnp.bfloat16),
        in_specs=[smem] + [vmem] * 4,
        out_specs=vmem,
        compiler_params=pltpu.CompilerParams(vmem_limit_bytes=16 << 20),
        cost_estimate=pl.CostEstimate(
            flops=2 * side * rows.size * weight.shape[0], bytes_accessed=4 * rows.size, transcendentals=0
        ),
    )(place, rows, weight, mine, other)


def settle_kernel(parts_ref, gain_ref, pair_ref):
    head_dim = gain_ref.shape[0]
    blocks, _, tokens = parts_ref.shape
    for n in range(blocks):
        flat = parts_ref[n].astype(jnp.float32)
        keys = rms_rows(flat[:head_dim], gain_ref[:, 1:2])
        pair = jnp.concatenate([keys, flat[head_dim:]], axis=0)
        pair_ref[:, pl.ds(n * tokens, tokens)] = pair.astype(jnp.bfloat16)


def settle(parts, gain):
    blocks, wide, tokens = parts.shape
    return pl.pallas_call(
        settle_kernel,
        out_shape=jax.ShapeDtypeStruct((wide, blocks * tokens), jnp.bfloat16),
        compiler_params=pltpu.CompilerParams(vmem_limit_bytes=16 << 20),
        cost_estimate=pl.CostEstimate(
            flops=8 * parts.size, bytes_accessed=4 * parts.size, transcendentals=0
        ),
    )(parts, gain)


def spread_pair(pair_ref, keys_ref, values_ref):
    head_dim = keys_ref.shape[1]
    pair = pair_ref[...].astype(jnp.float32)
    ones = jnp.ones((values_ref.shape[0] - head_dim, pair.shape[1]), jnp.float32)
    keys_ref[...] = pair[:head_dim].T.astype(jnp.bfloat16)
    values_ref[...] = jnp.concatenate([pair[head_dim:], ones], axis=0).astype(jnp.bfloat16)


def scores_of(keys, query):
    factor = math.log2(math.e) * float(query.shape[0]) ** (-0.5)
    return jnp.dot(keys, query, preferred_element_type=jnp.float32) * factor


def weighted(scores, shift, values):
    weights = jnp.exp2(scores - shift).astype(jnp.bfloat16)
    return jnp.dot(values, weights, preferred_element_type=jnp.float32)


def cross_update(on, scores, values, best):
    most = jnp.maximum(best, jnp.max(scores, axis=0, keepdims=True))
    newbest = jnp.where(on, most, best)
    shift = jnp.where(on, newbest, BLANK)
    return newbest, jnp.exp2(best - newbest), weighted(scores, shift, values)


def finish(acc, head_dim):
    return acc[:head_dim] / jnp.maximum(acc[head_dim : head_dim + 1], 1.0)


def near_kernel(
    tile, active_ref, query_ref, own_ref, far_ref, own_out_ref, state_ref, best_ref, keys_ref, values_ref
):
    head_dim, tokens = query_ref.shape
    for n, ref in enumerate((own_ref, far_ref)):
        spread_pair(ref, keys_ref.at[n], values_ref.at[n])
    for at in range(tokens // tile):
        columns = pl.ds(at * tile, tile)
        query = query_ref[:, columns]
        scores = scores_of(keys_ref[0], query)
        acc = weighted(scores, jnp.max(scores, axis=0, keepdims=True), values_ref[0])
        own_out_ref[:, columns] = finish(acc, head_dim)
        start = jnp.full((1, tile), -BLANK, jnp.float32)
        scores = scores_of(keys_ref[1], query)
        best, _, acc = cross_update(active_ref[0] > 0, scores, values_ref[1], start)
        state_ref[:, columns] = acc
        best_ref[:, columns] = best


def middle_kernel(
    tile, which, active_ref, query_ref, state_ref, best_ref, far_ref, state_out_ref, best_out_ref,
    keys_ref, values_ref,
):
    tokens = query_ref.shape[1]
    spread_pair(far_ref, keys_ref, values_ref)
    for at in range(tokens // tile):
        columns = pl.ds(at * tile, tile)
        scores = scores_of(keys_ref[...], query_ref[:, columns])
        on = active_ref[which] > 0
        best, factor, term = cross_update(on, scores, values_ref[...], best_ref[:, columns])
        state_out_ref[:, columns] = state_ref[:, columns] * factor + term
        best_out_ref[:, columns] = best


def last_kernel(
    tile, which, active_ref, query_ref, own_in_ref, state_ref, best_ref, far_ref, out_ref,
    keys_ref, values_ref,
):
    head_dim, tokens = query_ref.shape
    block = out_ref.shape[-1]
    spread_pair(far_ref, keys_ref, values_ref)
    for at in range(tokens // tile):
        columns = pl.ds(at * tile, tile)
        scores = scores_of(keys_ref[...], query_ref[:, columns])
        on = active_ref[which] > 0
        _, factor, term = cross_update(on, scores, values_ref[...], best_ref[:, columns])
        cross = finish(state_ref[:, columns] * factor + term, head_dim)
        result = (own_in_ref[:, columns] + cross).astype(jnp.bfloat16)
        for n in range(tile // block):
            out_ref[at * (tile // block) + n] = result[:, n * block : (n + 1) * block]


ONES = 8


def call_attend(kernel, out_shape, blocks, arrays):
    head_dim, tokens = arrays[1].shape
    lead = () if blocks == 1 else (blocks,)
    smem, vmem = pl.BlockSpec(memory_space=pltpu.SMEM), pl.BlockSpec(memory_space=pltpu.VMEM)
    several = isinstance(out_shape, list)
    return pl.pallas_call(
        kernel,
        out_shape=out_shape,
        in_specs=[smem] + [vmem] * (len(arrays) - 1),
        out_specs=[vmem] * len(out_shape) if several else vmem,
        scratch_shapes=[
            pltpu.VMEM(lead + (tokens, head_dim), jnp.bfloat16),
            pltpu.VMEM(lead + (head_dim + ONES, tokens), jnp.bfloat16),
        ],
        compiler_params=pltpu.CompilerParams(vmem_limit_bytes=24 << 20),
        cost_estimate=pl.CostEstimate(
            flops=4 * blocks * tokens * tokens * 256,
            bytes_accessed=4 * blocks * tokens * head_dim,
            transcendentals=blocks * tokens * tokens,
        ),
    )(*arrays)


def attend_near(active, query, own, far):
    head_dim, tokens = query.shape
    out_shape = [
        jax.ShapeDtypeStruct((rows, tokens), jnp.float32) for rows in (head_dim, head_dim + ONES, 1)
    ]
    kernel = functools.partial(near_kernel, tokens // 2)
    return call_attend(kernel, out_shape, 2, (active, query, own, far))


def attend_middle(active, which, query, state, best, far):
    out_shape = [jax.ShapeDtypeStruct(array.shape, jnp.float32) for array in (state, best)]
    kernel = functools.partial(middle_kernel, query.shape[1] // 2, which)
    return call_attend(kernel, out_shape, 1, (active, query, state, best, far))


def attend_last(active, which, query, own_result, state, best, far):
    head_dim, tokens = query.shape
    side = len(groups(0))
    out_shape = jax.ShapeDtypeStruct((side, head_dim, tokens // side), jnp.bfloat16)
    kernel = functools.partial(last_kernel, tokens // 2, which)
    return call_attend(kernel, out_shape, 1, (active, query, own_result, state, best, far))


def groups(which):
    heads = lax.axis_size("head")
    side = math.isqrt(heads)
    table = [[side * i + j for j in range(side)] for i in range(side)]
    return table if which == 0 else [list(column) for column in zip(*table)]


def exchange(slots, which):
    return lax.all_to_all(
        slots, "head", split_axis=0, concat_axis=0, tiled=True, axis_index_groups=groups(which)
    )


def column_weights(weight, out_weight):
    views, heads = lax.axis_size("view"), lax.axis_size("head")
    side = len(groups(0))
    core = lax.axis_index("view") % 2
    blank = jnp.zeros((PAD, weight.shape[1]), weight.dtype)
    packed = jnp.concatenate([out_weight, blank, weight, blank], axis=0)
    part = (COLUMN // 2 + 15) // 16 * 16
    pairs = []
    for view in range(views):
        step = side if view % 2 == 0 else -side
        for head in range(heads):
            pairs.append((view * heads + (head + step) % heads, view * heads + head))
    beside = lax.ppermute(packed, ("view", "head"), pairs)
    sent = jnp.where(core == 0, packed[:part], packed[COLUMN - part :])
    across = [(head, (head + heads // 2) % heads) for head in range(heads)]
    return jnp.concatenate([beside, lax.ppermute(sent, "head", across)], axis=0)


def project_out_kernel(place_ref, parts_ref, weight_ref, mine_ref, other_ref, out_ref):
    head_dim = weight_ref.shape[0]

    def rows_at(ref, start):
        return ref[start : start + head_dim + PAD].astype(jnp.float32)[:head_dim]

    first, second = rows_at(mine_ref, COLUMN), rows_at(other_ref, COLUMN)
    far = jnp.where(place_ref[4] == 0, first, second)
    weights = [rows_at(mine_ref, 0), rows_at(other_ref, 0), far]
    total = None
    for n, weight in enumerate([weight_ref[...]] + [rows.astype(jnp.bfloat16) for rows in weights]):
        term = lax.dot_general(
            parts_ref[place_ref[n]], weight, (((0,), (0,)), ((), ())), preferred_element_type=jnp.float32
        )
        total = term if total is None else total + term
    out_ref[...] = total.reshape(out_ref.shape).astype(jnp.bfloat16)


def project_out(place, parts, weight, mine, other):
    side, head_dim, tokens = parts.shape
    width = weight.shape[1]
    smem, vmem = pl.BlockSpec(memory_space=pltpu.SMEM), pl.BlockSpec(memory_space=pltpu.VMEM)
    partial = pl.pallas_call(
        project_out_kernel,
        out_shape=jax.ShapeDtypeStruct((side, tokens // side, width), jnp.bfloat16),
        in_specs=[smem] + [vmem] * 4,
        out_specs=vmem,
        compiler_params=pltpu.CompilerParams(vmem_limit_bytes=16 << 20),
        cost_estimate=pl.CostEstimate(
            flops=2 * parts.size * width, bytes_accessed=2 * (side * head_dim + tokens) * width, transcendentals=0
        ),
    )(place, parts, weight, mine, other)
    partial = exchange(partial, 0)
    return jnp.sum(partial.astype(jnp.float32), axis=0).astype(jnp.bfloat16)


def on_device(latents, norm_gain, qkv_weight, qk_gain, out_weight, intersection):
    loc_len, view_dev, width = latents.shape
    rows = latents.reshape(loc_len, width)
    levels = lax.axis_size("view").bit_length() - 1
    rounds = intersection.shape[0]
    bits = [step * (levels - 1) // (rounds - 1) for step in range(rounds)]
    gain = qk_gain[0].T
    head_dim = gain.shape[0]
    weight = qkv_weight[0]
    active = intersection[:, 0]
    heads = lax.axis_size("head")
    normed, slots = normalize(rows, norm_gain, heads)
    core, side = lax.axis_index("view") % 2, len(groups(0))
    line = lax.axis_index("head") // side
    turn = jnp.where(core == 0, 1, side - 1)
    place = jnp.stack([line, line + turn, line + side - turn, line + side // 2]) % side
    place = jnp.concatenate([place, core[None]]).astype(jnp.int32)
    far_normed, mine, gain, active = lax.optimization_barrier(
        (partner(normed, bits[-1]), column_weights(weight, out_weight[0]), gain, active)
    )
    far_slots = copies_of(far_normed, side)
    every, far_slots = lax.optimization_barrier((gather_tokens(slots), far_slots))
    far_tokens = exchange(far_slots, 0).reshape(-1, width)
    query, own = project(every, weight, gain)
    near = [partner(own, bit) for bit in bits[:-1]]
    other = partner(mine, 0)
    far_parts = project_far(place, far_tokens, weight, mine, other, head_dim)
    far_parts = exchange(far_parts, 1)
    own_result, state, best = attend_near(active, query, own, near[0])
    far_parts, own_result, state, best, near[1] = lax.optimization_barrier(
        (far_parts, own_result, state, best, near[1])
    )
    state, best = attend_middle(active, rounds - 1, query, state, best, settle(far_parts, gain))
    attended = attend_last(active, 1, query, own_result, state, best, near[1])
    mixed = project_out(place, exchange(attended, 1), out_weight[0], mine, other)
    return mixed.reshape(loc_len, view_dev, width)


def solution(mesh):
    placed = (
        P("head", "view", None),
        P(),
        P("head", None, None),
        P("head", None, None),
        P("head", None, None),
        P(None, "view"),
    )
    return jax.shard_map(
        on_device, mesh=mesh, in_specs=placed, out_specs=P("head", "view", None), check_vma=False
    )
```

```python
import functools
import math
import jax
import jax.numpy as jnp
from jax import lax
from jax.experimental import pallas as pl
from jax.experimental.pallas import tpu as pltpu
from jax.sharding import PartitionSpec as P

BLANK = 1e30


def partner(array, bit):
    return lax.ppermute(array, "view", [(i, i ^ 1 << bit) for i in range(lax.axis_size("view"))])


def spread(source_ref, slots_ref, sems):
    copies = [
        pltpu.make_async_copy(source_ref, slots_ref.at[n], sems.at[n]) for n in range(slots_ref.shape[0])
    ]
    for copy in copies:
        copy.start()
    for copy in copies:
        copy.wait()


def normalize_kernel(rows_ref, gain_ref, out_ref, slots_ref, held_ref, held_gain_ref, read_sems, sems):
    reads = [
        pltpu.make_async_copy(rows_ref, held_ref, read_sems.at[0]),
        pltpu.make_async_copy(gain_ref, held_gain_ref, read_sems.at[1]),
    ]
    for read in reads:
        read.start()
    for read in reads:
        read.wait()
    values = held_ref[...].astype(jnp.float32)
    mean = jnp.mean(values, axis=-1, keepdims=True)
    centred = values - mean
    var = jnp.mean(centred * centred, axis=-1, keepdims=True)
    gain = held_gain_ref[...].reshape(1, -1)
    out_ref[...] = (centred * lax.rsqrt(var + 1e-06) * gain).astype(jnp.bfloat16)
    spread(out_ref, slots_ref, sems)


def normalize(rows, norm_gain, slots):
    vmem, hbm = pl.BlockSpec(memory_space=pltpu.VMEM), pl.BlockSpec(memory_space=pltpu.HBM)
    rows = pltpu.with_memory_space_constraint(rows, pltpu.HBM)
    norm_gain = pltpu.with_memory_space_constraint(norm_gain, pltpu.HBM)
    return pl.pallas_call(
        normalize_kernel,
        out_shape=[
            jax.ShapeDtypeStruct(rows.shape, jnp.bfloat16),
            pltpu.HBM((slots,) + rows.shape, jnp.bfloat16),
        ],
        in_specs=[hbm, hbm],
        out_specs=[vmem, hbm],
        scratch_shapes=[
            pltpu.VMEM(rows.shape, rows.dtype),
            pltpu.VMEM(norm_gain.shape, norm_gain.dtype),
            pltpu.SemaphoreType.DMA((2,)),
            pltpu.SemaphoreType.DMA((slots,)),
        ],
        compiler_params=pltpu.CompilerParams(vmem_limit_bytes=16 << 20),
        cost_estimate=pl.CostEstimate(
            flops=8 * rows.size, bytes_accessed=2 * slots * rows.size, transcendentals=0
        ),
    )(rows, norm_gain)


def copies_of(rows, slots):
    return pl.pallas_call(
        spread,
        out_shape=pltpu.HBM((slots,) + rows.shape, rows.dtype),
        in_specs=[pl.BlockSpec(memory_space=pltpu.VMEM)],
        out_specs=pl.BlockSpec(memory_space=pltpu.HBM),
        scratch_shapes=[pltpu.SemaphoreType.DMA((slots,))],
        compiler_params=pltpu.CompilerParams(vmem_limit_bytes=16 << 20),
        cost_estimate=pl.CostEstimate(flops=0, bytes_accessed=2 * slots * rows.size, transcendentals=0),
    )(rows)


def gather_tokens(slots):
    rows = lax.all_to_all(slots, "head", split_axis=0, concat_axis=0, tiled=True)
    return rows.reshape(-1, slots.shape[-1])


def rms_rows(part, gain):
    square = jnp.mean(part * part, axis=0, keepdims=True) + 1e-06
    return part * lax.rsqrt(square) * gain


def project_kernel(rows_ref, weight_ref, gain_ref, query_ref, pair_ref):
    head_dim = gain_ref.shape[0]
    flat = lax.dot_general(
        weight_ref[...], rows_ref[...], (((1,), (1,)), ((), ())), preferred_element_type=jnp.float32
    )
    flat = flat.astype(jnp.bfloat16).astype(jnp.float32)
    query_ref[...] = rms_rows(flat[:head_dim], gain_ref[:, 0:1]).astype(jnp.bfloat16)
    keys = rms_rows(flat[head_dim : 2 * head_dim], gain_ref[:, 1:2])
    pair = jnp.concatenate([keys, flat[2 * head_dim :]], axis=0)
    pair_ref[...] = pair.astype(jnp.bfloat16)


def project(rows, weight, gain):
    tokens, width = rows.shape
    head_dim = gain.shape[0]
    return pl.pallas_call(
        project_kernel,
        out_shape=[
            jax.ShapeDtypeStruct((head_dim, tokens), jnp.bfloat16),
            jax.ShapeDtypeStruct((2 * head_dim, tokens), jnp.bfloat16),
        ],
        compiler_params=pltpu.CompilerParams(vmem_limit_bytes=16 << 20),
        cost_estimate=pl.CostEstimate(
            flops=2 * tokens * width * weight.shape[0], bytes_accessed=2 * tokens * width, transcendentals=0
        ),
    )(rows, weight, gain)


def project_far_kernel(place_ref, rows_ref, weight_ref, mine_ref, other_ref, out_ref):
    tokens = rows_ref[...]
    wide = out_ref.shape[1]
    column = weight_ref.shape[0] // 3 + PAD + wide
    start = weight_ref.shape[0] - wide
    even = start // 16 * 16

    def product(rows):
        return lax.dot_general(
            rows, tokens, (((1,), (1,)), ((), ())), preferred_element_type=jnp.float32
        )

    own = product(weight_ref[even:])[start - even :]
    mine, other = product(mine_ref[column - wide : column]), product(other_ref[column - wide : column])
    first, second = product(mine_ref[column:]), product(other_ref[column:])
    low = jnp.where(place_ref[4] == 0, first, second)
    high = jnp.where(place_ref[4] == 0, second, first)
    far = jnp.concatenate([low[column - wide :], high], axis=0)
    for n, flat in enumerate((own, mine, other, far)):
        out_ref[place_ref[n]] = flat.astype(jnp.bfloat16)


PAD = 8


def project_far(place, rows, weight, mine, other, head_dim):
    side = len(groups(0))
    smem, vmem = pl.BlockSpec(memory_space=pltpu.SMEM), pl.BlockSpec(memory_space=pltpu.VMEM)
    return pl.pallas_call(
        project_far_kernel,
        out_shape=jax.ShapeDtypeStruct((side, 2 * head_dim, rows.shape[0]), jnp.bfloat16),
        in_specs=[smem] + [vmem] * 4,
        out_specs=vmem,
        compiler_params=pltpu.CompilerParams(vmem_limit_bytes=16 << 20),
        cost_estimate=pl.CostEstimate(
            flops=2 * side * rows.size * weight.shape[0], bytes_accessed=4 * rows.size, transcendentals=0
        ),
    )(place, rows, weight, mine, other)


def settle_kernel(parts_ref, gain_ref, pair_ref):
    head_dim = gain_ref.shape[0]
    blocks, _, tokens = parts_ref.shape
    for n in range(blocks):
        flat = parts_ref[n].astype(jnp.float32)
        keys = rms_rows(flat[:head_dim], gain_ref[:, 1:2])
        pair = jnp.concatenate([keys, flat[head_dim:]], axis=0)
        pair_ref[:, pl.ds(n * tokens, tokens)] = pair.astype(jnp.bfloat16)


def settle(parts, gain):
    blocks, wide, tokens = parts.shape
    return pl.pallas_call(
        settle_kernel,
        out_shape=jax.ShapeDtypeStruct((wide, blocks * tokens), jnp.bfloat16),
        compiler_params=pltpu.CompilerParams(vmem_limit_bytes=16 << 20),
        cost_estimate=pl.CostEstimate(
            flops=8 * parts.size, bytes_accessed=4 * parts.size, transcendentals=0
        ),
    )(parts, gain)


def spread_pair(pair_ref, keys_ref, values_ref):
    head_dim = keys_ref.shape[1]
    pair = pair_ref[...].astype(jnp.float32)
    ones = jnp.ones((values_ref.shape[0] - head_dim, pair.shape[1]), jnp.float32)
    keys_ref[...] = pair[:head_dim].T.astype(jnp.bfloat16)
    values_ref[...] = jnp.concatenate([pair[head_dim:], ones], axis=0).astype(jnp.bfloat16)


def scores_of(keys, query):
    factor = math.log2(math.e) * float(query.shape[0]) ** (-0.5)
    return jnp.dot(keys, query, preferred_element_type=jnp.float32) * factor


def weighted(scores, shift, values):
    weights = jnp.exp2(scores - shift).astype(jnp.bfloat16)
    return jnp.dot(values, weights, preferred_element_type=jnp.float32)


def cross_update(on, scores, values, best):
    most = jnp.maximum(best, jnp.max(scores, axis=0, keepdims=True))
    newbest = jnp.where(on, most, best)
    shift = jnp.where(on, newbest, BLANK)
    return newbest, jnp.exp2(best - newbest), weighted(scores, shift, values)


def finish(acc, head_dim):
    return acc[:head_dim] / jnp.maximum(acc[head_dim : head_dim + 1], 1.0)


def near_kernel(
    tile, active_ref, query_ref, own_ref, far_ref, own_out_ref, state_ref, best_ref, keys_ref, values_ref
):
    head_dim, tokens = query_ref.shape
    for n, ref in enumerate((own_ref, far_ref)):
        spread_pair(ref, keys_ref.at[n], values_ref.at[n])
    for at in range(tokens // tile):
        columns = pl.ds(at * tile, tile)
        query = query_ref[:, columns]
        scores = scores_of(keys_ref[0], query)
        acc = weighted(scores, jnp.max(scores, axis=0, keepdims=True), values_ref[0])
        own_out_ref[:, columns] = finish(acc, head_dim)
        start = jnp.full((1, tile), -BLANK, jnp.float32)
        scores = scores_of(keys_ref[1], query)
        best, _, acc = cross_update(active_ref[0] > 0, scores, values_ref[1], start)
        state_ref[:, columns] = acc
        best_ref[:, columns] = best


def middle_kernel(
    tile, which, active_ref, query_ref, state_ref, best_ref, far_ref, state_out_ref, best_out_ref,
    keys_ref, values_ref,
):
    tokens = query_ref.shape[1]
    spread_pair(far_ref, keys_ref, values_ref)
    for at in range(tokens // tile):
        columns = pl.ds(at * tile, tile)
        scores = scores_of(keys_ref[...], query_ref[:, columns])
        on = active_ref[which] > 0
        best, factor, term = cross_update(on, scores, values_ref[...], best_ref[:, columns])
        state_out_ref[:, columns] = state_ref[:, columns] * factor + term
        best_out_ref[:, columns] = best


def last_kernel(
    tile, which, active_ref, query_ref, own_in_ref, state_ref, best_ref, far_ref, out_ref,
    keys_ref, values_ref,
):
    head_dim, tokens = query_ref.shape
    block = out_ref.shape[-1]
    spread_pair(far_ref, keys_ref, values_ref)
    for at in range(tokens // tile):
        columns = pl.ds(at * tile, tile)
        scores = scores_of(keys_ref[...], query_ref[:, columns])
        on = active_ref[which] > 0
        _, factor, term = cross_update(on, scores, values_ref[...], best_ref[:, columns])
        cross = finish(state_ref[:, columns] * factor + term, head_dim)
        result = (own_in_ref[:, columns] + cross).astype(jnp.bfloat16)
        for n in range(tile // block):
            out_ref[at * (tile // block) + n] = result[:, n * block : (n + 1) * block]


ONES = 8


def call_attend(kernel, out_shape, blocks, arrays):
    head_dim, tokens = arrays[1].shape
    lead = () if blocks == 1 else (blocks,)
    smem, vmem = pl.BlockSpec(memory_space=pltpu.SMEM), pl.BlockSpec(memory_space=pltpu.VMEM)
    several = isinstance(out_shape, list)
    return pl.pallas_call(
        kernel,
        out_shape=out_shape,
        in_specs=[smem] + [vmem] * (len(arrays) - 1),
        out_specs=[vmem] * len(out_shape) if several else vmem,
        scratch_shapes=[
            pltpu.VMEM(lead + (tokens, head_dim), jnp.bfloat16),
            pltpu.VMEM(lead + (head_dim + ONES, tokens), jnp.bfloat16),
        ],
        compiler_params=pltpu.CompilerParams(vmem_limit_bytes=24 << 20),
        cost_estimate=pl.CostEstimate(
            flops=4 * blocks * tokens * tokens * 256,
            bytes_accessed=4 * blocks * tokens * head_dim,
            transcendentals=blocks * tokens * tokens,
        ),
    )(*arrays)


def attend_near(active, query, own, far):
    head_dim, tokens = query.shape
    out_shape = [
        jax.ShapeDtypeStruct((rows, tokens), jnp.float32) for rows in (head_dim, head_dim + ONES, 1)
    ]
    kernel = functools.partial(near_kernel, tokens // 2)
    return call_attend(kernel, out_shape, 2, (active, query, own, far))


def attend_middle(active, which, query, state, best, far):
    out_shape = [jax.ShapeDtypeStruct(array.shape, jnp.float32) for array in (state, best)]
    kernel = functools.partial(middle_kernel, query.shape[1] // 2, which)
    return call_attend(kernel, out_shape, 1, (active, query, state, best, far))


def attend_last(active, which, query, own_result, state, best, far):
    head_dim, tokens = query.shape
    side = len(groups(0))
    out_shape = jax.ShapeDtypeStruct((side, head_dim, tokens // side), jnp.bfloat16)
    kernel = functools.partial(last_kernel, tokens // 2, which)
    return call_attend(kernel, out_shape, 1, (active, query, own_result, state, best, far))


def groups(which):
    heads = lax.axis_size("head")
    side = math.isqrt(heads)
    table = [[side * i + j for j in range(side)] for i in range(side)]
    return table if which == 0 else [list(column) for column in zip(*table)]


def exchange(slots, which):
    return lax.all_to_all(
        slots, "head", split_axis=0, concat_axis=0, tiled=True, axis_index_groups=groups(which)
    )


def column_weights(weight, out_weight):
    views, heads = lax.axis_size("view"), lax.axis_size("head")
    side = len(groups(0))
    core = lax.axis_index("view") % 2
    blank = jnp.zeros((PAD, weight.shape[1]), weight.dtype)
    packed = jnp.concatenate([out_weight, blank, weight[out_weight.shape[0] :]], axis=0)
    part = packed.shape[0] // 2
    pairs = []
    for view in range(views):
        step = side if view % 2 == 0 else -side
        for head in range(heads):
            pairs.append((view * heads + (head + step) % heads, view * heads + head))
    beside = lax.ppermute(packed, ("view", "head"), pairs)
    sent = jnp.where(core == 0, packed[:part], packed[part:])
    across = [(head, (head + heads // 2) % heads) for head in range(heads)]
    return jnp.concatenate([beside, lax.ppermute(sent, "head", across)], axis=0)


def project_out_kernel(place_ref, parts_ref, weight_ref, mine_ref, other_ref, out_ref):
    head_dim = weight_ref.shape[0]

    def rows_at(ref, start):
        return ref[start : start + head_dim + PAD].astype(jnp.float32)[:head_dim]

    column = 3 * head_dim + PAD
    first, second = rows_at(mine_ref, column), rows_at(other_ref, column)
    far = jnp.where(place_ref[4] == 0, first, second)
    weights = [rows_at(mine_ref, 0), rows_at(other_ref, 0), far]
    total = None
    for n, weight in enumerate([weight_ref[...]] + [rows.astype(jnp.bfloat16) for rows in weights]):
        term = lax.dot_general(
            parts_ref[place_ref[n]], weight, (((0,), (0,)), ((), ())), preferred_element_type=jnp.float32
        )
        total = term if total is None else total + term
    out_ref[...] = total.reshape(out_ref.shape).astype(jnp.bfloat16)


def project_out(place, parts, weight, mine, other):
    side, head_dim, tokens = parts.shape
    width = weight.shape[1]
    smem, vmem = pl.BlockSpec(memory_space=pltpu.SMEM), pl.BlockSpec(memory_space=pltpu.VMEM)
    partial = pl.pallas_call(
        project_out_kernel,
        out_shape=jax.ShapeDtypeStruct((side, tokens // side, width), jnp.bfloat16),
        in_specs=[smem] + [vmem] * 4,
        out_specs=vmem,
        compiler_params=pltpu.CompilerParams(vmem_limit_bytes=16 << 20),
        cost_estimate=pl.CostEstimate(
            flops=2 * parts.size * width, bytes_accessed=2 * (side * head_dim + tokens) * width, transcendentals=0
        ),
    )(place, parts, weight, mine, other)
    partial = exchange(partial, 0)
    return jnp.sum(partial.astype(jnp.float32), axis=0).astype(jnp.bfloat16)


def on_device(latents, norm_gain, qkv_weight, qk_gain, out_weight, intersection):
    loc_len, view_dev, width = latents.shape
    rows = latents.reshape(loc_len, width)
    levels = lax.axis_size("view").bit_length() - 1
    rounds = intersection.shape[0]
    bits = [step * (levels - 1) // (rounds - 1) for step in range(rounds)]
    gain = qk_gain[0].T
    head_dim = gain.shape[0]
    weight = qkv_weight[0]
    active = intersection[:, 0]
    heads = lax.axis_size("head")
    normed, slots = normalize(rows, norm_gain, heads)
    core, side = lax.axis_index("view") % 2, len(groups(0))
    line = lax.axis_index("head") // side
    turn = jnp.where(core == 0, 1, side - 1)
    place = jnp.stack([line, line + turn, line + side - turn, line + side // 2]) % side
    place = jnp.concatenate([place, core[None]]).astype(jnp.int32)
    far_normed, gain, active = lax.optimization_barrier((partner(normed, bits[-1]), gain, active))
    far_slots = copies_of(far_normed, side)
    every, far_slots, mine = lax.optimization_barrier(
        (gather_tokens(slots), far_slots, column_weights(weight, out_weight[0]))
    )
    far_tokens = exchange(far_slots, 0).reshape(-1, width)
    query, own = project(every, weight, gain)
    near = [partner(own, bit) for bit in bits[:-1]]
    other = partner(mine, 0)
    far_parts = project_far(place, far_tokens, weight, mine, other, head_dim)
    far_parts = exchange(far_parts, 1)
    own_result, state, best = attend_near(active, query, own, near[0])
    far_parts, own_result, state, best, near[1] = lax.optimization_barrier(
        (far_parts, own_result, state, best, near[1])
    )
    state, best = attend_middle(active, rounds - 1, query, state, best, settle(far_parts, gain))
    attended = attend_last(active, 1, query, own_result, state, best, near[1])
    mixed = project_out(place, exchange(attended, 1), out_weight[0], mine, other)
    return mixed.reshape(loc_len, view_dev, width)


def solution(mesh):
    placed = (
        P("head", "view", None),
        P(),
        P("head", None, None),
        P("head", None, None),
        P("head", None, None),
        P(None, "view"),
    )
    return jax.shard_map(
        on_device, mesh=mesh, in_specs=placed, out_specs=P("head", "view", None), check_vma=False
    )
```

```python
import functools
import math
import jax
import jax.numpy as jnp
from jax import lax
from jax.experimental import pallas as pl
from jax.experimental.pallas import tpu as pltpu
from jax.sharding import PartitionSpec as P

BLANK = 1e30


def partner(array, bit):
    return lax.ppermute(array, "view", [(i, i ^ 1 << bit) for i in range(lax.axis_size("view"))])


def spread(source_ref, slots_ref, sems):
    copies = [
        pltpu.make_async_copy(source_ref, slots_ref.at[n], sems.at[n]) for n in range(slots_ref.shape[0])
    ]
    for copy in copies:
        copy.start()
    for copy in copies:
        copy.wait()


def normalize_kernel(rows_ref, gain_ref, out_ref, slots_ref, held_ref, held_gain_ref, read_sems, sems):
    reads = [
        pltpu.make_async_copy(rows_ref, held_ref, read_sems.at[0]),
        pltpu.make_async_copy(gain_ref, held_gain_ref, read_sems.at[1]),
    ]
    for read in reads:
        read.start()
    for read in reads:
        read.wait()
    values = held_ref[...].astype(jnp.float32)
    mean = jnp.mean(values, axis=-1, keepdims=True)
    centred = values - mean
    var = jnp.mean(centred * centred, axis=-1, keepdims=True)
    gain = held_gain_ref[...].reshape(1, -1)
    out_ref[...] = (centred * lax.rsqrt(var + 1e-06) * gain).astype(jnp.bfloat16)
    spread(out_ref, slots_ref, sems)


def normalize(rows, norm_gain, slots):
    vmem, hbm = pl.BlockSpec(memory_space=pltpu.VMEM), pl.BlockSpec(memory_space=pltpu.HBM)
    rows = pltpu.with_memory_space_constraint(rows, pltpu.HBM)
    norm_gain = pltpu.with_memory_space_constraint(norm_gain, pltpu.HBM)
    return pl.pallas_call(
        normalize_kernel,
        out_shape=[
            jax.ShapeDtypeStruct(rows.shape, jnp.bfloat16),
            pltpu.HBM((slots,) + rows.shape, jnp.bfloat16),
        ],
        in_specs=[hbm, hbm],
        out_specs=[vmem, hbm],
        scratch_shapes=[
            pltpu.VMEM(rows.shape, rows.dtype),
            pltpu.VMEM(norm_gain.shape, norm_gain.dtype),
            pltpu.SemaphoreType.DMA((2,)),
            pltpu.SemaphoreType.DMA((slots,)),
        ],
        compiler_params=pltpu.CompilerParams(vmem_limit_bytes=16 << 20),
        cost_estimate=pl.CostEstimate(
            flops=8 * rows.size, bytes_accessed=2 * slots * rows.size, transcendentals=0
        ),
    )(rows, norm_gain)


def copies_of(rows, slots):
    return pl.pallas_call(
        spread,
        out_shape=pltpu.HBM((slots,) + rows.shape, rows.dtype),
        in_specs=[pl.BlockSpec(memory_space=pltpu.VMEM)],
        out_specs=pl.BlockSpec(memory_space=pltpu.HBM),
        scratch_shapes=[pltpu.SemaphoreType.DMA((slots,))],
        compiler_params=pltpu.CompilerParams(vmem_limit_bytes=16 << 20),
        cost_estimate=pl.CostEstimate(flops=0, bytes_accessed=2 * slots * rows.size, transcendentals=0),
    )(rows)


def gather_tokens(slots):
    rows = lax.all_to_all(slots, "head", split_axis=0, concat_axis=0, tiled=True)
    return rows.reshape(-1, slots.shape[-1])


def rms_rows(part, gain):
    square = jnp.mean(part * part, axis=0, keepdims=True) + 1e-06
    return part * lax.rsqrt(square) * gain


def project_kernel(rows_ref, weight_ref, gain_ref, query_ref, pair_ref):
    head_dim = gain_ref.shape[0]
    flat = lax.dot_general(
        weight_ref[...], rows_ref[...], (((1,), (1,)), ((), ())), preferred_element_type=jnp.float32
    )
    flat = flat.astype(jnp.bfloat16).astype(jnp.float32)
    query_ref[...] = rms_rows(flat[:head_dim], gain_ref[:, 0:1]).astype(jnp.bfloat16)
    keys = rms_rows(flat[head_dim : 2 * head_dim], gain_ref[:, 1:2])
    pair = jnp.concatenate([keys, flat[2 * head_dim :]], axis=0)
    pair_ref[...] = pair.astype(jnp.bfloat16)


def project(rows, weight, gain):
    tokens, width = rows.shape
    head_dim = gain.shape[0]
    return pl.pallas_call(
        project_kernel,
        out_shape=[
            jax.ShapeDtypeStruct((head_dim, tokens), jnp.bfloat16),
            jax.ShapeDtypeStruct((2 * head_dim, tokens), jnp.bfloat16),
        ],
        compiler_params=pltpu.CompilerParams(vmem_limit_bytes=16 << 20),
        cost_estimate=pl.CostEstimate(
            flops=2 * tokens * width * weight.shape[0], bytes_accessed=2 * tokens * width, transcendentals=0
        ),
    )(rows, weight, gain)


def project_far_kernel(
    place_ref, rows_ref, weight_ref, mine_ref, other_ref, mine_half_ref, other_half_ref, out_ref
):
    wide = out_ref.shape[1]
    column, part = mine_ref.shape[0], mine_half_ref.shape[0]
    start = weight_ref.shape[0] - wide
    even = start // 16 * 16
    stacked = jnp.concatenate(
        [
            mine_ref[column - wide :],
            other_ref[column - wide :],
            mine_half_ref[...],
            other_half_ref[...],
            weight_ref[even:],
        ],
        axis=0,
    )
    flat = lax.dot_general(
        stacked, rows_ref[...], (((1,), (1,)), ((), ())), preferred_element_type=jnp.float32
    )
    mine, other = flat[:wide], flat[wide : 2 * wide]
    first, second = flat[2 * wide : 2 * wide + part], flat[2 * wide + part : 2 * wide + 2 * part]
    own = flat[2 * wide + 2 * part + start - even :]
    low = jnp.where(place_ref[4] == 0, first, second)
    high = jnp.where(place_ref[4] == 0, second, first)
    far = jnp.concatenate([low[column - wide :], high], axis=0)
    for n, rows in enumerate((own, mine, other, far)):
        out_ref[place_ref[n]] = rows.astype(jnp.bfloat16)


PAD = 8


def project_far(place, rows, weight, column, head_dim):
    side = len(groups(0))
    smem, vmem = pl.BlockSpec(memory_space=pltpu.SMEM), pl.BlockSpec(memory_space=pltpu.VMEM)
    return pl.pallas_call(
        project_far_kernel,
        out_shape=jax.ShapeDtypeStruct((side, 2 * head_dim, rows.shape[0]), jnp.bfloat16),
        in_specs=[smem] + [vmem] * (2 + len(column)),
        out_specs=vmem,
        compiler_params=pltpu.CompilerParams(vmem_limit_bytes=16 << 20),
        cost_estimate=pl.CostEstimate(
            flops=2 * side * rows.size * weight.shape[0], bytes_accessed=4 * rows.size, transcendentals=0
        ),
    )(place, rows, weight, *column)


def settle_kernel(parts_ref, gain_ref, pair_ref):
    head_dim = gain_ref.shape[0]
    blocks, _, tokens = parts_ref.shape
    for n in range(blocks):
        flat = parts_ref[n].astype(jnp.float32)
        keys = rms_rows(flat[:head_dim], gain_ref[:, 1:2])
        pair = jnp.concatenate([keys, flat[head_dim:]], axis=0)
        pair_ref[:, pl.ds(n * tokens, tokens)] = pair.astype(jnp.bfloat16)


def settle(parts, gain):
    blocks, wide, tokens = parts.shape
    return pl.pallas_call(
        settle_kernel,
        out_shape=jax.ShapeDtypeStruct((wide, blocks * tokens), jnp.bfloat16),
        compiler_params=pltpu.CompilerParams(vmem_limit_bytes=16 << 20),
        cost_estimate=pl.CostEstimate(
            flops=8 * parts.size, bytes_accessed=4 * parts.size, transcendentals=0
        ),
    )(parts, gain)


def spread_pair(pair_ref, keys_ref, values_ref):
    head_dim = keys_ref.shape[1]
    pair = pair_ref[...].astype(jnp.float32)
    ones = jnp.ones((values_ref.shape[0] - head_dim, pair.shape[1]), jnp.float32)
    keys_ref[...] = pair[:head_dim].T.astype(jnp.bfloat16)
    values_ref[...] = jnp.concatenate([pair[head_dim:], ones], axis=0).astype(jnp.bfloat16)


def scores_of(keys, query):
    factor = math.log2(math.e) * float(query.shape[0]) ** (-0.5)
    return jnp.dot(keys, query, preferred_element_type=jnp.float32) * factor


def weighted(scores, shift, values):
    weights = jnp.exp2(scores - shift).astype(jnp.bfloat16)
    return jnp.dot(values, weights, preferred_element_type=jnp.float32)


def cross_update(on, scores, values, best):
    most = jnp.maximum(best, jnp.max(scores, axis=0, keepdims=True))
    newbest = jnp.where(on, most, best)
    shift = jnp.where(on, newbest, BLANK)
    return newbest, jnp.exp2(best - newbest), weighted(scores, shift, values)


def finish(acc, head_dim):
    return acc[:head_dim] / jnp.maximum(acc[head_dim : head_dim + 1], 1.0)


def near_kernel(
    tile, active_ref, query_ref, own_ref, far_ref, own_out_ref, state_ref, best_ref, keys_ref, values_ref
):
    head_dim, tokens = query_ref.shape
    for n, ref in enumerate((own_ref, far_ref)):
        spread_pair(ref, keys_ref.at[n], values_ref.at[n])
    for at in range(tokens // tile):
        columns = pl.ds(at * tile, tile)
        query = query_ref[:, columns]
        scores = scores_of(keys_ref[0], query)
        acc = weighted(scores, jnp.max(scores, axis=0, keepdims=True), values_ref[0])
        own_out_ref[:, columns] = finish(acc, head_dim)
        start = jnp.full((1, tile), -BLANK, jnp.float32)
        scores = scores_of(keys_ref[1], query)
        best, _, acc = cross_update(active_ref[0] > 0, scores, values_ref[1], start)
        state_ref[:, columns] = acc
        best_ref[:, columns] = best


def middle_kernel(
    tile, which, active_ref, query_ref, state_ref, best_ref, far_ref, state_out_ref, best_out_ref,
    keys_ref, values_ref,
):
    tokens = query_ref.shape[1]
    spread_pair(far_ref, keys_ref, values_ref)
    for at in range(tokens // tile):
        columns = pl.ds(at * tile, tile)
        scores = scores_of(keys_ref[...], query_ref[:, columns])
        on = active_ref[which] > 0
        best, factor, term = cross_update(on, scores, values_ref[...], best_ref[:, columns])
        state_out_ref[:, columns] = state_ref[:, columns] * factor + term
        best_out_ref[:, columns] = best


def last_kernel(
    tile, which, active_ref, query_ref, own_in_ref, state_ref, best_ref, far_ref, out_ref,
    keys_ref, values_ref,
):
    head_dim, tokens = query_ref.shape
    block = out_ref.shape[-1]
    spread_pair(far_ref, keys_ref, values_ref)
    for at in range(tokens // tile):
        columns = pl.ds(at * tile, tile)
        scores = scores_of(keys_ref[...], query_ref[:, columns])
        on = active_ref[which] > 0
        _, factor, term = cross_update(on, scores, values_ref[...], best_ref[:, columns])
        cross = finish(state_ref[:, columns] * factor + term, head_dim)
        result = (own_in_ref[:, columns] + cross).astype(jnp.bfloat16)
        for n in range(tile // block):
            out_ref[at * (tile // block) + n] = result[:, n * block : (n + 1) * block]


ONES = 8


def call_attend(kernel, out_shape, blocks, arrays):
    head_dim, tokens = arrays[1].shape
    lead = () if blocks == 1 else (blocks,)
    smem, vmem = pl.BlockSpec(memory_space=pltpu.SMEM), pl.BlockSpec(memory_space=pltpu.VMEM)
    several = isinstance(out_shape, list)
    return pl.pallas_call(
        kernel,
        out_shape=out_shape,
        in_specs=[smem] + [vmem] * (len(arrays) - 1),
        out_specs=[vmem] * len(out_shape) if several else vmem,
        scratch_shapes=[
            pltpu.VMEM(lead + (tokens, head_dim), jnp.bfloat16),
            pltpu.VMEM(lead + (head_dim + ONES, tokens), jnp.bfloat16),
        ],
        compiler_params=pltpu.CompilerParams(vmem_limit_bytes=24 << 20),
        cost_estimate=pl.CostEstimate(
            flops=4 * blocks * tokens * tokens * 256,
            bytes_accessed=4 * blocks * tokens * head_dim,
            transcendentals=blocks * tokens * tokens,
        ),
    )(*arrays)


def attend_near(active, query, own, far):
    head_dim, tokens = query.shape
    out_shape = [
        jax.ShapeDtypeStruct((rows, tokens), jnp.float32) for rows in (head_dim, head_dim + ONES, 1)
    ]
    kernel = functools.partial(near_kernel, tokens // 2)
    return call_attend(kernel, out_shape, 2, (active, query, own, far))


def attend_middle(active, which, query, state, best, far):
    out_shape = [jax.ShapeDtypeStruct(array.shape, jnp.float32) for array in (state, best)]
    kernel = functools.partial(middle_kernel, query.shape[1] // 2, which)
    return call_attend(kernel, out_shape, 1, (active, query, state, best, far))


def attend_last(active, which, query, own_result, state, best, far):
    head_dim, tokens = query.shape
    side = len(groups(0))
    out_shape = jax.ShapeDtypeStruct((side, head_dim, tokens // side), jnp.bfloat16)
    kernel = functools.partial(last_kernel, tokens // 2, which)
    return call_attend(kernel, out_shape, 1, (active, query, own_result, state, best, far))


def groups(which):
    heads = lax.axis_size("head")
    side = math.isqrt(heads)
    table = [[side * i + j for j in range(side)] for i in range(side)]
    return table if which == 0 else [list(column) for column in zip(*table)]


def exchange(slots, which):
    return lax.all_to_all(
        slots, "head", split_axis=0, concat_axis=0, tiled=True, axis_index_groups=groups(which)
    )


def column_weights(weight, out_weight):
    views, heads = lax.axis_size("view"), lax.axis_size("head")
    side = len(groups(0))
    core = lax.axis_index("view") % 2
    blank = jnp.zeros((PAD, weight.shape[1]), weight.dtype)
    packed = jnp.concatenate([out_weight, blank, weight[out_weight.shape[0] :]], axis=0)
    part = packed.shape[0] // 2
    pairs = []
    for view in range(views):
        step = side if view % 2 == 0 else -side
        for head in range(heads):
            pairs.append((view * heads + (head + step) % heads, view * heads + head))
    beside = lax.ppermute(packed, ("view", "head"), pairs)
    sent = jnp.where(core == 0, packed[:part], packed[part:])
    across = [(head, (head + heads // 2) % heads) for head in range(heads)]
    return beside, lax.ppermute(sent, "head", across)


def project_out_kernel(
    place_ref, parts_ref, weight_ref, mine_ref, other_ref, mine_half_ref, other_half_ref, out_ref
):
    head_dim = weight_ref.shape[0]

    def rows_at(ref):
        return ref[: head_dim + PAD].astype(jnp.float32)[:head_dim]

    first, second = rows_at(mine_half_ref), rows_at(other_half_ref)
    far = jnp.where(place_ref[4] == 0, first, second)
    weights = [rows_at(mine_ref), rows_at(other_ref), far]
    total = None
    for n, weight in enumerate([weight_ref[...]] + [rows.astype(jnp.bfloat16) for rows in weights]):
        term = lax.dot_general(
            parts_ref[place_ref[n]], weight, (((0,), (0,)), ((), ())), preferred_element_type=jnp.float32
        )
        total = term if total is None else total + term
    out_ref[...] = total.reshape(out_ref.shape).astype(jnp.bfloat16)


def project_out(place, parts, weight, column):
    side, head_dim, tokens = parts.shape
    width = weight.shape[1]
    smem, vmem = pl.BlockSpec(memory_space=pltpu.SMEM), pl.BlockSpec(memory_space=pltpu.VMEM)
    partial = pl.pallas_call(
        project_out_kernel,
        out_shape=jax.ShapeDtypeStruct((side, tokens // side, width), jnp.bfloat16),
        in_specs=[smem] + [vmem] * (2 + len(column)),
        out_specs=vmem,
        compiler_params=pltpu.CompilerParams(vmem_limit_bytes=16 << 20),
        cost_estimate=pl.CostEstimate(
            flops=2 * parts.size * width, bytes_accessed=2 * (side * head_dim + tokens) * width, transcendentals=0
        ),
    )(place, parts, weight, *column)
    partial = exchange(partial, 0)
    return jnp.sum(partial.astype(jnp.float32), axis=0).astype(jnp.bfloat16)


def on_device(latents, norm_gain, qkv_weight, qk_gain, out_weight, intersection):
    loc_len, view_dev, width = latents.shape
    rows = latents.reshape(loc_len, width)
    levels = lax.axis_size("view").bit_length() - 1
    rounds = intersection.shape[0]
    bits = [step * (levels - 1) // (rounds - 1) for step in range(rounds)]
    gain = qk_gain[0].T
    head_dim = gain.shape[0]
    weight = qkv_weight[0]
    active = intersection[:, 0]
    heads = lax.axis_size("head")
    normed, slots = normalize(rows, norm_gain, heads)
    core, side = lax.axis_index("view") % 2, len(groups(0))
    line = lax.axis_index("head") // side
    turn = jnp.where(core == 0, 1, side - 1)
    place = jnp.stack([line, line + turn, line + side - turn, line + side // 2]) % side
    place = jnp.concatenate([place, core[None]]).astype(jnp.int32)
    far_normed, gain, active = lax.optimization_barrier((partner(normed, bits[-1]), gain, active))
    far_slots = copies_of(far_normed, side)
    whole, half = column_weights(weight, out_weight[0])
    every, far_slots, whole = lax.optimization_barrier((gather_tokens(slots), far_slots, whole))
    far_tokens = exchange(far_slots, 0).reshape(-1, width)
    query, own = project(every, weight, gain)
    near = [partner(own, bit) for bit in bits[:-1]]
    column = [whole, partner(whole, 0), half, partner(half, 0)]
    far_parts = project_far(place, far_tokens, weight, column, head_dim)
    far_parts = exchange(far_parts, 1)
    own_result, state, best = attend_near(active, query, own, near[0])
    far_parts, own_result, state, best, near[1] = lax.optimization_barrier(
        (far_parts, own_result, state, best, near[1])
    )
    state, best = attend_middle(active, rounds - 1, query, state, best, settle(far_parts, gain))
    attended = attend_last(active, 1, query, own_result, state, best, near[1])
    mixed = project_out(place, exchange(attended, 1), out_weight[0], column)
    return mixed.reshape(loc_len, view_dev, width)


def solution(mesh):
    placed = (
        P("head", "view", None),
        P(),
        P("head", None, None),
        P("head", None, None),
        P("head", None, None),
        P(None, "view"),
    )
    return jax.shard_map(
        on_device, mesh=mesh, in_specs=placed, out_specs=P("head", "view", None), check_vma=False
    )
```

```python
import functools
import math
import jax
import jax.numpy as jnp
from jax import lax
from jax.experimental import pallas as pl
from jax.experimental.pallas import tpu as pltpu
from jax.sharding import PartitionSpec as P

BLANK = 1e30


def partner(array, bit):
    return lax.ppermute(array, "view", [(i, i ^ 1 << bit) for i in range(lax.axis_size("view"))])


def spread(source_ref, slots_ref, sems):
    copies = [
        pltpu.make_async_copy(source_ref, slots_ref.at[n], sems.at[n]) for n in range(slots_ref.shape[0])
    ]
    for copy in copies:
        copy.start()
    for copy in copies:
        copy.wait()


def normalize_kernel(rows_ref, gain_ref, out_ref, slots_ref, held_ref, held_gain_ref, read_sems, sems):
    reads = [
        pltpu.make_async_copy(rows_ref, held_ref, read_sems.at[0]),
        pltpu.make_async_copy(gain_ref, held_gain_ref, read_sems.at[1]),
    ]
    for read in reads:
        read.start()
    for read in reads:
        read.wait()
    values = held_ref[...].astype(jnp.float32)
    mean = jnp.mean(values, axis=-1, keepdims=True)
    centred = values - mean
    var = jnp.mean(centred * centred, axis=-1, keepdims=True)
    gain = held_gain_ref[...].reshape(1, -1)
    out_ref[...] = (centred * lax.rsqrt(var + 1e-06) * gain).astype(jnp.bfloat16)
    spread(out_ref, slots_ref, sems)


def normalize(rows, norm_gain, slots):
    vmem, hbm = pl.BlockSpec(memory_space=pltpu.VMEM), pl.BlockSpec(memory_space=pltpu.HBM)
    rows = pltpu.with_memory_space_constraint(rows, pltpu.HBM)
    norm_gain = pltpu.with_memory_space_constraint(norm_gain, pltpu.HBM)
    return pl.pallas_call(
        normalize_kernel,
        out_shape=[
            jax.ShapeDtypeStruct(rows.shape, jnp.bfloat16),
            pltpu.HBM((slots,) + rows.shape, jnp.bfloat16),
        ],
        in_specs=[hbm, hbm],
        out_specs=[vmem, hbm],
        scratch_shapes=[
            pltpu.VMEM(rows.shape, rows.dtype),
            pltpu.VMEM(norm_gain.shape, norm_gain.dtype),
            pltpu.SemaphoreType.DMA((2,)),
            pltpu.SemaphoreType.DMA((slots,)),
        ],
        compiler_params=pltpu.CompilerParams(vmem_limit_bytes=16 << 20),
        cost_estimate=pl.CostEstimate(
            flops=8 * rows.size, bytes_accessed=2 * slots * rows.size, transcendentals=0
        ),
    )(rows, norm_gain)


def copies_of(rows, slots):
    return pl.pallas_call(
        spread,
        out_shape=pltpu.HBM((slots,) + rows.shape, rows.dtype),
        in_specs=[pl.BlockSpec(memory_space=pltpu.VMEM)],
        out_specs=pl.BlockSpec(memory_space=pltpu.HBM),
        scratch_shapes=[pltpu.SemaphoreType.DMA((slots,))],
        compiler_params=pltpu.CompilerParams(vmem_limit_bytes=16 << 20),
        cost_estimate=pl.CostEstimate(flops=0, bytes_accessed=2 * slots * rows.size, transcendentals=0),
    )(rows)


def gather_tokens(slots):
    rows = lax.all_to_all(slots, "head", split_axis=0, concat_axis=0, tiled=True)
    return rows.reshape(-1, slots.shape[-1])


def rms_rows(part, gain):
    square = jnp.mean(part * part, axis=0, keepdims=True) + 1e-06
    return part * lax.rsqrt(square) * gain


def project_kernel(rows_ref, weight_ref, gain_ref, query_ref, pair_ref):
    head_dim = gain_ref.shape[0]
    flat = lax.dot_general(
        weight_ref[...], rows_ref[...], (((1,), (1,)), ((), ())), preferred_element_type=jnp.float32
    )
    flat = flat.astype(jnp.bfloat16).astype(jnp.float32)
    query_ref[...] = rms_rows(flat[:head_dim], gain_ref[:, 0:1]).astype(jnp.bfloat16)
    keys = rms_rows(flat[head_dim : 2 * head_dim], gain_ref[:, 1:2])
    pair = jnp.concatenate([keys, flat[2 * head_dim :]], axis=0)
    pair_ref[...] = pair.astype(jnp.bfloat16)


def project(rows, weight, gain):
    tokens, width = rows.shape
    head_dim = gain.shape[0]
    return pl.pallas_call(
        project_kernel,
        out_shape=[
            jax.ShapeDtypeStruct((head_dim, tokens), jnp.bfloat16),
            jax.ShapeDtypeStruct((2 * head_dim, tokens), jnp.bfloat16),
        ],
        compiler_params=pltpu.CompilerParams(vmem_limit_bytes=16 << 20),
        cost_estimate=pl.CostEstimate(
            flops=2 * tokens * width * weight.shape[0], bytes_accessed=2 * tokens * width, transcendentals=0
        ),
    )(rows, weight, gain)


def project_far_kernel(
    place_ref, rows_ref, weight_ref, mine_ref, other_ref, mine_half_ref, other_half_ref, out_ref
):
    wide = out_ref.shape[1]
    column, part = mine_ref.shape[0], mine_half_ref.shape[0]
    start = weight_ref.shape[0] - wide
    even = start // 16 * 16
    stacked = jnp.concatenate(
        [
            mine_ref[column - wide :],
            other_ref[column - wide :],
            mine_half_ref[...],
            other_half_ref[...],
            weight_ref[even:],
        ],
        axis=0,
    )
    flat = lax.dot_general(
        stacked, rows_ref[...], (((1,), (1,)), ((), ())), preferred_element_type=jnp.float32
    )
    mine, other = flat[:wide], flat[wide : 2 * wide]
    first, second = flat[2 * wide : 2 * wide + part], flat[2 * wide + part : 2 * wide + 2 * part]
    own = flat[2 * wide + 2 * part + start - even :]
    low = jnp.where(place_ref[4] == 0, first, second)
    high = jnp.where(place_ref[4] == 0, second, first)
    far = jnp.concatenate([low[column - wide :], high], axis=0)
    for n, rows in enumerate((own, mine, other, far)):
        out_ref[place_ref[n]] = rows.astype(jnp.bfloat16)


PAD = 8


def project_far(place, rows, weight, column, head_dim):
    side = len(groups(0))
    smem, vmem = pl.BlockSpec(memory_space=pltpu.SMEM), pl.BlockSpec(memory_space=pltpu.VMEM)
    return pl.pallas_call(
        project_far_kernel,
        out_shape=jax.ShapeDtypeStruct((side, 2 * head_dim, rows.shape[0]), jnp.bfloat16),
        in_specs=[smem] + [vmem] * (2 + len(column)),
        out_specs=vmem,
        compiler_params=pltpu.CompilerParams(vmem_limit_bytes=16 << 20),
        cost_estimate=pl.CostEstimate(
            flops=2 * side * rows.size * weight.shape[0], bytes_accessed=4 * rows.size, transcendentals=0
        ),
    )(place, rows, weight, *column)


def settle_kernel(parts_ref, gain_ref, pair_ref):
    head_dim = gain_ref.shape[0]
    blocks, _, tokens = parts_ref.shape
    for n in range(blocks):
        flat = parts_ref[n].astype(jnp.float32)
        keys = rms_rows(flat[:head_dim], gain_ref[:, 1:2])
        pair = jnp.concatenate([keys, flat[head_dim:]], axis=0)
        pair_ref[:, pl.ds(n * tokens, tokens)] = pair.astype(jnp.bfloat16)


def settle(parts, gain):
    blocks, wide, tokens = parts.shape
    return pl.pallas_call(
        settle_kernel,
        out_shape=jax.ShapeDtypeStruct((wide, blocks * tokens), jnp.bfloat16),
        compiler_params=pltpu.CompilerParams(vmem_limit_bytes=16 << 20),
        cost_estimate=pl.CostEstimate(
            flops=8 * parts.size, bytes_accessed=4 * parts.size, transcendentals=0
        ),
    )(parts, gain)


def spread_pair(pair_ref, keys_ref, values_ref):
    head_dim = keys_ref.shape[1]
    pair = pair_ref[...].astype(jnp.float32)
    ones = jnp.ones((values_ref.shape[0] - head_dim, pair.shape[1]), jnp.float32)
    keys_ref[...] = pair[:head_dim].T.astype(jnp.bfloat16)
    values_ref[...] = jnp.concatenate([pair[head_dim:], ones], axis=0).astype(jnp.bfloat16)


def scores_of(keys, query):
    factor = math.log2(math.e) * float(query.shape[0]) ** (-0.5)
    return jnp.dot(keys, query, preferred_element_type=jnp.float32) * factor


def weighted(scores, shift, values):
    weights = jnp.exp2(scores - shift).astype(jnp.bfloat16)
    return jnp.dot(values, weights, preferred_element_type=jnp.float32)


def cross_update(on, scores, values, best):
    most = jnp.maximum(best, jnp.max(scores, axis=0, keepdims=True))
    newbest = jnp.where(on, most, best)
    shift = jnp.where(on, newbest, BLANK)
    return newbest, jnp.exp2(best - newbest), weighted(scores, shift, values)


def finish(acc, head_dim):
    return acc[:head_dim] / jnp.maximum(acc[head_dim : head_dim + 1], 1.0)


def near_kernel(
    tile, active_ref, query_ref, own_ref, far_ref, own_out_ref, state_ref, best_ref, keys_ref, values_ref
):
    head_dim, tokens = query_ref.shape
    for n, ref in enumerate((own_ref, far_ref)):
        spread_pair(ref, keys_ref.at[n], values_ref.at[n])
    for at in range(tokens // tile):
        columns = pl.ds(at * tile, tile)
        query = query_ref[:, columns]
        scores = scores_of(keys_ref[0], query)
        acc = weighted(scores, jnp.max(scores, axis=0, keepdims=True), values_ref[0])
        own_out_ref[:, columns] = finish(acc, head_dim)
        start = jnp.full((1, tile), -BLANK, jnp.float32)
        scores = scores_of(keys_ref[1], query)
        best, _, acc = cross_update(active_ref[0] > 0, scores, values_ref[1], start)
        state_ref[:, columns] = acc
        best_ref[:, columns] = best


def middle_kernel(
    tile, which, active_ref, query_ref, state_ref, best_ref, far_ref, state_out_ref, best_out_ref,
    keys_ref, values_ref,
):
    tokens = query_ref.shape[1]
    spread_pair(far_ref, keys_ref, values_ref)
    for at in range(tokens // tile):
        columns = pl.ds(at * tile, tile)
        scores = scores_of(keys_ref[...], query_ref[:, columns])
        on = active_ref[which] > 0
        best, factor, term = cross_update(on, scores, values_ref[...], best_ref[:, columns])
        state_out_ref[:, columns] = state_ref[:, columns] * factor + term
        best_out_ref[:, columns] = best


def last_kernel(
    tile, which, active_ref, query_ref, own_in_ref, state_ref, best_ref, far_ref, out_ref,
    keys_ref, values_ref,
):
    head_dim, tokens = query_ref.shape
    block = out_ref.shape[-1]
    spread_pair(far_ref, keys_ref, values_ref)
    for at in range(tokens // tile):
        columns = pl.ds(at * tile, tile)
        scores = scores_of(keys_ref[...], query_ref[:, columns])
        on = active_ref[which] > 0
        _, factor, term = cross_update(on, scores, values_ref[...], best_ref[:, columns])
        cross = finish(state_ref[:, columns] * factor + term, head_dim)
        blank = jnp.zeros((out_ref.shape[1] - head_dim, tile), jnp.float32)
        result = jnp.concatenate([own_in_ref[:, columns] + cross, blank], axis=0).astype(jnp.bfloat16)
        for n in range(tile // block):
            out_ref[at * (tile // block) + n] = result[:, n * block : (n + 1) * block]


ONES = 8


def call_attend(kernel, out_shape, blocks, arrays):
    head_dim, tokens = arrays[1].shape
    lead = () if blocks == 1 else (blocks,)
    smem, vmem = pl.BlockSpec(memory_space=pltpu.SMEM), pl.BlockSpec(memory_space=pltpu.VMEM)
    several = isinstance(out_shape, list)
    return pl.pallas_call(
        kernel,
        out_shape=out_shape,
        in_specs=[smem] + [vmem] * (len(arrays) - 1),
        out_specs=[vmem] * len(out_shape) if several else vmem,
        scratch_shapes=[
            pltpu.VMEM(lead + (tokens, head_dim), jnp.bfloat16),
            pltpu.VMEM(lead + (head_dim + ONES, tokens), jnp.bfloat16),
        ],
        compiler_params=pltpu.CompilerParams(vmem_limit_bytes=24 << 20),
        cost_estimate=pl.CostEstimate(
            flops=4 * blocks * tokens * tokens * 256,
            bytes_accessed=4 * blocks * tokens * head_dim,
            transcendentals=blocks * tokens * tokens,
        ),
    )(*arrays)


def attend_near(active, query, own, far):
    head_dim, tokens = query.shape
    out_shape = [
        jax.ShapeDtypeStruct((rows, tokens), jnp.float32) for rows in (head_dim, head_dim + ONES, 1)
    ]
    kernel = functools.partial(near_kernel, tokens // 2)
    return call_attend(kernel, out_shape, 2, (active, query, own, far))


def attend_middle(active, which, query, state, best, far):
    out_shape = [jax.ShapeDtypeStruct(array.shape, jnp.float32) for array in (state, best)]
    kernel = functools.partial(middle_kernel, query.shape[1] // 2, which)
    return call_attend(kernel, out_shape, 1, (active, query, state, best, far))


def attend_last(active, which, query, own_result, state, best, far):
    head_dim, tokens = query.shape
    side = len(groups(0))
    out_shape = jax.ShapeDtypeStruct((side, head_dim + PAD, tokens // side), jnp.bfloat16)
    kernel = functools.partial(last_kernel, tokens // 2, which)
    return call_attend(kernel, out_shape, 1, (active, query, own_result, state, best, far))


def groups(which):
    heads = lax.axis_size("head")
    side = math.isqrt(heads)
    table = [[side * i + j for j in range(side)] for i in range(side)]
    return table if which == 0 else [list(column) for column in zip(*table)]


def exchange(slots, which):
    return lax.all_to_all(
        slots, "head", split_axis=0, concat_axis=0, tiled=True, axis_index_groups=groups(which)
    )


def column_weights(weight, out_weight):
    views, heads = lax.axis_size("view"), lax.axis_size("head")
    side = len(groups(0))
    core = lax.axis_index("view") % 2
    blank = jnp.zeros((PAD, weight.shape[1]), weight.dtype)
    packed = jnp.concatenate([out_weight, blank, weight[out_weight.shape[0] :]], axis=0)
    part = packed.shape[0] // 2
    pairs = []
    for view in range(views):
        step = side if view % 2 == 0 else -side
        for head in range(heads):
            pairs.append((view * heads + (head + step) % heads, view * heads + head))
    beside = lax.ppermute(packed, ("view", "head"), pairs)
    sent = jnp.where(core == 0, packed[:part], packed[part:])
    across = [(head, (head + heads // 2) % heads) for head in range(heads)]
    return packed, beside, lax.ppermute(sent, "head", across)


def project_out_kernel(
    place_ref, parts_ref, weight_ref, mine_ref, other_ref, mine_half_ref, other_half_ref, out_ref
):
    wide = parts_ref.shape[1]
    far = parts_ref[place_ref[3]].astype(jnp.float32)
    blank = jnp.zeros_like(far)
    first = jnp.where(place_ref[4] == 0, far, blank).astype(jnp.bfloat16)
    second = jnp.where(place_ref[4] == 0, blank, far).astype(jnp.bfloat16)
    total = None
    for part, rows_ref in (
        (parts_ref[place_ref[0]], weight_ref),
        (parts_ref[place_ref[1]], mine_ref),
        (parts_ref[place_ref[2]], other_ref),
        (first, mine_half_ref),
        (second, other_half_ref),
    ):
        term = lax.dot_general(
            part, rows_ref[:wide], (((0,), (0,)), ((), ())), preferred_element_type=jnp.float32
        )
        total = term if total is None else total + term
    out_ref[...] = total.reshape(out_ref.shape).astype(jnp.bfloat16)


def project_out(place, parts, column):
    side, wide, tokens = parts.shape
    width = column[0].shape[1]
    smem, vmem = pl.BlockSpec(memory_space=pltpu.SMEM), pl.BlockSpec(memory_space=pltpu.VMEM)
    partial = pl.pallas_call(
        project_out_kernel,
        out_shape=jax.ShapeDtypeStruct((side, tokens // side, width), jnp.bfloat16),
        in_specs=[smem] + [vmem] * (1 + len(column)),
        out_specs=vmem,
        compiler_params=pltpu.CompilerParams(vmem_limit_bytes=16 << 20),
        cost_estimate=pl.CostEstimate(
            flops=2 * parts.size * width, bytes_accessed=2 * (side * wide + tokens) * width, transcendentals=0
        ),
    )(place, parts, *column)
    partial = exchange(partial, 0)
    return jnp.sum(partial.astype(jnp.float32), axis=0).astype(jnp.bfloat16)


def on_device(latents, norm_gain, qkv_weight, qk_gain, out_weight, intersection):
    loc_len, view_dev, width = latents.shape
    rows = latents.reshape(loc_len, width)
    levels = lax.axis_size("view").bit_length() - 1
    rounds = intersection.shape[0]
    bits = [step * (levels - 1) // (rounds - 1) for step in range(rounds)]
    gain = qk_gain[0].T
    head_dim = gain.shape[0]
    weight = qkv_weight[0]
    active = intersection[:, 0]
    heads = lax.axis_size("head")
    normed, slots = normalize(rows, norm_gain, heads)
    core, side = lax.axis_index("view") % 2, len(groups(0))
    line = lax.axis_index("head") // side
    turn = jnp.where(core == 0, 1, side - 1)
    place = jnp.stack([line, line + turn, line + side - turn, line + side // 2]) % side
    place = jnp.concatenate([place, core[None]]).astype(jnp.int32)
    far_normed, gain, active = lax.optimization_barrier((partner(normed, bits[-1]), gain, active))
    far_slots = copies_of(far_normed, side)
    packed, whole, half = column_weights(weight, out_weight[0])
    every, far_slots, whole = lax.optimization_barrier((gather_tokens(slots), far_slots, whole))
    far_tokens = exchange(far_slots, 0).reshape(-1, width)
    query, own = project(every, weight, gain)
    near = [partner(own, bit) for bit in bits[:-1]]
    column = [whole, partner(whole, 0), half, partner(half, 0)]
    far_parts = project_far(place, far_tokens, weight, column, head_dim)
    far_parts = exchange(far_parts, 1)
    own_result, state, best = attend_near(active, query, own, near[0])
    far_parts, own_result, state, best, near[1] = lax.optimization_barrier(
        (far_parts, own_result, state, best, near[1])
    )
    state, best = attend_middle(active, rounds - 1, query, state, best, settle(far_parts, gain))
    attended = attend_last(active, 1, query, own_result, state, best, near[1])
    mixed = project_out(place, exchange(attended, 1), [packed] + column)
    return mixed.reshape(loc_len, view_dev, width)


def solution(mesh):
    placed = (
        P("head", "view", None),
        P(),
        P("head", None, None),
        P("head", None, None),
        P("head", None, None),
        P(None, "view"),
    )
    return jax.shard_map(
        on_device, mesh=mesh, in_specs=placed, out_specs=P("head", "view", None), check_vma=False
    )
```

```python
import functools
import math
import jax
import jax.numpy as jnp
from jax import lax
from jax.experimental import pallas as pl
from jax.experimental.pallas import tpu as pltpu
from jax.sharding import PartitionSpec as P

BLANK = 1e30


def partner(array, bit):
    return lax.ppermute(array, "view", [(i, i ^ 1 << bit) for i in range(lax.axis_size("view"))])


def spread(source_ref, slots_ref, sems):
    copies = [
        pltpu.make_async_copy(source_ref, slots_ref.at[n], sems.at[n]) for n in range(slots_ref.shape[0])
    ]
    for copy in copies:
        copy.start()
    for copy in copies:
        copy.wait()


def normalize_kernel(rows_ref, gain_ref, out_ref, slots_ref, held_ref, held_gain_ref, read_sems, sems):
    reads = [
        pltpu.make_async_copy(rows_ref, held_ref, read_sems.at[0]),
        pltpu.make_async_copy(gain_ref, held_gain_ref, read_sems.at[1]),
    ]
    for read in reads:
        read.start()
    for read in reads:
        read.wait()
    values = held_ref[...].astype(jnp.float32)
    mean = jnp.mean(values, axis=-1, keepdims=True)
    centred = values - mean
    var = jnp.mean(centred * centred, axis=-1, keepdims=True)
    gain = held_gain_ref[...].reshape(1, -1)
    out_ref[...] = (centred * lax.rsqrt(var + 1e-06) * gain).astype(jnp.bfloat16)
    spread(out_ref, slots_ref, sems)


def normalize(rows, norm_gain, slots):
    vmem, hbm = pl.BlockSpec(memory_space=pltpu.VMEM), pl.BlockSpec(memory_space=pltpu.HBM)
    rows = pltpu.with_memory_space_constraint(rows, pltpu.HBM)
    norm_gain = pltpu.with_memory_space_constraint(norm_gain, pltpu.HBM)
    return pl.pallas_call(
        normalize_kernel,
        out_shape=[
            jax.ShapeDtypeStruct(rows.shape, jnp.bfloat16),
            pltpu.HBM((slots,) + rows.shape, jnp.bfloat16),
        ],
        in_specs=[hbm, hbm],
        out_specs=[vmem, hbm],
        scratch_shapes=[
            pltpu.VMEM(rows.shape, rows.dtype),
            pltpu.VMEM(norm_gain.shape, norm_gain.dtype),
            pltpu.SemaphoreType.DMA((2,)),
            pltpu.SemaphoreType.DMA((slots,)),
        ],
        compiler_params=pltpu.CompilerParams(vmem_limit_bytes=16 << 20),
        cost_estimate=pl.CostEstimate(
            flops=8 * rows.size, bytes_accessed=2 * slots * rows.size, transcendentals=0
        ),
    )(rows, norm_gain)


def copies_of(rows, slots):
    return pl.pallas_call(
        spread,
        out_shape=pltpu.HBM((slots,) + rows.shape, rows.dtype),
        in_specs=[pl.BlockSpec(memory_space=pltpu.VMEM)],
        out_specs=pl.BlockSpec(memory_space=pltpu.HBM),
        scratch_shapes=[pltpu.SemaphoreType.DMA((slots,))],
        compiler_params=pltpu.CompilerParams(vmem_limit_bytes=16 << 20),
        cost_estimate=pl.CostEstimate(flops=0, bytes_accessed=2 * slots * rows.size, transcendentals=0),
    )(rows)


def gather_tokens(slots):
    rows = lax.all_to_all(slots, "head", split_axis=0, concat_axis=0, tiled=True)
    return rows.reshape(-1, slots.shape[-1])


def rms_rows(part, gain):
    square = jnp.mean(part * part, axis=0, keepdims=True) + 1e-06
    return part * lax.rsqrt(square) * gain


def project_kernel(rows_ref, weight_ref, gain_ref, query_ref, pair_ref):
    head_dim = gain_ref.shape[0]
    flat = lax.dot_general(
        weight_ref[...], rows_ref[...], (((1,), (1,)), ((), ())), preferred_element_type=jnp.float32
    )
    flat = flat.astype(jnp.bfloat16).astype(jnp.float32)
    query_ref[...] = rms_rows(flat[:head_dim], gain_ref[:, 0:1]).astype(jnp.bfloat16)
    keys = rms_rows(flat[head_dim : 2 * head_dim], gain_ref[:, 1:2])
    pair = jnp.concatenate([keys, flat[2 * head_dim :]], axis=0)
    pair_ref[...] = pair.astype(jnp.bfloat16)


def project(rows, weight, gain):
    tokens, width = rows.shape
    head_dim = gain.shape[0]
    return pl.pallas_call(
        project_kernel,
        out_shape=[
            jax.ShapeDtypeStruct((head_dim, tokens), jnp.bfloat16),
            jax.ShapeDtypeStruct((2 * head_dim, tokens), jnp.bfloat16),
        ],
        compiler_params=pltpu.CompilerParams(vmem_limit_bytes=16 << 20),
        cost_estimate=pl.CostEstimate(
            flops=2 * tokens * width * weight.shape[0], bytes_accessed=2 * tokens * width, transcendentals=0
        ),
    )(rows, weight, gain)


def project_far_kernel(
    place_ref, rows_ref, weight_ref, mine_ref, other_ref, mine_half_ref, other_half_ref, out_ref
):
    wide = out_ref.shape[1]
    column, part = mine_ref.shape[0], mine_half_ref.shape[0]
    start = weight_ref.shape[0] - wide
    even = start // 16 * 16
    stacked = jnp.concatenate(
        [
            mine_ref[column - wide :],
            other_ref[column - wide :],
            mine_half_ref[...],
            other_half_ref[...],
            weight_ref[even:],
        ],
        axis=0,
    )
    flat = lax.dot_general(
        stacked, rows_ref[...], (((1,), (1,)), ((), ())), preferred_element_type=jnp.float32
    )
    mine, other = flat[:wide], flat[wide : 2 * wide]
    first, second = flat[2 * wide : 2 * wide + part], flat[2 * wide + part : 2 * wide + 2 * part]
    own = flat[2 * wide + 2 * part + start - even :]
    low = jnp.where(place_ref[4] == 0, first, second)
    high = jnp.where(place_ref[4] == 0, second, first)
    far = jnp.concatenate([low[column - wide :], high], axis=0)
    for n, rows in enumerate((own, mine, other, far)):
        out_ref[place_ref[n]] = rows.astype(jnp.bfloat16)


PAD = 8


def project_far(place, rows, weight, column, head_dim):
    side = len(groups(0))
    smem, vmem = pl.BlockSpec(memory_space=pltpu.SMEM), pl.BlockSpec(memory_space=pltpu.VMEM)
    return pl.pallas_call(
        project_far_kernel,
        out_shape=jax.ShapeDtypeStruct((side, 2 * head_dim, rows.shape[0]), jnp.bfloat16),
        in_specs=[smem] + [vmem] * (2 + len(column)),
        out_specs=vmem,
        compiler_params=pltpu.CompilerParams(vmem_limit_bytes=16 << 20),
        cost_estimate=pl.CostEstimate(
            flops=2 * side * rows.size * weight.shape[0], bytes_accessed=4 * rows.size, transcendentals=0
        ),
    )(place, rows, weight, *column)


def settle_kernel(parts_ref, gain_ref, pair_ref):
    head_dim = gain_ref.shape[0]
    blocks, _, tokens = parts_ref.shape
    for n in range(blocks):
        flat = parts_ref[n].astype(jnp.float32)
        keys = rms_rows(flat[:head_dim], gain_ref[:, 1:2])
        pair = jnp.concatenate([keys, flat[head_dim:]], axis=0)
        pair_ref[:, pl.ds(n * tokens, tokens)] = pair.astype(jnp.bfloat16)


def settle(parts, gain):
    blocks, wide, tokens = parts.shape
    return pl.pallas_call(
        settle_kernel,
        out_shape=jax.ShapeDtypeStruct((wide, blocks * tokens), jnp.bfloat16),
        compiler_params=pltpu.CompilerParams(vmem_limit_bytes=16 << 20),
        cost_estimate=pl.CostEstimate(
            flops=8 * parts.size, bytes_accessed=4 * parts.size, transcendentals=0
        ),
    )(parts, gain)


def spread_pair(pair_ref, keys_ref, values_ref):
    head_dim = keys_ref.shape[1]
    pair = pair_ref[...].astype(jnp.float32)
    ones = jnp.ones((values_ref.shape[0] - head_dim, pair.shape[1]), jnp.float32)
    keys_ref[...] = pair[:head_dim].T.astype(jnp.bfloat16)
    values_ref[...] = jnp.concatenate([pair[head_dim:], ones], axis=0).astype(jnp.bfloat16)


def scores_of(keys, query):
    factor = math.log2(math.e) * float(query.shape[0]) ** (-0.5)
    return jnp.dot(keys, query, preferred_element_type=jnp.float32) * factor


def weighted(scores, shift, values):
    weights = jnp.exp2(scores - shift).astype(jnp.bfloat16)
    return jnp.dot(values, weights, preferred_element_type=jnp.float32)


def cross_update(on, scores, values, best):
    most = jnp.maximum(best, jnp.max(scores, axis=0, keepdims=True))
    newbest = jnp.where(on, most, best)
    shift = jnp.where(on, newbest, BLANK)
    return newbest, jnp.exp2(best - newbest), weighted(scores, shift, values)


def finish(acc, head_dim):
    return acc[:head_dim] / jnp.maximum(acc[head_dim : head_dim + 1], 1.0)


def near_kernel(
    tile, active_ref, query_ref, own_ref, far_ref, own_out_ref, state_ref, best_ref, keys_ref, values_ref
):
    head_dim, tokens = query_ref.shape
    for n, ref in enumerate((own_ref, far_ref)):
        spread_pair(ref, keys_ref.at[n], values_ref.at[n])
    for at in range(tokens // tile):
        columns = pl.ds(at * tile, tile)
        query = query_ref[:, columns]
        scores = scores_of(keys_ref[0], query)
        acc = weighted(scores, jnp.max(scores, axis=0, keepdims=True), values_ref[0])
        own_out_ref[:, columns] = finish(acc, head_dim)
        start = jnp.full((1, tile), -BLANK, jnp.float32)
        scores = scores_of(keys_ref[1], query)
        best, _, acc = cross_update(active_ref[0] > 0, scores, values_ref[1], start)
        state_ref[:, columns] = acc
        best_ref[:, columns] = best


def middle_kernel(
    tile, which, active_ref, query_ref, state_ref, best_ref, far_ref, state_out_ref, best_out_ref,
    keys_ref, values_ref,
):
    tokens = query_ref.shape[1]
    spread_pair(far_ref, keys_ref, values_ref)
    for at in range(tokens // tile):
        columns = pl.ds(at * tile, tile)
        scores = scores_of(keys_ref[...], query_ref[:, columns])
        on = active_ref[which] > 0
        best, factor, term = cross_update(on, scores, values_ref[...], best_ref[:, columns])
        state_out_ref[:, columns] = state_ref[:, columns] * factor + term
        best_out_ref[:, columns] = best


def last_kernel(
    tile, which, active_ref, query_ref, own_in_ref, state_ref, best_ref, far_ref, out_ref,
    keys_ref, values_ref,
):
    head_dim, tokens = query_ref.shape
    block = out_ref.shape[-1]
    spread_pair(far_ref, keys_ref, values_ref)
    for at in range(tokens // tile):
        columns = pl.ds(at * tile, tile)
        scores = scores_of(keys_ref[...], query_ref[:, columns])
        on = active_ref[which] > 0
        _, factor, term = cross_update(on, scores, values_ref[...], best_ref[:, columns])
        cross = finish(state_ref[:, columns] * factor + term, head_dim)
        blank = jnp.zeros((out_ref.shape[1] - head_dim, tile), jnp.float32)
        result = jnp.concatenate([own_in_ref[:, columns] + cross, blank], axis=0).astype(jnp.bfloat16)
        for n in range(tile // block):
            out_ref[at * (tile // block) + n] = result[:, n * block : (n + 1) * block]


ONES = 8


def call_attend(kernel, out_shape, blocks, arrays):
    head_dim, tokens = arrays[1].shape
    lead = () if blocks == 1 else (blocks,)
    smem, vmem = pl.BlockSpec(memory_space=pltpu.SMEM), pl.BlockSpec(memory_space=pltpu.VMEM)
    several = isinstance(out_shape, list)
    return pl.pallas_call(
        kernel,
        out_shape=out_shape,
        in_specs=[smem] + [vmem] * (len(arrays) - 1),
        out_specs=[vmem] * len(out_shape) if several else vmem,
        scratch_shapes=[
            pltpu.VMEM(lead + (tokens, head_dim), jnp.bfloat16),
            pltpu.VMEM(lead + (head_dim + ONES, tokens), jnp.bfloat16),
        ],
        compiler_params=pltpu.CompilerParams(vmem_limit_bytes=24 << 20),
        cost_estimate=pl.CostEstimate(
            flops=4 * blocks * tokens * tokens * 256,
            bytes_accessed=4 * blocks * tokens * head_dim,
            transcendentals=blocks * tokens * tokens,
        ),
    )(*arrays)


def attend_near(active, query, own, far):
    head_dim, tokens = query.shape
    out_shape = [
        jax.ShapeDtypeStruct((rows, tokens), jnp.float32) for rows in (head_dim, head_dim + ONES, 1)
    ]
    kernel = functools.partial(near_kernel, tokens // 2)
    return call_attend(kernel, out_shape, 2, (active, query, own, far))


def attend_middle(active, which, query, state, best, far):
    out_shape = [jax.ShapeDtypeStruct(array.shape, jnp.float32) for array in (state, best)]
    kernel = functools.partial(middle_kernel, query.shape[1] // 2, which)
    return call_attend(kernel, out_shape, 1, (active, query, state, best, far))


def attend_last(active, which, query, own_result, state, best, far):
    head_dim, tokens = query.shape
    side = len(groups(0))
    out_shape = jax.ShapeDtypeStruct((side, head_dim + PAD, tokens // side), jnp.bfloat16)
    kernel = functools.partial(last_kernel, tokens // 2, which)
    return call_attend(kernel, out_shape, 1, (active, query, own_result, state, best, far))


def groups(which):
    heads = lax.axis_size("head")
    side = math.isqrt(heads)
    table = [[side * i + j for j in range(side)] for i in range(side)]
    return table if which == 0 else [list(column) for column in zip(*table)]


def exchange(slots, which):
    return lax.all_to_all(
        slots, "head", split_axis=0, concat_axis=0, tiled=True, axis_index_groups=groups(which)
    )


def column_weights(weight, out_weight):
    views, heads = lax.axis_size("view"), lax.axis_size("head")
    side = len(groups(0))
    core = lax.axis_index("view") % 2
    blank = jnp.zeros((PAD, weight.shape[1]), weight.dtype)
    packed = jnp.concatenate([out_weight, blank, weight[out_weight.shape[0] :]], axis=0)
    part = packed.shape[0] // 2
    pairs = []
    for view in range(views):
        step = side if view % 2 == 0 else -side
        for head in range(heads):
            pairs.append((view * heads + (head + step) % heads, view * heads + head))
    beside = lax.ppermute(packed, ("view", "head"), pairs)
    sent = jnp.where(core == 0, packed[:part], packed[part:])
    across = [(head, (head + heads // 2) % heads) for head in range(heads)]
    return packed, beside, lax.ppermute(sent, "head", across)


def project_out_kernel(
    place_ref, parts_ref, weight_ref, mine_ref, other_ref, mine_half_ref, other_half_ref, out_ref
):
    wide = parts_ref.shape[1]
    far = parts_ref[place_ref[3]].astype(jnp.float32)
    blank = jnp.zeros_like(far)
    first = jnp.where(place_ref[4] == 0, far, blank).astype(jnp.bfloat16)
    second = jnp.where(place_ref[4] == 0, blank, far).astype(jnp.bfloat16)
    total = None
    for part, rows_ref in (
        (parts_ref[place_ref[0]], weight_ref),
        (parts_ref[place_ref[1]], mine_ref),
        (parts_ref[place_ref[2]], other_ref),
        (first, mine_half_ref),
        (second, other_half_ref),
    ):
        term = lax.dot_general(
            part, rows_ref[:wide], (((0,), (0,)), ((), ())), preferred_element_type=jnp.float32
        )
        total = term if total is None else total + term
    out_ref[...] = total.reshape(out_ref.shape).astype(jnp.bfloat16)


def project_out(place, parts, column):
    side, wide, tokens = parts.shape
    width = column[0].shape[1]
    smem, vmem = pl.BlockSpec(memory_space=pltpu.SMEM), pl.BlockSpec(memory_space=pltpu.VMEM)
    partial = pl.pallas_call(
        project_out_kernel,
        out_shape=jax.ShapeDtypeStruct((side, tokens // side, width), jnp.bfloat16),
        grid=(1,),
        in_specs=[smem, vmem] + [pl.BlockSpec((wide, width), lambda n: (0, 0))] * len(column),
        out_specs=vmem,
        compiler_params=pltpu.CompilerParams(vmem_limit_bytes=16 << 20),
        cost_estimate=pl.CostEstimate(
            flops=2 * parts.size * width, bytes_accessed=2 * (side * wide + tokens) * width, transcendentals=0
        ),
    )(place, parts, *column)
    partial = exchange(partial, 0)
    return jnp.sum(partial.astype(jnp.float32), axis=0).astype(jnp.bfloat16)


def on_device(latents, norm_gain, qkv_weight, qk_gain, out_weight, intersection):
    loc_len, view_dev, width = latents.shape
    rows = latents.reshape(loc_len, width)
    levels = lax.axis_size("view").bit_length() - 1
    rounds = intersection.shape[0]
    bits = [step * (levels - 1) // (rounds - 1) for step in range(rounds)]
    gain = qk_gain[0].T
    head_dim = gain.shape[0]
    weight = qkv_weight[0]
    active = intersection[:, 0]
    heads = lax.axis_size("head")
    normed, slots = normalize(rows, norm_gain, heads)
    core, side = lax.axis_index("view") % 2, len(groups(0))
    line = lax.axis_index("head") // side
    turn = jnp.where(core == 0, 1, side - 1)
    place = jnp.stack([line, line + turn, line + side - turn, line + side // 2]) % side
    place = jnp.concatenate([place, core[None]]).astype(jnp.int32)
    far_normed, gain, active = lax.optimization_barrier((partner(normed, bits[-1]), gain, active))
    far_slots = copies_of(far_normed, side)
    packed, whole, half = column_weights(weight, out_weight[0])
    every, far_slots, whole = lax.optimization_barrier((gather_tokens(slots), far_slots, whole))
    far_tokens = exchange(far_slots, 0).reshape(-1, width)
    query, own = project(every, weight, gain)
    near = [partner(own, bit) for bit in bits[:-1]]
    column = [whole, partner(whole, 0), half, partner(half, 0)]
    far_parts = project_far(place, far_tokens, weight, column, head_dim)
    far_parts = exchange(far_parts, 1)
    own_result, state, best = attend_near(active, query, own, near[0])
    far_parts, own_result, state, best, near[1] = lax.optimization_barrier(
        (far_parts, own_result, state, best, near[1])
    )
    state, best = attend_middle(active, rounds - 1, query, state, best, settle(far_parts, gain))
    attended = attend_last(active, 1, query, own_result, state, best, near[1])
    mixed = project_out(place, exchange(attended, 1), [packed] + column)
    return mixed.reshape(loc_len, view_dev, width)


def solution(mesh):
    placed = (
        P("head", "view", None),
        P(),
        P("head", None, None),
        P("head", None, None),
        P("head", None, None),
        P(None, "view"),
    )
    return jax.shard_map(
        on_device, mesh=mesh, in_specs=placed, out_specs=P("head", "view", None), check_vma=False
    )
```

```python
import functools
import math
import jax
import jax.numpy as jnp
from jax import lax
from jax.experimental import pallas as pl
from jax.experimental.pallas import tpu as pltpu
from jax.sharding import PartitionSpec as P

BLANK = 1e30


def partner(array, bit):
    return lax.ppermute(array, "view", [(i, i ^ 1 << bit) for i in range(lax.axis_size("view"))])


def spread(source_ref, slots_ref, sems):
    copies = [
        pltpu.make_async_copy(source_ref, slots_ref.at[n], sems.at[n]) for n in range(slots_ref.shape[0])
    ]
    for copy in copies:
        copy.start()
    for copy in copies:
        copy.wait()


def normalize_kernel(rows_ref, gain_ref, out_ref, slots_ref, held_ref, held_gain_ref, read_sems, sems):
    reads = [
        pltpu.make_async_copy(rows_ref, held_ref, read_sems.at[0]),
        pltpu.make_async_copy(gain_ref, held_gain_ref, read_sems.at[1]),
    ]
    for read in reads:
        read.start()
    for read in reads:
        read.wait()
    values = held_ref[...].astype(jnp.float32)
    mean = jnp.mean(values, axis=-1, keepdims=True)
    centred = values - mean
    var = jnp.mean(centred * centred, axis=-1, keepdims=True)
    gain = held_gain_ref[...].reshape(1, -1)
    out_ref[...] = (centred * lax.rsqrt(var + 1e-06) * gain).astype(jnp.bfloat16)
    spread(out_ref, slots_ref, sems)


def normalize(rows, norm_gain, slots):
    vmem, hbm = pl.BlockSpec(memory_space=pltpu.VMEM), pl.BlockSpec(memory_space=pltpu.HBM)
    rows = pltpu.with_memory_space_constraint(rows, pltpu.HBM)
    norm_gain = pltpu.with_memory_space_constraint(norm_gain, pltpu.HBM)
    return pl.pallas_call(
        normalize_kernel,
        out_shape=[
            jax.ShapeDtypeStruct(rows.shape, jnp.bfloat16),
            pltpu.HBM((slots,) + rows.shape, jnp.bfloat16),
        ],
        in_specs=[hbm, hbm],
        out_specs=[vmem, hbm],
        scratch_shapes=[
            pltpu.VMEM(rows.shape, rows.dtype),
            pltpu.VMEM(norm_gain.shape, norm_gain.dtype),
            pltpu.SemaphoreType.DMA((2,)),
            pltpu.SemaphoreType.DMA((slots,)),
        ],
        compiler_params=pltpu.CompilerParams(vmem_limit_bytes=16 << 20),
        cost_estimate=pl.CostEstimate(
            flops=8 * rows.size, bytes_accessed=2 * slots * rows.size, transcendentals=0
        ),
    )(rows, norm_gain)


def copies_of(rows, slots):
    return pl.pallas_call(
        spread,
        out_shape=pltpu.HBM((slots,) + rows.shape, rows.dtype),
        in_specs=[pl.BlockSpec(memory_space=pltpu.VMEM)],
        out_specs=pl.BlockSpec(memory_space=pltpu.HBM),
        scratch_shapes=[pltpu.SemaphoreType.DMA((slots,))],
        compiler_params=pltpu.CompilerParams(vmem_limit_bytes=16 << 20),
        cost_estimate=pl.CostEstimate(flops=0, bytes_accessed=2 * slots * rows.size, transcendentals=0),
    )(rows)


def gather_tokens(slots):
    rows = lax.all_to_all(slots, "head", split_axis=0, concat_axis=0, tiled=True)
    return rows.reshape(-1, slots.shape[-1])


def rms_rows(part, gain):
    square = jnp.mean(part * part, axis=0, keepdims=True) + 1e-06
    return part * lax.rsqrt(square) * gain


def project_kernel(rows_ref, weight_ref, gain_ref, query_ref, pair_ref):
    head_dim = gain_ref.shape[0]
    flat = lax.dot_general(
        weight_ref[...], rows_ref[...], (((1,), (1,)), ((), ())), preferred_element_type=jnp.float32
    )
    flat = flat.astype(jnp.bfloat16).astype(jnp.float32)
    query_ref[...] = rms_rows(flat[:head_dim], gain_ref[:, 0:1]).astype(jnp.bfloat16)
    keys = rms_rows(flat[head_dim : 2 * head_dim], gain_ref[:, 1:2])
    pair = jnp.concatenate([keys, flat[2 * head_dim :]], axis=0)
    pair_ref[...] = pair.astype(jnp.bfloat16)


def project(rows, weight, gain):
    tokens, width = rows.shape
    head_dim = gain.shape[0]
    return pl.pallas_call(
        project_kernel,
        out_shape=[
            jax.ShapeDtypeStruct((head_dim, tokens), jnp.bfloat16),
            jax.ShapeDtypeStruct((2 * head_dim, tokens), jnp.bfloat16),
        ],
        compiler_params=pltpu.CompilerParams(vmem_limit_bytes=16 << 20),
        cost_estimate=pl.CostEstimate(
            flops=2 * tokens * width * weight.shape[0], bytes_accessed=2 * tokens * width, transcendentals=0
        ),
    )(rows, weight, gain)


def project_far_kernel(
    place_ref, rows_ref, weight_ref, mine_ref, other_ref, mine_half_ref, other_half_ref, out_ref
):
    wide = out_ref.shape[1]
    column, part = mine_ref.shape[0], mine_half_ref.shape[0]
    start = weight_ref.shape[0] - wide
    even = start // 16 * 16
    stacked = jnp.concatenate(
        [
            mine_ref[column - wide :],
            other_ref[column - wide :],
            mine_half_ref[...],
            other_half_ref[...],
            weight_ref[even:],
        ],
        axis=0,
    )
    flat = lax.dot_general(
        stacked, rows_ref[...], (((1,), (1,)), ((), ())), preferred_element_type=jnp.float32
    )
    mine, other = flat[:wide], flat[wide : 2 * wide]
    first, second = flat[2 * wide : 2 * wide + part], flat[2 * wide + part : 2 * wide + 2 * part]
    own = flat[2 * wide + 2 * part + start - even :]
    low = jnp.where(place_ref[4] == 0, first, second)
    high = jnp.where(place_ref[4] == 0, second, first)
    far = jnp.concatenate([low[column - wide :], high], axis=0)
    for n, rows in enumerate((own, mine, other, far)):
        out_ref[place_ref[n]] = rows.astype(jnp.bfloat16)


PAD = 8


def project_far(place, rows, weight, column, head_dim):
    side = len(groups(0))
    smem, vmem = pl.BlockSpec(memory_space=pltpu.SMEM), pl.BlockSpec(memory_space=pltpu.VMEM)
    return pl.pallas_call(
        project_far_kernel,
        out_shape=jax.ShapeDtypeStruct((side, 2 * head_dim, rows.shape[0]), jnp.bfloat16),
        in_specs=[smem] + [vmem] * (2 + len(column)),
        out_specs=vmem,
        compiler_params=pltpu.CompilerParams(vmem_limit_bytes=16 << 20),
        cost_estimate=pl.CostEstimate(
            flops=2 * side * rows.size * weight.shape[0], bytes_accessed=4 * rows.size, transcendentals=0
        ),
    )(place, rows, weight, *column)


def settle_kernel(parts_ref, gain_ref, pair_ref):
    head_dim = gain_ref.shape[0]
    blocks, _, tokens = parts_ref.shape
    for n in range(blocks):
        flat = parts_ref[n].astype(jnp.float32)
        keys = rms_rows(flat[:head_dim], gain_ref[:, 1:2])
        pair = jnp.concatenate([keys, flat[head_dim:]], axis=0)
        pair_ref[:, pl.ds(n * tokens, tokens)] = pair.astype(jnp.bfloat16)


def settle(parts, gain):
    blocks, wide, tokens = parts.shape
    return pl.pallas_call(
        settle_kernel,
        out_shape=jax.ShapeDtypeStruct((wide, blocks * tokens), jnp.bfloat16),
        compiler_params=pltpu.CompilerParams(vmem_limit_bytes=16 << 20),
        cost_estimate=pl.CostEstimate(
            flops=8 * parts.size, bytes_accessed=4 * parts.size, transcendentals=0
        ),
    )(parts, gain)


def spread_pair(pair_ref, keys_ref, values_ref):
    head_dim = keys_ref.shape[1]
    pair = pair_ref[...].astype(jnp.float32)
    ones = jnp.ones((values_ref.shape[0] - head_dim, pair.shape[1]), jnp.float32)
    keys_ref[...] = pair[:head_dim].T.astype(jnp.bfloat16)
    values_ref[...] = jnp.concatenate([pair[head_dim:], ones], axis=0).astype(jnp.bfloat16)


def scores_of(keys, query):
    factor = math.log2(math.e) * float(query.shape[0]) ** (-0.5)
    return jnp.dot(keys, query, preferred_element_type=jnp.float32) * factor


def weighted(scores, shift, values):
    weights = jnp.exp2(scores - shift).astype(jnp.bfloat16)
    return jnp.dot(values, weights, preferred_element_type=jnp.float32)


def cross_update(on, scores, values, best):
    most = jnp.maximum(best, jnp.max(scores, axis=0, keepdims=True))
    newbest = jnp.where(on, most, best)
    shift = jnp.where(on, newbest, BLANK)
    return newbest, jnp.exp2(best - newbest), weighted(scores, shift, values)


def finish(acc, head_dim):
    return acc[:head_dim] / jnp.maximum(acc[head_dim : head_dim + 1], 1.0)


def near_kernel(
    tile, active_ref, query_ref, own_ref, far_ref, own_out_ref, state_ref, best_ref, keys_ref, values_ref
):
    head_dim, tokens = query_ref.shape
    for n, ref in enumerate((own_ref, far_ref)):
        spread_pair(ref, keys_ref.at[n], values_ref.at[n])
    for at in range(tokens // tile):
        columns = pl.ds(at * tile, tile)
        query = query_ref[:, columns]
        scores = scores_of(keys_ref[0], query)
        acc = weighted(scores, jnp.max(scores, axis=0, keepdims=True), values_ref[0])
        own_out_ref[:, columns] = finish(acc, head_dim)
        start = jnp.full((1, tile), -BLANK, jnp.float32)
        scores = scores_of(keys_ref[1], query)
        best, _, acc = cross_update(active_ref[0] > 0, scores, values_ref[1], start)
        state_ref[:, columns] = acc
        best_ref[:, columns] = best


def middle_kernel(
    tile, which, active_ref, query_ref, state_ref, best_ref, far_ref, state_out_ref, best_out_ref,
    keys_ref, values_ref,
):
    tokens = query_ref.shape[1]
    spread_pair(far_ref, keys_ref, values_ref)
    for at in range(tokens // tile):
        columns = pl.ds(at * tile, tile)
        scores = scores_of(keys_ref[...], query_ref[:, columns])
        on = active_ref[which] > 0
        best, factor, term = cross_update(on, scores, values_ref[...], best_ref[:, columns])
        state_out_ref[:, columns] = state_ref[:, columns] * factor + term
        best_out_ref[:, columns] = best


def last_kernel(
    tile, which, active_ref, query_ref, own_in_ref, state_ref, best_ref, far_ref, out_ref,
    keys_ref, values_ref,
):
    head_dim, tokens = query_ref.shape
    block = out_ref.shape[-1]
    spread_pair(far_ref, keys_ref, values_ref)
    for at in range(tokens // tile):
        columns = pl.ds(at * tile, tile)
        scores = scores_of(keys_ref[...], query_ref[:, columns])
        on = active_ref[which] > 0
        _, factor, term = cross_update(on, scores, values_ref[...], best_ref[:, columns])
        cross = finish(state_ref[:, columns] * factor + term, head_dim)
        blank = jnp.zeros((out_ref.shape[1] - head_dim, tile), jnp.float32)
        result = jnp.concatenate([own_in_ref[:, columns] + cross, blank], axis=0).astype(jnp.bfloat16)
        for n in range(tile // block):
            out_ref[at * (tile // block) + n] = result[:, n * block : (n + 1) * block]


ONES = 8


def call_attend(kernel, out_shape, blocks, arrays):
    head_dim, tokens = arrays[1].shape
    lead = () if blocks == 1 else (blocks,)
    smem, vmem = pl.BlockSpec(memory_space=pltpu.SMEM), pl.BlockSpec(memory_space=pltpu.VMEM)
    several = isinstance(out_shape, list)
    return pl.pallas_call(
        kernel,
        out_shape=out_shape,
        in_specs=[smem] + [vmem] * (len(arrays) - 1),
        out_specs=[vmem] * len(out_shape) if several else vmem,
        scratch_shapes=[
            pltpu.VMEM(lead + (tokens, head_dim), jnp.bfloat16),
            pltpu.VMEM(lead + (head_dim + ONES, tokens), jnp.bfloat16),
        ],
        compiler_params=pltpu.CompilerParams(vmem_limit_bytes=24 << 20),
        cost_estimate=pl.CostEstimate(
            flops=4 * blocks * tokens * tokens * 256,
            bytes_accessed=4 * blocks * tokens * head_dim,
            transcendentals=blocks * tokens * tokens,
        ),
    )(*arrays)


def attend_near(active, query, own, far):
    head_dim, tokens = query.shape
    out_shape = [
        jax.ShapeDtypeStruct((rows, tokens), jnp.float32) for rows in (head_dim, head_dim + ONES, 1)
    ]
    kernel = functools.partial(near_kernel, tokens // 2)
    return call_attend(kernel, out_shape, 2, (active, query, own, far))


def attend_middle(active, which, query, state, best, far):
    out_shape = [jax.ShapeDtypeStruct(array.shape, jnp.float32) for array in (state, best)]
    kernel = functools.partial(middle_kernel, query.shape[1] // 2, which)
    return call_attend(kernel, out_shape, 1, (active, query, state, best, far))


def attend_last(active, which, query, own_result, state, best, far):
    head_dim, tokens = query.shape
    side = len(groups(0))
    out_shape = jax.ShapeDtypeStruct((side, head_dim + PAD, tokens // side), jnp.bfloat16)
    kernel = functools.partial(last_kernel, tokens // 2, which)
    return call_attend(kernel, out_shape, 1, (active, query, own_result, state, best, far))


def groups(which):
    heads = lax.axis_size("head")
    side = math.isqrt(heads)
    table = [[side * i + j for j in range(side)] for i in range(side)]
    return table if which == 0 else [list(column) for column in zip(*table)]


def exchange(slots, which):
    return lax.all_to_all(
        slots, "head", split_axis=0, concat_axis=0, tiled=True, axis_index_groups=groups(which)
    )


def column_weights(weight, out_weight):
    views, heads = lax.axis_size("view"), lax.axis_size("head")
    side = len(groups(0))
    core = lax.axis_index("view") % 2
    blank = jnp.zeros((PAD, weight.shape[1]), weight.dtype)
    packed = jnp.concatenate([out_weight, blank, weight[out_weight.shape[0] :]], axis=0)
    part = packed.shape[0] // 2
    pairs = []
    for view in range(views):
        step = side if view % 2 == 0 else -side
        for head in range(heads):
            pairs.append((view * heads + (head + step) % heads, view * heads + head))
    beside = lax.ppermute(packed, ("view", "head"), pairs)
    sent = jnp.where(core == 0, packed[:part], packed[part:])
    across = [(head, (head + heads // 2) % heads) for head in range(heads)]
    return packed, beside, lax.ppermute(sent, "head", across)


def project_out_kernel(
    place_ref, parts_ref, weight_ref, mine_ref, other_ref, mine_half_ref, other_half_ref, out_ref
):
    wide = parts_ref.shape[1]
    far = parts_ref[place_ref[3]].astype(jnp.float32)
    blank = jnp.zeros_like(far)
    first = jnp.where(place_ref[4] == 0, far, blank).astype(jnp.bfloat16)
    second = jnp.where(place_ref[4] == 0, blank, far).astype(jnp.bfloat16)
    total = None
    for part, rows_ref in (
        (parts_ref[place_ref[0]], weight_ref),
        (parts_ref[place_ref[1]], mine_ref),
        (parts_ref[place_ref[2]], other_ref),
        (first, mine_half_ref),
        (second, other_half_ref),
    ):
        term = lax.dot_general(
            part, rows_ref[:wide], (((0,), (0,)), ((), ())), preferred_element_type=jnp.float32
        )
        total = term if total is None else total + term
    out_ref[...] = total.reshape(out_ref.shape).astype(jnp.bfloat16)


def project_out(place, parts, column):
    side, wide, tokens = parts.shape
    width = column[0].shape[1]
    smem, vmem = pl.BlockSpec(memory_space=pltpu.SMEM), pl.BlockSpec(memory_space=pltpu.VMEM)
    partial = pl.pallas_call(
        project_out_kernel,
        out_shape=jax.ShapeDtypeStruct((side, tokens // side, width), jnp.bfloat16),
        in_specs=[smem] + [vmem] * (1 + len(column)),
        out_specs=vmem,
        compiler_params=pltpu.CompilerParams(vmem_limit_bytes=16 << 20),
        cost_estimate=pl.CostEstimate(
            flops=2 * parts.size * width, bytes_accessed=2 * (side * wide + tokens) * width, transcendentals=0
        ),
    )(place, parts, *column)
    partial = exchange(partial, 0)
    return jnp.sum(partial.astype(jnp.float32), axis=0).astype(jnp.bfloat16)


def on_device(latents, norm_gain, qkv_weight, qk_gain, out_weight, intersection):
    loc_len, view_dev, width = latents.shape
    rows = latents.reshape(loc_len, width)
    levels = lax.axis_size("view").bit_length() - 1
    rounds = intersection.shape[0]
    bits = [step * (levels - 1) // (rounds - 1) for step in range(rounds)]
    gain = qk_gain[0].T
    head_dim = gain.shape[0]
    weight = qkv_weight[0]
    active = intersection[:, 0]
    heads = lax.axis_size("head")
    normed, slots = normalize(rows, norm_gain, heads)
    core, side = lax.axis_index("view") % 2, len(groups(0))
    line = lax.axis_index("head") // side
    turn = jnp.where(core == 0, 1, side - 1)
    place = jnp.stack([line, line + turn, line + side - turn, line + side // 2]) % side
    place = jnp.concatenate([place, core[None]]).astype(jnp.int32)
    far_normed, gain, active = lax.optimization_barrier((partner(normed, bits[-1]), gain, active))
    far_slots = copies_of(far_normed, side)
    packed, whole, half = column_weights(weight, out_weight[0])
    every, far_slots, whole = lax.optimization_barrier((gather_tokens(slots), far_slots, whole))
    far_tokens = exchange(far_slots, 0).reshape(-1, width)
    query, own = project(every, weight, gain)
    near = [partner(own, bit) for bit in bits[:-1]]
    column = [whole, partner(whole, 0), half, partner(half, 0)]
    far_parts = project_far(place, far_tokens, weight, column, head_dim)
    far_parts = exchange(far_parts, 1)
    own_result, state, best = attend_near(active, query, own, near[0])
    out_rows = [rows[: head_dim + PAD] for rows in [packed] + column]
    far_parts, own_result, state, best, near[1], out_rows = lax.optimization_barrier(
        (far_parts, own_result, state, best, near[1], out_rows)
    )
    state, best = attend_middle(active, rounds - 1, query, state, best, settle(far_parts, gain))
    attended = attend_last(active, 1, query, own_result, state, best, near[1])
    mixed = project_out(place, exchange(attended, 1), out_rows)
    return mixed.reshape(loc_len, view_dev, width)


def solution(mesh):
    placed = (
        P("head", "view", None),
        P(),
        P("head", None, None),
        P("head", None, None),
        P("head", None, None),
        P(None, "view"),
    )
    return jax.shard_map(
        on_device, mesh=mesh, in_specs=placed, out_specs=P("head", "view", None), check_vma=False
    )
```
